128 devices in a mesh: inner: 16 (over z_lo, y, core), rows: 8 (over x, z_hi).
Axes of the slice: x: 4, y: 4, z: 4 (z_hi: 2, z_lo: 2; z = z_hi * 2 + z_lo), core: 2. Of those that a mesh axis runs over, the one named last changes fastest.
Arguments:
- left_u: bfloat16 [8, 64, 2048, 128], P('rows', 'inner'), may hold values from -6 to 6
- left_v: bfloat16 [8, 64, 2048, 128], P('rows', 'inner'), may hold values from -0.035888672 to 0.035888672
- tile_p: bfloat16 [8, 8, 2048, 128], P('rows'), may hold values from -6 to 6
- tile_q: bfloat16 [8, 8, 2048, 128], P('rows'), may hold values from -0.5390625 to 0.5390625
- sketch: bfloat16 [2048, 128], replicated, may hold values from -6 to 6
- tile_cols: int32 [8, 8], P('rows'), may hold values from 0 to 7
Outputs:
- new_left: float32 [8, 8, 2048, 128], P('rows', None, 'inner')
- new_right: float32 [8, 8, 2048, 128], P('rows', None, 'inner')
The draws below stay inside these ranges and needn't reach their ends.
All inputs are finite; a program needn't handle non-finite values.
Results may differ from the reference program's by a relative error of at most 0.0023.
Values may be sent and summed in bfloat16 or wider, within the bound.
A program may use at most 128 MiB of HBM per device.

```python
import math
import jax
import jax.numpy as jnp
from jax import lax

B = 2048
R = 128
C = 8
NT = 8
K = 64


def set_ends(values, stream_key, least, top_value):
    index_at = [jax.random.randint(jax.random.fold_in(stream_key, axis), (), 0, length) for axis, length in enumerate(values.shape)]
    longest = values.shape.index(max(values.shape))
    next_to = index_at[:longest] + [(index_at[longest] + 1) % values.shape[longest]] + index_at[longest + 1:]
    return values.at[tuple(index_at)].set(least).at[tuple(next_to)].set(top_value)


def shard_levels(stream_key, dims, split, smallest, high):
    level = 1.0
    for position, shards_of in split:
        draws = jax.random.uniform(jax.random.fold_in(jax.random.fold_in(stream_key, 6), position), (shards_of,), jnp.float32, smallest / len(split), high / len(split))
        level = level * jnp.repeat(jnp.exp(draws), dims[position] // shards_of).reshape((-1,) + (1,) * (len(dims) - 1 - position))
    return level


def noise(stream_key, shape, deviation, reach, cuts=(), held_as=jnp.bfloat16):
    factor_of = shard_levels(stream_key, shape, cuts, -0.22, 0.18) if cuts else 1.0
    entries = jax.random.normal(stream_key, shape, jnp.float32) * deviation * factor_of
    return jnp.minimum(jnp.maximum(entries, -reach), reach).astype(held_as)


def setup_inputs(seed: int = 0) -> dict:
    arg_keys = jax.random.split(jax.random.key(seed), 7)
    return {
        "left_u": noise(arg_keys[0], (NT, K, B, R), 1.0, 6.0, ((0, 8), (1, 16))),
        "left_v": noise(arg_keys[1], (NT, K, B, R), 0.006, 0.035888672, ((0, 8), (1, 16))),
        "tile_p": noise(arg_keys[2], (NT, C, B, R), 1.0, 6.0, ((0, 8),)),
        "tile_q": noise(arg_keys[3], (NT, C, B, R), 0.09, 0.5390625, ((0, 8),)),
        "sketch": noise(arg_keys[4], (B, R), 1.0, 6.0),
        "tile_cols": set_ends(jax.random.randint(arg_keys[5], (NT, C), 0, NT), jax.random.fold_in(arg_keys[5], 1), 0, NT - 1).astype(jnp.int32),
    }


def from_gram(gram, sample):
    order = gram.shape[0]
    ridge = 1e-06 * jnp.trace(gram) / order
    gram = gram + ridge * jnp.eye(order, dtype=jnp.float32)
    triangle = jnp.linalg.cholesky(gram)
    return jax.scipy.linalg.solve_triangular(triangle, sample.T, lower=True).T

def reference(left_u, left_v, tile_p, tile_q, sketch, tile_cols):
    highest = lax.Precision.HIGHEST
    ntile, per_row = tile_cols.shape
    factor_scale = math.sqrt(B)
    omega_f = sketch.astype(jnp.float32)

    def one_tile(target):
        row_id = target // per_row
        slot = target % per_row
        column = tile_cols[row_id, slot]
        row_u = left_u[row_id].astype(jnp.float32)
        row_v = left_v[row_id].astype(jnp.float32)
        col_u = left_u[column].astype(jnp.float32)
        col_v = left_v[column].astype(jnp.float32)
        left_p = tile_p[row_id, slot].astype(jnp.float32)
        right_q = tile_q[row_id, slot].astype(jnp.float32)
        coupling = jnp.einsum('kbr,kbs->krs', row_v, col_v, precision=highest)
        sketched = jnp.einsum('kbs,bt->kst', col_u, omega_f, precision=highest)
        coupled = jnp.einsum('krs,kst->krt', coupling, sketched, precision=highest)
        coupled = coupled.astype(jnp.bfloat16).astype(jnp.float32)
        sample = jnp.dot(left_p, jnp.dot(right_q.T, omega_f, precision=highest), precision=highest)
        sample = sample - jnp.einsum('kbr,krt->bt', row_u, coupled, precision=highest)
        gram = jnp.dot(sample.T, sample, precision=highest)
        ortho_basis = from_gram(gram, sample)
        basis_half = ortho_basis.astype(jnp.bfloat16).astype(jnp.float32)
        inner_a = jnp.einsum('kbr,bt->krt', row_u, basis_half, precision=highest)
        inner_b = jnp.einsum('krs,krt->kst', coupling, inner_a, precision=highest)
        inner_b = inner_b.astype(jnp.bfloat16).astype(jnp.float32)
        new_right = jnp.dot(right_q, jnp.dot(left_p.T, ortho_basis, precision=highest), precision=highest)
        new_right = new_right - jnp.einsum('kbs,kst->bt', col_u, inner_b, precision=highest)
        return (ortho_basis * factor_scale, new_right / factor_scale)
    lefts, rights = lax.map(one_tile, jnp.arange(ntile * per_row, dtype=jnp.int32))
    shape = (ntile, per_row, lefts.shape[1], lefts.shape[2])
    return (lefts.reshape(shape), rights.reshape(shape))
```

```python
import math

import jax
import jax.numpy as jnp
from jax import lax
from jax.experimental import pallas as pl
from jax.experimental.pallas import tpu as pltpu
from jax.sharding import PartitionSpec as P

MESH = pl.DeviceIdType.MESH
HIGHEST = lax.Precision.HIGHEST
F32 = jnp.float32
BF16 = jnp.bfloat16
VMEM_LIMIT = 56 * 1024 * 1024


def device(row, place):
    return {"rows": row, "inner": place}


def greet(partners, count):
    barrier = pltpu.get_barrier_semaphore()
    for row, place in partners:
        pl.semaphore_signal(barrier, inc=1, device_id=device(row, place), device_id_type=MESH)
    pl.semaphore_wait(barrier, count)


def remote(src, dst, send_sem, recv_sem, row, place):
    return pltpu.make_async_remote_copy(
        src_ref=src, dst_ref=dst, send_sem=send_sem, recv_sem=recv_sem,
        device_id=device(row, place), device_id_type=MESH,
    )


class Send:
    def __init__(self, src, dst, send_sem, recv_sem, row, place, is_self):
        self.far = remote(src, dst, send_sem, recv_sem, row, place)
        self.near = pltpu.make_async_copy(src, dst, recv_sem)
        self.is_self = is_self

    def start(self):
        @pl.when(jnp.logical_not(self.is_self))
        def _():
            self.far.start()

        @pl.when(self.is_self)
        def _():
            self.near.start()

    def wait_send(self):
        @pl.when(jnp.logical_not(self.is_self))
        def _():
            self.far.wait_send()


def arrived(ref, sem):
    pltpu.make_async_copy(ref, ref, sem).wait()


def dot(a, b, precision=None):
    return jnp.dot(a, b, preferred_element_type=F32, precision=precision)


def dot_t(a, b, precision=None):
    return lax.dot_general(
        a, b, (((0,), (0,)), ((), ())), preferred_element_type=F32, precision=precision
    )


def dot_nt(a, b, precision=None):
    return lax.dot_general(
        a, b, (((1,), (1,)), ((), ())), preferred_element_type=F32, precision=precision
    )


def couple_kernel(
    v_ref, u_ref, sketch_ref, coupled_ref, coupling_ref,
    vbuf, sown, sbuf, gown, gout, gsib, cown,
    v_send, v_recv, s_send, s_recv, g_send, g_recv, c_send, c_recv, k_send, k_recv,
):
    row, me = lax.axis_index("rows"), lax.axis_index("inner")
    core = lax.rem(me, 2)
    base = me - core
    sib = base + 1 - core
    owner_core = row // 4
    slot = lax.rem(row, 4)

    partners = [(lax.rem(row + d, 8), base + h) for d in range(1, 8) for h in range(2)]
    greet(partners + [(row, sib)], 15)

    v_copies = []
    for kk in range(4):
        for hh in range(2):
            to = core * 4 + kk
            v_copies.append(
                Send(
                    v_ref.at[kk, pl.ds(hh * 1024, 1024), :],
                    vbuf.at[:, pl.ds(pl.multiple_of(row * 128, 128), 128)],
                    v_send.at[kk * 2 + hh], v_recv.at[row], to, base + hh,
                    jnp.logical_and(to == row, core == hh),
                )
            )
            v_copies[-1].start()

    s_copies = []
    for kk in range(4):
        sown[kk] = dot_t(u_ref[kk], sketch_ref[...])
        to = core * 4 + kk
        s_copies.append(
            Send(
                sown.at[kk], sbuf.at[slot], s_send.at[kk], s_recv.at[slot],
                to, base + owner_core, jnp.logical_and(to == row, core == owner_core),
            )
        )
        s_copies[-1].start()

    for i in range(8):
        arrived(vbuf.at[:, pl.ds(i * 128, 128)], v_recv.at[i])

    def gram_half(half, out):
        right = vbuf[:, pl.ds(pl.multiple_of(half * 512, 512), 512)]
        for pair in range(4):
            value = dot_t(vbuf[:, pl.ds(pair * 256, 256)], right)
            for p in range(2):
                for j in range(4):
                    out[pair * 2 + p, j] = value[p * 128 : p * 128 + 128, j * 128 : j * 128 + 128]

    gram_half(1 - core, gout)
    g_copy = remote(gout, gsib, g_send, g_recv, row, sib)
    g_copy.start()
    gram_half(core, gown)
    g_copy.wait_recv()

    for j in range(4):
        arrived(sbuf.at[j], s_recv.at[j])
    for i in range(8):
        for j in range(4):
            total = gown[i, j] + gsib[i, j]
            gown[i, j] = total
            cown[i * 128 : i * 128 + 128, j * 128 : j * 128 + 128] = dot(
                total, sbuf[j], HIGHEST
            ).astype(BF16)

    c_copies = []
    for i in range(8):
        is_self = jnp.logical_and(row == i, core == owner_core)
        c_copies.append(
            Send(
                cown.at[pl.ds(i * 128, 128), :],
                coupled_ref.at[
                    pl.ds(pl.multiple_of(slot * 128, 128), 128),
                    pl.ds(pl.multiple_of(core * 512, 512), 512),
                ],
                c_send.at[i], c_recv.at[slot * 2 + core], i, base + owner_core, is_self,
            )
        )
        c_copies[-1].start()
    for i in range(8):
        is_self = jnp.logical_and(row == i, core == owner_core)
        c_copies.append(
            Send(
                gown.at[i], coupling_ref.at[slot, pl.ds(core * 4, 4)],
                k_send.at[i], k_recv.at[slot * 2 + core], i, base + owner_core, is_self,
            )
        )
        c_copies[-1].start()
    for kk in range(4):
        for hh in range(2):
            arrived(
                coupled_ref.at[pl.ds(kk * 128, 128), pl.ds(hh * 512, 512)],
                c_recv.at[kk * 2 + hh],
            )
            arrived(coupling_ref.at[kk, pl.ds(hh * 4, 4)], k_recv.at[kk * 2 + hh])
    for copy in v_copies + s_copies + [g_copy] + c_copies:
        copy.wait_send()


def couple(v, u, sketch):
    dma = pltpu.SemaphoreType.DMA
    vmem = pl.BlockSpec(memory_space=pltpu.VMEM)
    hbm = pl.BlockSpec(memory_space=pl.ANY)
    return pl.pallas_call(
        couple_kernel,
        out_shape=(
            jax.ShapeDtypeStruct((512, 1024), BF16),
            jax.ShapeDtypeStruct((4, 8, 128, 128), F32),
        ),
        in_specs=[hbm, vmem, vmem],
        out_specs=(hbm, hbm),
        scratch_shapes=[
            pltpu.VMEM((1024, 1024), BF16),
            pltpu.VMEM((4, 128, 128), F32),
            pltpu.VMEM((4, 128, 128), F32),
            pltpu.VMEM((8, 4, 128, 128), F32),
            pltpu.VMEM((8, 4, 128, 128), F32),
            pltpu.VMEM((8, 4, 128, 128), F32),
            pltpu.VMEM((1024, 512), BF16),
            dma((8,)), dma((8,)), dma((4,)), dma((4,)), dma, dma,
            dma((8,)), dma((8,)), dma((8,)), dma((8,)),
        ],
        compiler_params=pltpu.CompilerParams(
            collective_id=1, has_side_effects=True, vmem_limit_bytes=VMEM_LIMIT
        ),
        cost_estimate=pl.CostEstimate(
            flops=2_500_000_000, bytes_accessed=60_000_000, transcendentals=0
        ),
    )(v, u, sketch)


def neighbours(row, me):
    return [(row, lax.rem(me + d, 16)) for d in range(1, 16)]


def chip_at(chip, step):
    z, y = chip // 4, lax.rem(chip, 4)
    return lax.rem(z + step[0], 2) * 4 + lax.rem(y + step[1], 4)


def chip_back(chip, step):
    z, y = chip // 4, lax.rem(chip, 4)
    return lax.rem(z + step[0], 2) * 4 + lax.rem(y + 4 - step[1], 4)


STEPS = [(1, 2), (0, 2), (1, 1), (1, 3), (0, 1), (0, 3), (1, 0)]


def sample_kernel(
    cols_ref, u_ref, coupled_ref, p_ref, sq_ref, sample_ref, gram_ref,
    dpart, tosib, sibbuf, rsbuf, dsum, gpart, grbuf,
    i_send, i_recv, x_send, x_recv, gr_send, gr_recv,
):
    row, me = lax.axis_index("rows"), lax.axis_index("inner")
    core = lax.rem(me, 2)
    chip = me // 2
    sib = chip * 2 + 1 - core
    greet(neighbours(row, me), 15)

    steps = STEPS + [(0, 0)]
    inner_copies, chip_copies = [], []

    def pass_on(n):
        inner_copies[n].wait_recv()
        dpart[n] = dpart[n] + sibbuf[n]
        if n < 7:
            target = chip_at(chip, steps[n])
            copy = remote(
                dpart.at[n], rsbuf.at[n], x_send.at[n], x_recv.at[n], row, target * 2 + core
            )
            copy.start()
            chip_copies.append(copy)

    for n, step in enumerate(steps):
        target = chip_at(chip, step)
        for h in range(2):
            which = core if h else 1 - core
            rows = pl.ds(pl.multiple_of(target * 256 + which * 128, 128), 128)
            left = jnp.concatenate([u_ref[kk, rows, :] for kk in range(4)], axis=1)
            part = dot(left, coupled_ref[...])
            if h:
                dpart[n] = part
            else:
                tosib[n] = part
                copy = remote(tosib.at[n], sibbuf.at[n], i_send.at[n], i_recv.at[n], row, sib)
                copy.start()
                inner_copies.append(copy)
        if n >= 1:
            pass_on(n - 1)
    pass_on(7)
    total = dpart[7]
    for n in range(7):
        chip_copies[n].wait_recv()
        total = total + rsbuf[n]
    for j in range(8):
        dsum[j] = total[:, j * 128 : j * 128 + 128]

    gram_copies = []
    for c in range(8):
        value = dot(p_ref[c].astype(F32), sq_ref[c], HIGHEST) - dsum[cols_ref[c]]
        sample_ref[c] = value
        gpart[c] = dot_t(value, value, HIGHEST)
        for h in range(2):
            copy = Send(
                gpart.at[c], grbuf.at[me], gr_send.at[c * 2 + h], gr_recv.at[me],
                row, c * 2 + h, me == c * 2 + h,
            )
            copy.start()
            gram_copies.append(copy)
    gram = jnp.zeros((128, 128), F32)
    for m in range(16):
        arrived(grbuf.at[m], gr_recv.at[m])
        gram = gram + grbuf[m]
    gram_ref[...] = gram
    for copy in inner_copies + chip_copies + gram_copies:
        copy.wait_send()


def make_sample(cols, u, coupled, p_rows, sketched_q):
    dma = pltpu.SemaphoreType.DMA
    vmem = pl.BlockSpec(memory_space=pltpu.VMEM)
    smem = pl.BlockSpec(memory_space=pltpu.SMEM)
    return pl.pallas_call(
        sample_kernel,
        out_shape=(
            jax.ShapeDtypeStruct((8, 128, 128), F32),
            jax.ShapeDtypeStruct((128, 128), F32),
        ),
        in_specs=[smem, vmem, vmem, vmem, vmem],
        out_specs=(vmem, vmem),
        scratch_shapes=[
            pltpu.VMEM((8, 128, 1024), F32),
            pltpu.VMEM((8, 128, 1024), F32),
            pltpu.VMEM((8, 128, 1024), F32),
            pltpu.VMEM((7, 128, 1024), F32),
            pltpu.VMEM((8, 128, 128), F32),
            pltpu.VMEM((8, 128, 128), F32),
            pltpu.VMEM((16, 128, 128), F32),
            dma((8,)), dma((8,)), dma((7,)), dma((7,)), dma((16,)), dma((16,)),
        ],
        compiler_params=pltpu.CompilerParams(
            collective_id=2, has_side_effects=True, vmem_limit_bytes=VMEM_LIMIT
        ),
        cost_estimate=pl.CostEstimate(
            flops=2_500_000_000, bytes_accessed=100_000_000, transcendentals=0
        ),
    )(cols, u, coupled, p_rows, sketched_q)


def basis_kernel(
    scale, linv_ref, sample_ref, left_ref, all_ref, lbuf, bown,
    l_send, l_recv, b_send, b_recv, f_send,
):
    row, me = lax.axis_index("rows"), lax.axis_index("inner")
    core = lax.rem(me, 2)
    chip = me // 2
    sib = chip * 2 + 1 - core
    greet(neighbours(row, me), 15)

    copies = []
    for n, step in enumerate(STEPS):
        target = chip_at(chip, step)
        copy = remote(
            linv_ref, lbuf.at[chip], l_send.at[n], l_recv.at[chip], row, target * 2 + core
        )
        copy.start()
        copies.append(copy)
    lbuf[chip] = linv_ref[...]
    for step in STEPS:
        source = chip_back(chip, step)
        arrived(lbuf.at[source], l_recv.at[source])
    for c in range(8):
        value = dot_nt(sample_ref[c], lbuf[c], HIGHEST)
        left_ref[c] = value * scale
        bown[:, c * 128 : c * 128 + 128] = value.astype(BF16)

    def block(m):
        return all_ref.at[pl.ds(pl.multiple_of(m * 128, 128), 128), :]

    for n, step in enumerate(STEPS):
        target = chip_at(chip, step)
        copy = remote(bown, block(me), b_send.at[n], b_recv.at[me], row, target * 2 + core)
        copy.start()
        copies.append(copy)
    copy = remote(bown, block(me), b_send.at[7], b_recv.at[me], row, sib)
    copy.start()
    copies.append(copy)
    all_ref[pl.ds(pl.multiple_of(me * 128, 128), 128), :] = bown[...]
    order = STEPS[::-1]
    for n, step in enumerate(order):
        m = chip_back(chip, step) * 2 + core
        arrived(block(m), b_recv.at[m])
        copy = remote(block(m), block(m), f_send.at[n], b_recv.at[m], row, sib)
        copy.start()
        copies.append(copy)
    arrived(block(sib), b_recv.at[sib])
    for step in order:
        m = chip_back(chip, step) * 2 + 1 - core
        arrived(block(m), b_recv.at[m])
    for copy in copies:
        copy.wait_send()


def make_basis(linv, sample, scale):
    dma = pltpu.SemaphoreType.DMA
    vmem = pl.BlockSpec(memory_space=pltpu.VMEM)

    def kernel(*refs):
        basis_kernel(scale, *refs)

    return pl.pallas_call(
        kernel,
        out_shape=(
            jax.ShapeDtypeStruct((8, 128, 128), F32),
            jax.ShapeDtypeStruct((2048, 1024), BF16),
        ),
        in_specs=[vmem, vmem],
        out_specs=(vmem, vmem),
        scratch_shapes=[
            pltpu.VMEM((8, 128, 128), F32),
            pltpu.VMEM((128, 1024), BF16),
            dma((7,)), dma((8,)), dma((8,)), dma((16,)), dma((7,)),
        ],
        compiler_params=pltpu.CompilerParams(
            collective_id=3, has_side_effects=True, vmem_limit_bytes=VMEM_LIMIT
        ),
        cost_estimate=pl.CostEstimate(
            flops=200_000_000, bytes_accessed=40_000_000, transcendentals=0
        ),
    )(linv, sample)


def right_kernel(
    scale, cols_ref, u_ref, basis_ref, coupling_ref, panel_ref, q_ref, pb_ref, right_ref,
    panel, ib, dpart, tosib, sibbuf, xbuf, rsbuf,
    p_sem, i_send, i_recv, x_send, x_recv,
):
    row, me = lax.axis_index("rows"), lax.axis_index("inner")
    core = lax.rem(me, 2)
    chip = me // 2
    sib = chip * 2 + 1 - core
    load = pltpu.make_async_copy(panel_ref, panel, p_sem)
    load.start()
    greet(neighbours(row, me), 15)

    for kk in range(4):
        ia = dot_t(u_ref[kk], basis_ref[...])
        for c in range(8):
            ib[kk * 128 : kk * 128 + 128, c * 128 : c * 128 + 128] = dot_t(
                coupling_ref[kk, cols_ref[c]], ia[:, c * 128 : c * 128 + 128], HIGHEST
            ).astype(BF16)
    load.wait()

    steps = STEPS + [(0, 0)]
    inner_copies, chip_copies = [], []

    def pass_on(n):
        inner_copies[n].wait_recv()
        if n < 7:
            target = chip_at(chip, steps[n])
            xbuf[n] = (dpart[n] + sibbuf[n]).astype(BF16)
            copy = remote(
                xbuf.at[n], rsbuf.at[n], x_send.at[n], x_recv.at[n], row, target * 2 + core
            )
            copy.start()
            chip_copies.append(copy)

    for n, step in enumerate(steps):
        target = chip_at(chip, step)
        for h in range(2):
            which = core if h else 1 - core
            rows = pl.ds(pl.multiple_of(target * 256 + which * 128, 128), 128)
            out = dpart if h else tosib
            for c in range(8):
                col = cols_ref[c]
                left = jnp.concatenate([panel[col, kk, rows, :] for kk in range(4)], axis=1)
                out[n, :, c * 128 : c * 128 + 128] = dot(left, ib[:, c * 128 : c * 128 + 128])
            if not h:
                copy = remote(tosib.at[n], sibbuf.at[n], i_send.at[n], i_recv.at[n], row, sib)
                copy.start()
                inner_copies.append(copy)
        if n >= 1:
            pass_on(n - 1)
    pass_on(7)
    total = dpart[7] + sibbuf[7]
    for n in range(7):
        chip_copies[n].wait_recv()
        total = total + rsbuf[n].astype(F32)
    for c in range(8):
        value = dot(q_ref[c].astype(F32), pb_ref[c], HIGHEST)
        right_ref[c] = (value - total[:, c * 128 : c * 128 + 128]) * (1.0 / scale)
    for copy in inner_copies + chip_copies:
        copy.wait_send()


def make_right(cols, u, basis, coupling, panel, q_rows, p_basis, scale):
    dma = pltpu.SemaphoreType.DMA
    vmem = pl.BlockSpec(memory_space=pltpu.VMEM)
    smem = pl.BlockSpec(memory_space=pltpu.SMEM)
    hbm = pl.BlockSpec(memory_space=pl.ANY)

    def kernel(*refs):
        right_kernel(scale, *refs)

    return pl.pallas_call(
        kernel,
        out_shape=jax.ShapeDtypeStruct((8, 128, 128), F32),
        in_specs=[smem, vmem, vmem, vmem, hbm, vmem, vmem],
        out_specs=vmem,
        scratch_shapes=[
            pltpu.VMEM((8, 4, 2048, 128), BF16),
            pltpu.VMEM((512, 1024), BF16),
            pltpu.VMEM((8, 128, 1024), F32),
            pltpu.VMEM((8, 128, 1024), F32),
            pltpu.VMEM((8, 128, 1024), F32),
            pltpu.VMEM((7, 128, 1024), BF16),
            pltpu.VMEM((7, 128, 1024), BF16),
            dma, dma((8,)), dma((8,)), dma((7,)), dma((7,)),
        ],
        compiler_params=pltpu.CompilerParams(
            collective_id=4, has_side_effects=True, vmem_limit_bytes=VMEM_LIMIT
        ),
        cost_estimate=pl.CostEstimate(
            flops=4_500_000_000, bytes_accessed=100_000_000, transcendentals=0
        ),
    )(cols, u, basis, coupling, panel, q_rows, p_basis)


def body(left_u, left_v, tile_p, tile_q, sketch, tile_cols):
    width, rank = sketch.shape
    factor_scale = math.sqrt(width)
    u, v, p, q, cols = left_u[0], left_v[0], tile_p[0], tile_q[0], tile_cols[0]
    row_block = width // lax.axis_size("inner")
    offset = lax.axis_index("inner") * row_block

    panel = lax.all_gather(u, "rows", axis=0)
    coupled, coupling = couple(v, u, sketch)
    sketched_q = jnp.einsum("nbr,bt->nrt", q, sketch, preferred_element_type=F32)
    p_rows = lax.dynamic_slice_in_dim(p, offset, row_block, 1)
    q_rows = lax.dynamic_slice_in_dim(q, offset, row_block, 1)
    sample, gram = make_sample(cols, u, coupled, p_rows, sketched_q)
    eye = jnp.eye(rank, dtype=F32)
    ridge = 1e-06 * jnp.trace(gram) / rank
    triangle = jnp.linalg.cholesky(gram + ridge * eye)
    inverse = jax.scipy.linalg.solve_triangular(triangle, eye, lower=True)
    new_left, basis = make_basis(inverse, sample, factor_scale)
    p_basis = jnp.einsum(
        "nbr,bnt->nrt", p, basis.reshape(width, -1, rank), preferred_element_type=F32
    )
    new_right = make_right(cols, u, basis, coupling, panel, q_rows, p_basis, factor_scale)
    return new_left[None], new_right[None]


def solution(mesh):
    return jax.shard_map(
        body,
        mesh=mesh,
        in_specs=(
            P("rows", "inner", None, None),
            P("rows", "inner", None, None),
            P("rows", None, None, None),
            P("rows", None, None, None),
            P(),
            P("rows", None),
        ),
        out_specs=(P("rows", None, "inner", None), P("rows", None, "inner", None)),
        check_vma=False,
    )
```

```python
import math

import jax
import jax.numpy as jnp
from jax import lax
from jax.experimental import pallas as pl
from jax.experimental.pallas import tpu as pltpu
from jax.sharding import PartitionSpec as P

MESH = pl.DeviceIdType.MESH
HIGHEST = lax.Precision.HIGHEST
F32 = jnp.float32
BF16 = jnp.bfloat16
VMEM_LIMIT = 61 * 1024 * 1024


def device(row, place):
    return {"rows": row, "inner": place}


def greet(partners, count):
    barrier = pltpu.get_barrier_semaphore()
    for row, place in partners:
        pl.semaphore_signal(barrier, inc=1, device_id=device(row, place), device_id_type=MESH)
    pl.semaphore_wait(barrier, count)


def remote(src, dst, send_sem, recv_sem, row, place):
    return pltpu.make_async_remote_copy(
        src_ref=src, dst_ref=dst, send_sem=send_sem, recv_sem=recv_sem,
        device_id=device(row, place), device_id_type=MESH,
    )


class Send:
    def __init__(self, src, dst, send_sem, recv_sem, row, place, is_self):
        self.far = remote(src, dst, send_sem, recv_sem, row, place)
        self.near = pltpu.make_async_copy(src, dst, recv_sem)
        self.is_self = is_self

    def start(self):
        @pl.when(jnp.logical_not(self.is_self))
        def _():
            self.far.start()

        @pl.when(self.is_self)
        def _():
            self.near.start()

    def wait_send(self):
        @pl.when(jnp.logical_not(self.is_self))
        def _():
            self.far.wait_send()


def arrived(ref, sem):
    pltpu.make_async_copy(ref, ref, sem).wait()


def dot(a, b, precision=None):
    return jnp.dot(a, b, preferred_element_type=F32, precision=precision)


def dot_t(a, b, precision=None):
    return lax.dot_general(
        a, b, (((0,), (0,)), ((), ())), preferred_element_type=F32, precision=precision
    )


def dot_nt(a, b, precision=None):
    return lax.dot_general(
        a, b, (((1,), (1,)), ((), ())), preferred_element_type=F32, precision=precision
    )

LOW, HIGH = pl.ds(0, 512), pl.ds(512, 512)
ORDER = [(1, 2), (1, 1), (1, 3), (1, 0), (0, 2), (0, 1), (0, 3), (0, 0)]


class Place:
    def __init__(self):
        self.row, self.me = lax.axis_index("rows"), lax.axis_index("inner")
        self.core = lax.rem(self.me, 2)
        self.chip = self.me // 2
        self.z, self.y = self.chip // 4, lax.rem(self.chip, 4)
        self.base = self.me - self.core
        self.sib = self.base + 1 - self.core

    def chip_at(self, dz, dy):
        return lax.rem(self.z + dz, 2) * 4 + lax.rem(self.y + dy, 4)

    def inner_at(self, dz, dy):
        return self.chip_at(dz, dy) * 2 + self.core

    def row_at(self, dx, dz):
        x, z = self.row // 2, lax.rem(self.row, 2)
        return lax.rem(x + dx, 4) * 2 + lax.rem(z + dz, 2)


def inverse_factor(gram, work, inv):
    order = gram.shape[0]
    strip = 16
    row_id = lax.broadcasted_iota(jnp.int32, (order, order), 0)
    col_id = lax.broadcasted_iota(jnp.int32, (order, order), 1)
    diagonal = row_id == col_id
    ridge = 1e-06 * jnp.sum(jnp.where(diagonal, gram, 0.0)) / order
    work[...] = gram + jnp.where(diagonal, ridge, 0.0)
    inv[...] = jnp.where(diagonal, 1.0, 0.0)
    within = lax.broadcasted_iota(jnp.int32, (strip, order), 0)
    for lo in range(0, order, strip):
        a, m = work[lo : lo + strip, :], inv[lo : lo + strip, :]
        for j in range(strip):
            scale = lax.rsqrt(a[j : j + 1, lo + j : lo + j + 1])
            a_row, m_row = a[j : j + 1, :] * scale, m[j : j + 1, :] * scale
            factor = jnp.where(within > j, a[:, lo + j : lo + j + 1] * scale, 0.0)
            a = jnp.where(within == j, a_row, a - factor * a_row)
            m = jnp.where(within == j, m_row, m - factor * m_row)
        inv[lo : lo + strip, :] = m
        rest = lo + strip
        if rest < order:
            update = dot_t(a, jnp.concatenate([a, m], axis=1), HIGHEST)
            work[rest:, :] = work[rest:, :] - update[rest:, :order]
            inv[rest:, :] = inv[rest:, :] - update[rest:, order:]


class Reduction:
    def __init__(self, at, part, sibbuf, wire, hops, last, sems):
        self.at, self.part, self.sibbuf = at, part, sibbuf
        self.wire, self.hops, self.last = wire, hops, last
        self.i_send, self.i_recv, self.send, self.recv = sems
        self.copies, self.inner = [], []

    def own(self, n):
        return self.part.at[n, self.at.core]

    def offer(self, n):
        at = self.at
        copy = remote(
            self.part.at[n, 1 - at.core], self.sibbuf.at[n],
            self.i_send.at[n], self.i_recv.at[n], at.row, at.sib,
        )
        copy.start()
        self.inner.append(copy)

    def merge(self, n):
        self.inner[n].wait_recv()
        own = self.own(n)
        own[...] = own[...] + self.sibbuf[n]

    def hop(self, n, half, s, kind, way):
        at = self.at
        if self.wire is None:
            source = self.part.at[n, at.core, :, half]
        else:
            source = self.wire.at[pl.ds(n * 128, 128), half]
            source[...] = self.own(n)[:, half].astype(source.dtype)
        slot = (s * 3 + kind) * 2 + way
        to = at.inner_at(0, 1 if way == 0 else 3)
        copy = remote(source, self.hops.at[slot], self.send.at[slot], self.recv.at[slot], at.row, to)
        copy.start()
        self.copies.append(copy)

    def took(self, s, kind, way):
        slot = (s * 3 + kind) * 2 + way
        arrived(self.hops.at[slot], self.recv.at[slot])
        return self.hops[slot].astype(F32)

    def act(self, n):
        s, dy = ORDER[n]
        self.merge(n)
        if dy == 2:
            self.hop(n, LOW, s, 0, 0)
            self.hop(n, HIGH, s, 0, 1)
        elif dy == 1:
            self.hop(n, HIGH, s, 1, 0)
        elif dy == 3:
            self.hop(n, LOW, s, 1, 1)

    def relay(self, s):
        first = 4 * (1 - s)
        for n, half, way in ((first + 1, LOW, 0), (first + 2, HIGH, 1)):
            own = self.own(n)
            own[:, half] = own[:, half] + self.took(s, 0, way)
            self.hop(n, half, s, 2, way)

    def finish(self, s):
        own = self.own(4 * (1 - s) + 3)
        for half, kinds in ((LOW, (2, 1)), (HIGH, (1, 2))):
            own[:, half] = own[:, half] + self.took(s, kinds[0], 0) + self.took(s, kinds[1], 1)
        if s == 1:
            at = self.at
            copy = remote(
                own, self.last, self.send.at[12], self.recv.at[12], at.row, at.inner_at(1, 0)
            )
            copy.start()
            self.copies.append(copy)

    def total(self):
        arrived(self.last, self.recv.at[12])
        return self.own(7)[...] + self.last[...]

    def run(self, compute, between=None):
        for n in range(8):
            compute(n)
            self.offer(n)
            if 1 <= n <= 4:
                self.act(n - 1)
        self.relay(1)
        for n in range(4, 8):
            self.act(n)
        self.finish(1)
        self.relay(0)
        if between is not None:
            between()
        self.finish(0)
        return self.total()

    def wait_sends(self):
        for copy in self.inner + self.copies:
            copy.wait_send()


def update_kernel(
    scale, cols_ref, u_ref, v_ref, p_ref, q_ref, sketch_ref, left_ref, right_ref,
    panel, vbuf, sown, sbuf, gown, gsib, cown, coupled, coupling,
    tiles, mid, p_rows, q_rows, part, sibbuf, d_hops, d_last, r_hops, r_last,
    sample, dsum, gpart, grbuf, work, inv, lbuf, bown, basis, ib,
    local, v_send, v_recv, s_send, s_recv, g_send, g_recv, c_send, c_recv, k_send, k_recv,
    u_send, u_recv, di_send, di_recv, d_send, d_recv, gr_send, gr_recv, l_send, l_recv,
    b_send, b_recv, bh_recv, f_send, f_recv, ri_send, ri_recv, r_send, r_recv,
):
    at = Place()
    row, me, core, base, sib = at.row, at.me, at.core, at.base, at.sib
    owner_core = row // 4
    slot = lax.rem(row, 4)
    my_rows = pl.ds(pl.multiple_of(me * 128, 128), 128)

    own_u = pltpu.make_async_copy(u_ref, panel.at[row], local.at[0])
    own_u.start()
    load_p = pltpu.make_async_copy(p_ref.at[:, my_rows, :], p_rows, local.at[1])
    load_p.start()
    load_q = pltpu.make_async_copy(q_ref.at[:, my_rows, :], q_rows, local.at[2])
    load_q.start()
    load_tiles = pltpu.make_async_copy(q_ref.at[pl.ds(0, 4)], tiles, local.at[3])
    load_tiles.start()

    partners = [(lax.rem(row + d, 8), base + h) for d in range(1, 8) for h in range(2)]
    partners += [(row, lax.rem(me + d, 16)) for d in range(1, 16)]
    greet(partners, len(partners))

    v_copies = []
    for n in range(8):
        kk, hh = lax.rem(slot + n // 2, 4), lax.rem(n + core, 2)
        to = core * 4 + kk
        copy = Send(
            v_ref.at[kk, pl.ds(pl.multiple_of(hh * 1024, 1024), 1024), :],
            vbuf.at[:, pl.ds(pl.multiple_of(row * 128, 128), 128)],
            v_send.at[n], v_recv.at[row], to, base + hh,
            jnp.logical_and(to == row, core == hh),
        )
        copy.start()
        v_copies.append(copy)

    s_copies = []
    own_u.wait()
    for kk in range(4):
        sown[kk] = dot_t(panel[row, kk], sketch_ref[...])
        to = core * 4 + kk
        copy = Send(
            sown.at[kk], sbuf.at[slot], s_send.at[kk], s_recv.at[slot],
            to, base + owner_core, jnp.logical_and(to == row, core == owner_core),
        )
        copy.start()
        s_copies.append(copy)

    load_tiles.wait()
    for c in range(4):
        mid[c] = dot_t(tiles[c], sketch_ref[...])
    load_tiles = pltpu.make_async_copy(q_ref.at[pl.ds(4, 4)], tiles, local.at[3])
    load_tiles.start()
    load_tiles.wait()
    for c in range(4):
        mid[4 + c] = dot_t(tiles[c], sketch_ref[...])
    load_p.wait()
    for c in range(8):
        sample[c] = dot(p_rows[c].astype(F32), mid[c], HIGHEST)
    load_tiles = pltpu.make_async_copy(p_ref.at[pl.ds(0, 4)], tiles, local.at[3])
    load_tiles.start()

    for i in range(8):
        arrived(vbuf.at[:, pl.ds(i * 128, 128)], v_recv.at[i])

    u_copies = []

    def pass_panel(index, piece, dx, dz):
        ref = panel.at[index] if piece is None else panel.at[index, pl.ds(piece * 2, 2)]
        n = len(u_copies)
        copy = remote(ref, ref, u_send.at[n], u_recv.at[n], at.row_at(dx, dz), me)
        copy.start()
        u_copies.append(copy)

    def panel_here(n, index, piece=None):
        ref = panel.at[index] if piece is None else panel.at[index, pl.ds(piece * 2, 2)]
        arrived(ref, u_recv.at[n])

    pass_panel(row, None, 1, 0)
    pass_panel(row, None, 3, 0)
    pass_panel(row, None, 0, 1)

    def gram_half(half, write):
        right = vbuf[:, pl.ds(pl.multiple_of(half * 512, 512), 512)]
        for pair in range(4):
            value = dot_t(vbuf[:, pl.ds(pair * 256, 256)], right)
            for p in range(2):
                write(pair * 2 + p, value[p * 128 : p * 128 + 128])

    def write_out(i, value):
        part[i, 0, :, :512] = value

    def write_own(i, value):
        for j in range(4):
            gown[i, j] = value[:, j * 128 : j * 128 + 128]

    gram_half(1 - core, write_out)
    g_copy = remote(part.at[:, 0, :, LOW], gsib, g_send, g_recv, row, sib)
    g_copy.start()
    gram_half(core, write_own)
    g_copy.wait_recv()
    for j in range(4):
        arrived(sbuf.at[j], s_recv.at[j])
    c_copies = []
    for i in range(8):
        for j in range(4):
            total = gown[i, j] + gsib[i, :, j * 128 : j * 128 + 128]
            gown[i, j] = total
            cown[i * 128 : i * 128 + 128, j * 128 : j * 128 + 128] = dot(
                total, sbuf[j], HIGHEST
            ).astype(BF16)
        copy = Send(
            cown.at[pl.ds(i * 128, 128), :],
            coupled.at[
                pl.ds(pl.multiple_of(slot * 128, 128), 128),
                pl.ds(pl.multiple_of(core * 512, 512), 512),
            ],
            c_send.at[i], c_recv.at[slot * 2 + core], i, base + owner_core,
            jnp.logical_and(row == i, core == owner_core),
        )
        copy.start()
        c_copies.append(copy)
    for kk in range(4):
        for hh in range(2):
            arrived(
                coupled.at[pl.ds(kk * 128, 128), pl.ds(hh * 512, 512)], c_recv.at[kk * 2 + hh]
            )
    for i in range(8):
        copy = Send(
            gown.at[i], coupling.at[slot, pl.ds(core * 4, 4)],
            k_send.at[i], k_recv.at[slot * 2 + core], i, base + owner_core,
            jnp.logical_and(row == i, core == owner_core),
        )
        copy.start()
        c_copies.append(copy)
    g_copy.wait_send()

    def panel_block(n, index):
        rows = pl.ds(pl.multiple_of(at.chip_at(*ORDER[n]) * 256, 256), 256)
        return jnp.concatenate([panel[index, kk, rows, :] for kk in range(4)], axis=1)

    def d_block(n):
        value = dot(panel_block(n, row), coupled[...])
        part[n, 0] = value[:128]
        part[n, 1] = value[128:]

    def second_leg():
        panel_here(0, at.row_at(3, 0))
        panel_here(1, at.row_at(1, 0))
        pass_panel(at.row_at(3, 0), 0, 1, 0)
        pass_panel(at.row_at(1, 0), 1, 3, 0)
        panel_here(2, at.row_at(0, 1))
        pass_panel(at.row_at(0, 1), None, 1, 0)
        pass_panel(at.row_at(0, 1), None, 3, 0)

    reduction = Reduction(
        at, part, sibbuf, None, d_hops, d_last, (di_send, di_recv, d_send, d_recv)
    )
    total = reduction.run(d_block)
    for j in range(8):
        dsum[j] = total[:, j * 128 : j * 128 + 128]

    gram_copies = []
    for c in range(8):
        value = sample[c] - dsum[cols_ref[c]]
        sample[c] = value
        gpart[c] = dot_t(value, value, HIGHEST)
        for h in range(2):
            copy = Send(
                gpart.at[c], grbuf.at[me], gr_send.at[c * 2 + h], gr_recv.at[me],
                row, c * 2 + h, me == c * 2 + h,
            )
            copy.start()
            gram_copies.append(copy)
    second_leg()
    gram = jnp.zeros((128, 128), F32)
    for m in range(16):
        arrived(grbuf.at[m], gr_recv.at[m])
        gram = gram + grbuf[m]
    inverse_factor(gram, work, inv)

    l_copies = []
    for n, step in enumerate(ORDER[:7]):
        copy = remote(
            inv, lbuf.at[at.chip], l_send.at[n], l_recv.at[at.chip], row, at.inner_at(*step)
        )
        copy.start()
        l_copies.append(copy)
    lbuf[at.chip] = inv[...]
    panel_here(3, at.row_at(2, 0), 0)
    panel_here(4, at.row_at(2, 0), 1)
    pass_panel(at.row_at(2, 0), None, 0, 1)
    for step in ORDER[:7]:
        source = at.chip_at(*step)
        arrived(lbuf.at[source], l_recv.at[source])
    for c in range(8):
        value = dot_nt(sample[c], lbuf[c], HIGHEST)
        left_ref[c] = value * scale
        bown[:, c * 128 : c * 128 + 128] = value.astype(BF16)

    b_copies, f_copies = [], []

    def block(m, half=None):
        rows = pl.ds(pl.multiple_of(m * 128, 128), 128)
        return basis.at[rows, :] if half is None else basis.at[rows, half]

    def pass_basis(source, dest, recv, dz, dy):
        copy = remote(source, dest, b_send.at[len(b_copies)], recv, row, at.inner_at(dz, dy))
        copy.start()
        b_copies.append(copy)

    def to_sib(source, dest, n):
        copy = remote(source, dest, f_send.at[n], f_recv.at[n], row, sib)
        copy.start()
        f_copies.append(copy)

    pass_basis(bown, block(me), b_recv.at[0], 1, 0)
    pass_basis(bown, block(me), b_recv.at[1], 0, 1)
    pass_basis(bown, block(me), b_recv.at[2], 0, 3)
    to_sib(bown, block(me), 0)
    basis[my_rows, :] = bown[...]
    other = at.inner_at(1, 0)
    arrived(block(other), b_recv.at[0])
    pass_basis(block(other), block(other), b_recv.at[3], 0, 1)
    pass_basis(block(other), block(other), b_recv.at[4], 0, 3)
    to_sib(block(other), block(other), 1)
    for s in range(2):
        for way, dy in ((0, 3), (1, 1)):
            m = at.inner_at(s, dy)
            half = HIGH if way else LOW
            n = 1 + s * 2 + way
            arrived(block(m), b_recv.at[n])
            pass_basis(block(m, half), block(m, half), bh_recv.at[s * 2 + way], 0, 3 if way else 1)
            to_sib(block(m), block(m), 1 + n)
    reduction.wait_sends()

    def basis_term(n, dz, dy, first=False):
        chip = at.chip_at(dz, dy)
        if n < 6:
            m = chip * 2 + 1 - core
            arrived(block(m), f_recv.at[n])
        rows = pl.ds(pl.multiple_of(chip * 256, 256), 256)
        for kk in range(4):
            for h in range(2):
                value = dot_t(panel[row, kk, rows, :], basis[rows, h * 512 : h * 512 + 512])
                gsib[kk * 2 + h] = value if first else gsib[kk * 2 + h] + value

    basis_term(0, 0, 0, True)
    basis_term(1, 1, 0)
    basis_term(2, 0, 3)
    basis_term(3, 0, 1)
    basis_term(4, 1, 3)
    basis_term(5, 1, 1)
    for s in range(2):
        m = at.inner_at(s, 2)
        for way in range(2):
            half = HIGH if way else LOW
            arrived(block(m, half), bh_recv.at[s * 2 + way])
            to_sib(block(m, half), block(m, half), 6 + s * 2 + way)
    for s in range(2):
        m = at.chip_at(s, 2) * 2 + 1 - core
        for way in range(2):
            arrived(block(m, HIGH if way else LOW), f_recv.at[6 + s * 2 + way])
        basis_term(6 + s, s, 2)

    for kk in range(4):
        for hh in range(2):
            arrived(coupling.at[kk, pl.ds(hh * 4, 4)], k_recv.at[kk * 2 + hh])
    for kk in range(4):
        for c in range(8):
            lanes = pl.ds((c % 4) * 128, 128)
            ib[kk * 128 : kk * 128 + 128, c * 128 : c * 128 + 128] = dot_t(
                coupling[kk, cols_ref[c]], gsib[kk * 2 + c // 4, :, lanes], HIGHEST
            ).astype(BF16)
    panel_here(5, at.row_at(3, 1))
    panel_here(6, at.row_at(1, 1))
    panel_here(7, at.row_at(2, 1))

    def r_block(n):
        for c in range(8):
            value = dot(panel_block(n, cols_ref[c]), ib[:, c * 128 : c * 128 + 128])
            part[n, 0, :, c * 128 : c * 128 + 128] = value[:128]
            part[n, 1, :, c * 128 : c * 128 + 128] = value[128:]

    def p_basis():
        for t in range(2):
            if t == 1:
                again = pltpu.make_async_copy(p_ref.at[pl.ds(4, 4)], tiles, local.at[3])
                again.start()
                again.wait()
            for c in range(4):
                n = t * 4 + c
                mid[n] = dot_t(tiles[c], basis[:, n * 128 : n * 128 + 128])
        for c in range(8):
            sample[c] = dot(q_rows[c].astype(F32), mid[c], HIGHEST)

    load_tiles.wait()
    load_q.wait()
    projection = Reduction(
        at, part, sibbuf, vbuf, r_hops, r_last, (ri_send, ri_recv, r_send, r_recv)
    )
    total = projection.run(r_block, p_basis)
    for c in range(8):
        right_ref[c] = (sample[c] - total[:, c * 128 : c * 128 + 128]) * (1.0 / scale)

    for copy in v_copies + s_copies + c_copies + u_copies + gram_copies + l_copies:
        copy.wait_send()
    for copy in b_copies + f_copies:
        copy.wait_send()
    projection.wait_sends()


def update(u, v, p, q, sketch, cols, scale):
    dma = pltpu.SemaphoreType.DMA
    vmem = pl.BlockSpec(memory_space=pltpu.VMEM)
    smem = pl.BlockSpec(memory_space=pltpu.SMEM)
    hbm = pl.BlockSpec(memory_space=pl.ANY)

    def kernel(*refs):
        update_kernel(scale, *refs)

    squares = jax.ShapeDtypeStruct((8, 128, 128), F32)
    return pl.pallas_call(
        kernel,
        out_shape=(squares, squares),
        in_specs=[smem, hbm, hbm, hbm, hbm, vmem],
        out_specs=(vmem, vmem),
        scratch_shapes=[
            pltpu.VMEM((8, 4, 2048, 128), BF16),
            pltpu.VMEM((1024, 1024), BF16),
            pltpu.VMEM((4, 128, 128), F32),
            pltpu.VMEM((4, 128, 128), F32),
            pltpu.VMEM((8, 4, 128, 128), F32),
            pltpu.VMEM((8, 128, 512), F32),
            pltpu.VMEM((1024, 512), BF16),
            pltpu.VMEM((512, 1024), BF16),
            pltpu.VMEM((4, 8, 128, 128), F32),
            pltpu.VMEM((4, 2048, 128), BF16),
            pltpu.VMEM((8, 128, 128), F32),
            pltpu.VMEM((8, 128, 128), BF16),
            pltpu.VMEM((8, 128, 128), BF16),
            pltpu.VMEM((8, 2, 128, 1024), F32),
            pltpu.VMEM((8, 128, 1024), F32),
            pltpu.VMEM((12, 128, 512), F32),
            pltpu.VMEM((128, 1024), F32),
            pltpu.VMEM((12, 128, 512), BF16),
            pltpu.VMEM((128, 1024), F32),
            pltpu.VMEM((8, 128, 128), F32),
            pltpu.VMEM((8, 128, 128), F32),
            pltpu.VMEM((8, 128, 128), F32),
            pltpu.VMEM((16, 128, 128), F32),
            pltpu.VMEM((128, 128), F32),
            pltpu.VMEM((128, 128), F32),
            pltpu.VMEM((8, 128, 128), F32),
            pltpu.VMEM((128, 1024), BF16),
            pltpu.VMEM((2048, 1024), BF16),
            pltpu.VMEM((512, 1024), BF16),
            dma((4,)), dma((8,)), dma((8,)), dma((4,)), dma((4,)), dma, dma,
            dma((8,)), dma((8,)), dma((8,)), dma((8,)),
            dma((8,)), dma((8,)), dma((8,)), dma((8,)), dma((13,)), dma((13,)),
            dma((16,)), dma((16,)), dma((7,)), dma((8,)),
            dma((9,)), dma((5,)), dma((4,)), dma((10,)), dma((10,)),
            dma((8,)), dma((8,)), dma((13,)), dma((13,)),
        ],
        compiler_params=pltpu.CompilerParams(
            collective_id=1, has_side_effects=True, vmem_limit_bytes=VMEM_LIMIT
        ),
        cost_estimate=pl.CostEstimate(
            flops=13_000_000_000, bytes_accessed=30_000_000, transcendentals=0
        ),
    )(cols, u, v, p, q, sketch)


def body(left_u, left_v, tile_p, tile_q, sketch, tile_cols):
    factor_scale = math.sqrt(sketch.shape[0])
    new_left, new_right = update(
        left_u[0], left_v[0], tile_p[0], tile_q[0], sketch, tile_cols[0], factor_scale
    )
    return new_left[None], new_right[None]


def solution(mesh):
    return jax.shard_map(
        body,
        mesh=mesh,
        in_specs=(
            P("rows", "inner", None, None),
            P("rows", "inner", None, None),
            P("rows", None, None, None),
            P("rows", None, None, None),
            P(),
            P("rows", None),
        ),
        out_specs=(P("rows", None, "inner", None), P("rows", None, "inner", None)),
        check_vma=False,
    )
```

```python
import math

import jax
import jax.numpy as jnp
from jax import lax
from jax.experimental import pallas as pl
from jax.experimental.pallas import tpu as pltpu
from jax.sharding import PartitionSpec as P

MESH = pl.DeviceIdType.MESH
HIGHEST = lax.Precision.HIGHEST
F32 = jnp.float32
BF16 = jnp.bfloat16
VMEM_LIMIT = 61 * 1024 * 1024


def device(row, place):
    return {"rows": row, "inner": place}


def greet(partners, count):
    barrier = pltpu.get_barrier_semaphore()
    for row, place in partners:
        pl.semaphore_signal(barrier, inc=1, device_id=device(row, place), device_id_type=MESH)
    pl.semaphore_wait(barrier, count)


def remote(src, dst, send_sem, recv_sem, row, place):
    return pltpu.make_async_remote_copy(
        src_ref=src, dst_ref=dst, send_sem=send_sem, recv_sem=recv_sem,
        device_id=device(row, place), device_id_type=MESH,
    )


class Send:
    def __init__(self, src, dst, send_sem, recv_sem, row, place, is_self):
        self.far = remote(src, dst, send_sem, recv_sem, row, place)
        self.near = pltpu.make_async_copy(src, dst, recv_sem)
        self.is_self = is_self

    def start(self):
        @pl.when(jnp.logical_not(self.is_self))
        def _():
            self.far.start()

        @pl.when(self.is_self)
        def _():
            self.near.start()

    def wait_send(self):
        @pl.when(jnp.logical_not(self.is_self))
        def _():
            self.far.wait_send()


def arrived(ref, sem):
    pltpu.make_async_copy(ref, ref, sem).wait()


def dot(a, b, precision=None):
    return jnp.dot(a, b, preferred_element_type=F32, precision=precision)


def dot_t(a, b, precision=None):
    return lax.dot_general(
        a, b, (((0,), (0,)), ((), ())), preferred_element_type=F32, precision=precision
    )


def dot_nt(a, b, precision=None):
    return lax.dot_general(
        a, b, (((1,), (1,)), ((), ())), preferred_element_type=F32, precision=precision
    )

LOW, HIGH = pl.ds(0, 512), pl.ds(512, 512)
ORDER = [(1, 2), (1, 1), (1, 3), (1, 0), (0, 2), (0, 1), (0, 3), (0, 0)]


def position(n):
    return ORDER[n][0] * 4 + ORDER[n][1]


class Place:
    def __init__(self):
        self.row, self.me = lax.axis_index("rows"), lax.axis_index("inner")
        self.core = lax.rem(self.me, 2)
        self.chip = self.me // 2
        self.z, self.y = self.chip // 4, lax.rem(self.chip, 4)
        self.base = self.me - self.core
        self.sib = self.base + 1 - self.core

    def chip_at(self, dz, dy):
        return lax.rem(self.z + dz, 2) * 4 + lax.rem(self.y + dy, 4)

    def inner_at(self, dz, dy):
        return self.chip_at(dz, dy) * 2 + self.core

    def row_at(self, dx, dz):
        x, z = self.row // 2, lax.rem(self.row, 2)
        return lax.rem(x + dx, 4) * 2 + lax.rem(z + dz, 2)


def inverse_factor(gram, work, inv):
    order = gram.shape[0]
    strip = 16
    row_id = lax.broadcasted_iota(jnp.int32, (order, order), 0)
    col_id = lax.broadcasted_iota(jnp.int32, (order, order), 1)
    diagonal = row_id == col_id
    ridge = 1e-06 * jnp.sum(jnp.where(diagonal, gram, 0.0)) / order
    work[...] = gram + jnp.where(diagonal, ridge, 0.0)
    inv[...] = jnp.where(diagonal, 1.0, 0.0)
    within = lax.broadcasted_iota(jnp.int32, (strip, order), 0)
    for lo in range(0, order, strip):
        a, m = work[lo : lo + strip, :], inv[lo : lo + strip, :]
        for j in range(strip):
            scale = lax.rsqrt(a[j : j + 1, lo + j : lo + j + 1])
            a_row, m_row = a[j : j + 1, :] * scale, m[j : j + 1, :] * scale
            factor = jnp.where(within > j, a[:, lo + j : lo + j + 1] * scale, 0.0)
            a = jnp.where(within == j, a_row, a - factor * a_row)
            m = jnp.where(within == j, m_row, m - factor * m_row)
        inv[lo : lo + strip, :] = m
        rest = lo + strip
        if rest < order:
            update = dot_t(a, jnp.concatenate([a, m], axis=1), HIGHEST)
            work[rest:, :] = work[rest:, :] - update[rest:, :order]
            inv[rest:, :] = inv[rest:, :] - update[rest:, order:]


class Reduction:
    def __init__(self, at, part, sibbuf, wire, hops, last, sems):
        self.at, self.part, self.sibbuf = at, part, sibbuf
        self.wire, self.hops, self.last = wire, hops, last
        self.i_send, self.i_recv, self.send, self.recv = sems
        self.copies, self.inner = [], []

    def own(self, n):
        return self.part.at[position(n), self.at.core]

    def offer(self, n):
        at = self.at
        copy = remote(
            self.part.at[position(n), 1 - at.core], self.sibbuf.at[n],
            self.i_send.at[n], self.i_recv.at[n], at.row, at.sib,
        )
        copy.start()
        self.inner.append(copy)

    def merge(self, n):
        self.inner[n].wait_recv()
        own = self.own(n)
        own[...] = own[...] + self.sibbuf[n]

    def hop(self, n, half, s, kind, way):
        at = self.at
        if self.wire is None:
            source = self.part.at[position(n), at.core, :, half]
        else:
            source = self.wire.at[pl.ds(n * 128, 128), half]
            source[...] = self.own(n)[:, half].astype(source.dtype)
        slot = (s * 3 + kind) * 2 + way
        to = at.inner_at(0, 1 if way == 0 else 3)
        copy = remote(source, self.hops.at[slot], self.send.at[slot], self.recv.at[slot], at.row, to)
        copy.start()
        self.copies.append(copy)

    def took(self, s, kind, way):
        slot = (s * 3 + kind) * 2 + way
        arrived(self.hops.at[slot], self.recv.at[slot])
        return self.hops[slot].astype(F32)

    def act(self, n):
        s, dy = ORDER[n]
        self.merge(n)
        if dy == 2:
            self.hop(n, LOW, s, 0, 0)
            self.hop(n, HIGH, s, 0, 1)
        elif dy == 1:
            self.hop(n, HIGH, s, 1, 0)
        elif dy == 3:
            self.hop(n, LOW, s, 1, 1)

    def relay(self, s):
        first = 4 * (1 - s)
        for n, half, way in ((first + 1, LOW, 0), (first + 2, HIGH, 1)):
            own = self.own(n)
            own[:, half] = own[:, half] + self.took(s, 0, way)
            self.hop(n, half, s, 2, way)

    def finish(self, s):
        own = self.own(4 * (1 - s) + 3)
        for half, kinds in ((LOW, (2, 1)), (HIGH, (1, 2))):
            own[:, half] = own[:, half] + self.took(s, kinds[0], 0) + self.took(s, kinds[1], 1)
        if s == 1:
            at = self.at
            copy = remote(
                own, self.last, self.send.at[12], self.recv.at[12], at.row, at.inner_at(1, 0)
            )
            copy.start()
            self.copies.append(copy)

    def total(self):
        arrived(self.last, self.recv.at[12])
        own = self.own(7)
        own[...] = own[...] + self.last[...]
        return own

    def run(self, compute, between=None):
        for n in range(8):
            compute(n)
            self.offer(n)
            if 1 <= n <= 4:
                self.act(n - 1)
        self.relay(1)
        for n in range(4, 8):
            self.act(n)
        self.finish(1)
        self.relay(0)
        if between is not None:
            between()
        self.finish(0)
        return self.total()

    def wait_sends(self):
        for copy in self.inner + self.copies:
            copy.wait_send()


def update_kernel(
    scale, cols_ref, u_ref, v_ref, p_ref, q_ref, sketch_ref, left_ref, right_ref,
    panel, vbuf, sown, sbuf, gown, gsib, cown, coupled, coupling,
    tiles, mid, p_rows, q_rows, part, sibbuf, d_hops, d_last, r_hops, r_last,
    sample, dsum, gpart, grbuf, work, inv, lbuf, bown, basis, ib,
    local, v_send, v_recv, s_send, s_recv, g_send, g_recv, c_send, c_recv, k_send, k_recv,
    u_send, u_recv, di_send, di_recv, d_send, d_recv, gr_send, gr_recv, l_send, l_recv,
    b_send, b_recv, bh_recv, f_send, f_recv, ri_send, ri_recv, r_send, r_recv,
    u_own, their_cols, swapped, cols_sem, i_send, i_recv, t_send, t_recv,
):
    at = Place()
    row, me, core, base, sib = at.row, at.me, at.core, at.base, at.sib
    owner_core = row // 4
    slot = lax.rem(row, 4)
    my_rows = pl.ds(pl.multiple_of(me * 128, 128), 128)

    half_z = lax.rem(row, 2)
    partner = at.row_at(0, 1)
    own_u = pltpu.make_async_copy(u_ref, u_own, local.at[0])
    own_u.start()
    start_panel = pltpu.make_async_copy(u_ref.at[:, :, half_z], panel.at[row], local.at[4])
    start_panel.start()
    load_p = pltpu.make_async_copy(p_ref.at[:, my_rows, :], p_rows, local.at[1])
    load_p.start()
    load_q = pltpu.make_async_copy(q_ref.at[:, my_rows, :], q_rows, local.at[2])
    load_q.start()
    load_tiles = pltpu.make_async_copy(q_ref.at[pl.ds(0, 4)], tiles, local.at[3])
    load_tiles.start()

    partners = [(lax.rem(row + d, 8), base + h) for d in range(1, 8) for h in range(2)]
    partners += [(row, lax.rem(me + d, 16)) for d in range(1, 16)]
    greet(partners, len(partners))
    cols_copy = remote(cols_ref, their_cols, cols_sem.at[0], cols_sem.at[1], partner, me)
    cols_copy.start()

    v_copies = []
    for n in range(8):
        kk, hh = lax.rem(slot + n // 2, 4), lax.rem(n + core, 2)
        to = core * 4 + kk
        copy = Send(
            v_ref.at[kk, pl.ds(pl.multiple_of(hh * 1024, 1024), 1024), :],
            vbuf.at[:, pl.ds(pl.multiple_of(row * 128, 128), 128)],
            v_send.at[n], v_recv.at[row], to, base + hh,
            jnp.logical_and(to == row, core == hh),
        )
        copy.start()
        v_copies.append(copy)

    s_copies = []
    own_u.wait()
    for kk in range(4):
        sown[kk] = dot_t(u_own[kk].reshape(2048, 128), sketch_ref[...])
        to = core * 4 + kk
        copy = Send(
            sown.at[kk], sbuf.at[slot], s_send.at[kk], s_recv.at[slot],
            to, base + owner_core, jnp.logical_and(to == row, core == owner_core),
        )
        copy.start()
        s_copies.append(copy)

    load_tiles.wait()
    for c in range(4):
        mid[c] = dot_t(tiles[c], sketch_ref[...])
    load_tiles = pltpu.make_async_copy(q_ref.at[pl.ds(4, 4)], tiles, local.at[3])
    load_tiles.start()
    load_tiles.wait()
    for c in range(4):
        mid[4 + c] = dot_t(tiles[c], sketch_ref[...])
    load_p.wait()
    for c in range(8):
        sample[c] = dot(p_rows[c].astype(F32), mid[c], HIGHEST)
    load_tiles = pltpu.make_async_copy(p_ref.at[pl.ds(0, 4)], tiles, local.at[3])
    load_tiles.start()

    for i in range(8):
        arrived(vbuf.at[:, pl.ds(i * 128, 128)], v_recv.at[i])

    def gram_half(half, write):
        right = vbuf[:, pl.ds(pl.multiple_of(half * 512, 512), 512)]
        for pair in range(4):
            value = dot_t(vbuf[:, pl.ds(pair * 256, 256)], right)
            for p in range(2):
                write(pair * 2 + p, value[p * 128 : p * 128 + 128])

    def write_out(i, value):
        part[i, 0, :, :512] = value

    def write_own(i, value):
        for j in range(4):
            gown[i, j] = value[:, j * 128 : j * 128 + 128]

    gram_half(1 - core, write_out)
    g_copy = remote(part.at[:, 0, :, LOW], gsib, g_send, g_recv, row, sib)
    g_copy.start()
    gram_half(core, write_own)
    g_copy.wait_recv()
    for j in range(4):
        arrived(sbuf.at[j], s_recv.at[j])
    c_copies = []
    for i in range(8):
        for j in range(4):
            total = gown[i, j] + gsib[i, :, j * 128 : j * 128 + 128]
            gown[i, j] = total
            cown[i * 128 : i * 128 + 128, j * 128 : j * 128 + 128] = dot(
                total, sbuf[j], HIGHEST
            ).astype(BF16)
        copy = Send(
            cown.at[pl.ds(i * 128, 128), :],
            coupled.at[
                pl.ds(pl.multiple_of(slot * 128, 128), 128),
                pl.ds(pl.multiple_of(core * 512, 512), 512),
            ],
            c_send.at[i], c_recv.at[slot * 2 + core], i, base + owner_core,
            jnp.logical_and(row == i, core == owner_core),
        )
        copy.start()
        c_copies.append(copy)
    for kk in range(4):
        for hh in range(2):
            arrived(
                coupled.at[pl.ds(kk * 128, 128), pl.ds(hh * 512, 512)], c_recv.at[kk * 2 + hh]
            )
    for i in range(8):
        copy = Send(
            gown.at[i], coupling.at[slot, pl.ds(core * 4, 4)],
            k_send.at[i], k_recv.at[slot * 2 + core], i, base + owner_core,
            jnp.logical_and(row == i, core == owner_core),
        )
        copy.start()
        c_copies.append(copy)
    g_copy.wait_send()

    u_copies = []

    def pass_panel(index, piece, dx, dz):
        ref = panel.at[index] if piece is None else panel.at[index, pl.ds(piece * 2, 2)]
        n = len(u_copies)
        copy = remote(ref, ref, u_send.at[n], u_recv.at[n], at.row_at(dx, dz), me)
        copy.start()
        u_copies.append(copy)

    def panel_here(n, index, piece=None):
        ref = panel.at[index] if piece is None else panel.at[index, pl.ds(piece * 2, 2)]
        arrived(ref, u_recv.at[n])

    start_panel.wait()
    give = u_own.at[:, :, 1 - half_z]
    copy = remote(give, panel.at[row], u_send.at[0], u_recv.at[0], partner, me)
    copy.start()
    u_copies.append(copy)
    pass_panel(row, None, 1, 0)
    pass_panel(row, None, 3, 0)

    def d_block(n):
        chip = at.chip_at(*ORDER[n])
        left = jnp.concatenate([u_own[kk, chip].reshape(256, 128) for kk in range(4)], axis=1)
        value = dot(left, coupled[...])
        part[position(n), 0] = value[:128]
        part[position(n), 1] = value[128:]

    def second_leg():
        panel_here(0, partner)
        pass_panel(partner, None, 1, 0)
        pass_panel(partner, None, 3, 0)
        for n, dx in ((1, 3), (2, 1)):
            panel_here(n, at.row_at(dx, 0))
            pass_panel(at.row_at(dx, 0), n - 1, 4 - dx, 0)

    def third_leg():
        for n, dx in ((3, 3), (4, 1)):
            panel_here(n, at.row_at(dx, 1))
            pass_panel(at.row_at(dx, 1), n - 3, 4 - dx, 0)

    reduction = Reduction(
        at, part, sibbuf, None, d_hops, d_last, (di_send, di_recv, d_send, d_recv)
    )
    total = reduction.run(d_block)
    for j in range(8):
        dsum[j] = total[:, j * 128 : j * 128 + 128]

    gram_copies = []
    for c in range(8):
        value = sample[c] - dsum[cols_ref[c]]
        sample[c] = value
        gpart[c] = dot_t(value, value, HIGHEST)
        for h in range(2):
            copy = Send(
                gpart.at[c], grbuf.at[me], gr_send.at[c * 2 + h], gr_recv.at[me],
                row, c * 2 + h, me == c * 2 + h,
            )
            copy.start()
            gram_copies.append(copy)
    second_leg()
    gram = jnp.zeros((128, 128), F32)
    for m in range(16):
        arrived(grbuf.at[m], gr_recv.at[m])
        gram = gram + grbuf[m]
    inverse_factor(gram, work, inv)

    l_copies = []
    for n, step in enumerate(ORDER[:7]):
        copy = remote(
            inv, lbuf.at[at.chip], l_send.at[n], l_recv.at[at.chip], row, at.inner_at(*step)
        )
        copy.start()
        l_copies.append(copy)
    lbuf[at.chip] = inv[...]
    third_leg()
    for step in ORDER[:7]:
        source = at.chip_at(*step)
        arrived(lbuf.at[source], l_recv.at[source])
    for c in range(8):
        value = dot_nt(sample[c], lbuf[c], HIGHEST)
        left_ref[c] = value * scale
        bown[:, c * 128 : c * 128 + 128] = value.astype(BF16)

    b_copies, f_copies = [], []

    def block(m, half=None):
        rows = pl.ds(pl.multiple_of(m * 128, 128), 128)
        return basis.at[rows, :] if half is None else basis.at[rows, half]

    def pass_basis(source, dest, recv, dz, dy):
        copy = remote(source, dest, b_send.at[len(b_copies)], recv, row, at.inner_at(dz, dy))
        copy.start()
        b_copies.append(copy)

    def to_sib(source, dest, n):
        copy = remote(source, dest, f_send.at[n], f_recv.at[n], row, sib)
        copy.start()
        f_copies.append(copy)

    pass_basis(bown, block(me), b_recv.at[0], 1, 0)
    pass_basis(bown, block(me), b_recv.at[1], 0, 1)
    pass_basis(bown, block(me), b_recv.at[2], 0, 3)
    to_sib(bown, block(me), 0)
    basis[my_rows, :] = bown[...]
    other = at.inner_at(1, 0)
    arrived(block(other), b_recv.at[0])
    pass_basis(block(other), block(other), b_recv.at[3], 0, 1)
    pass_basis(block(other), block(other), b_recv.at[4], 0, 3)
    to_sib(block(other), block(other), 1)
    for s in range(2):
        for way, dy in ((0, 3), (1, 1)):
            m = at.inner_at(s, dy)
            half = HIGH if way else LOW
            n = 1 + s * 2 + way
            arrived(block(m), b_recv.at[n])
            pass_basis(block(m, half), block(m, half), bh_recv.at[s * 2 + way], 0, 3 if way else 1)
            to_sib(block(m), block(m), 1 + n)
    reduction.wait_sends()

    def basis_term(n, dz, dy, first=False):
        chip = at.chip_at(dz, dy)
        if n < 6:
            m = chip * 2 + 1 - core
            arrived(block(m), f_recv.at[n])
        rows = pl.ds(pl.multiple_of(chip * 256, 256), 256)
        for kk in range(4):
            for h in range(2):
                value = dot_t(u_own[kk, chip].reshape(256, 128), basis[rows, h * 512 : h * 512 + 512])
                gsib[kk * 2 + h] = value if first else gsib[kk * 2 + h] + value

    basis_term(0, 0, 0, True)
    basis_term(1, 1, 0)
    basis_term(2, 0, 3)
    basis_term(3, 0, 1)
    basis_term(4, 1, 3)
    basis_term(5, 1, 1)
    for s in range(2):
        m = at.inner_at(s, 2)
        for way in range(2):
            half = HIGH if way else LOW
            arrived(block(m, half), bh_recv.at[s * 2 + way])
            to_sib(block(m, half), block(m, half), 6 + s * 2 + way)
    for s in range(2):
        m = at.chip_at(s, 2) * 2 + 1 - core
        for way in range(2):
            arrived(block(m, HIGH if way else LOW), f_recv.at[6 + s * 2 + way])
        basis_term(6 + s, s, 2)

    for kk in range(4):
        for hh in range(2):
            arrived(coupling.at[kk, pl.ds(hh * 4, 4)], k_recv.at[kk * 2 + hh])
    i_copies = []
    for kk in range(4):
        for c in range(8):
            lanes = pl.ds((c % 4) * 128, 128)
            ib[half_z, kk * 128 : kk * 128 + 128, c * 128 : c * 128 + 128] = dot_t(
                coupling[kk, cols_ref[c]], gsib[kk * 2 + c // 4, :, lanes], HIGHEST
            ).astype(BF16)
        ref = ib.at[half_z, pl.ds(kk * 128, 128), :]
        copy = remote(ref, ref, i_send.at[kk], i_recv.at[kk], partner, me)
        copy.start()
        i_copies.append(copy)
    panel_here(5, at.row_at(2, 0), 0)
    panel_here(6, at.row_at(2, 0), 1)
    panel_here(7, at.row_at(2, 1), 0)
    panel_here(8, at.row_at(2, 1), 1)

    def terms(s, which, cols):
        chips = pl.ds(pl.multiple_of(lax.rem(at.z + s, 2) * 4, 4), 4)
        for c in range(8):
            lanes = pl.ds(c * 128, 128)
            col = cols[c]
            left = jnp.concatenate(
                [panel[col, kk, chips].reshape(512, 128) for kk in range(4)], axis=1
            )
            value = dot(left, ib[which, :, lanes])
            for y in range(4):
                part[s * 4 + lax.rem(y + 4 - at.y, 4), which, :, lanes] = value[
                    y * 128 : y * 128 + 128
                ]

    terms(1, half_z, cols_ref)
    terms(0, half_z, cols_ref)
    arrived(their_cols, cols_sem.at[1])
    for kk in range(4):
        arrived(ib.at[1 - half_z, pl.ds(kk * 128, 128), :], i_recv.at[kk])

    def r_block(n):
        if n % 4 == 0:
            terms(1 - n // 4, 1 - half_z, their_cols)

    def p_basis():
        for t in range(2):
            if t == 1:
                again = pltpu.make_async_copy(p_ref.at[pl.ds(4, 4)], tiles, local.at[3])
                again.start()
                again.wait()
            for c in range(4):
                n = t * 4 + c
                mid[n] = dot_t(tiles[c], basis[:, n * 128 : n * 128 + 128])
        for c in range(8):
            sample[c] = dot(q_rows[c].astype(F32), mid[c], HIGHEST)

    load_tiles.wait()
    load_q.wait()
    projection = Reduction(
        at, part, sibbuf, vbuf, r_hops, r_last, (ri_send, ri_recv, r_send, r_recv)
    )
    total = projection.run(r_block, p_basis)

    def write_right(source):
        for c in range(8):
            right_ref[c] = (sample[c] - source[:, c * 128 : c * 128 + 128]) * (1.0 / scale)

    swap = remote(total, swapped, t_send, t_recv, partner, sib)

    @pl.when(core == half_z)
    def _():
        write_right(total)

    @pl.when(core != half_z)
    def _():
        swap.start()
        swap.wait_recv()
        write_right(swapped)
        swap.wait_send()

    cols_copy.wait_send()
    for copy in v_copies + s_copies + c_copies + u_copies + gram_copies + l_copies:
        copy.wait_send()
    for copy in b_copies + f_copies + i_copies:
        copy.wait_send()
    projection.wait_sends()


def update(u, v, p, q, sketch, cols, scale):
    dma = pltpu.SemaphoreType.DMA
    vmem = pl.BlockSpec(memory_space=pltpu.VMEM)
    smem = pl.BlockSpec(memory_space=pltpu.SMEM)
    hbm = pl.BlockSpec(memory_space=pl.ANY)

    def kernel(*refs):
        update_kernel(scale, *refs)

    squares = jax.ShapeDtypeStruct((8, 128, 128), F32)
    return pl.pallas_call(
        kernel,
        out_shape=(squares, squares),
        in_specs=[smem, hbm, hbm, hbm, hbm, vmem],
        out_specs=(vmem, vmem),
        scratch_shapes=[
            pltpu.VMEM((8, 4, 8, 128, 128), BF16),
            pltpu.VMEM((1024, 1024), BF16),
            pltpu.VMEM((4, 128, 128), F32),
            pltpu.VMEM((4, 128, 128), F32),
            pltpu.VMEM((8, 4, 128, 128), F32),
            pltpu.VMEM((8, 128, 512), F32),
            pltpu.VMEM((1024, 512), BF16),
            pltpu.VMEM((512, 1024), BF16),
            pltpu.VMEM((4, 8, 128, 128), F32),
            pltpu.VMEM((4, 2048, 128), BF16),
            pltpu.VMEM((8, 128, 128), F32),
            pltpu.VMEM((8, 128, 128), BF16),
            pltpu.VMEM((8, 128, 128), BF16),
            pltpu.VMEM((8, 2, 128, 1024), F32),
            pltpu.VMEM((8, 128, 1024), F32),
            pltpu.VMEM((12, 128, 512), F32),
            pltpu.VMEM((128, 1024), F32),
            pltpu.VMEM((12, 128, 512), BF16),
            pltpu.VMEM((128, 1024), F32),
            pltpu.VMEM((8, 128, 128), F32),
            pltpu.VMEM((8, 128, 128), F32),
            pltpu.VMEM((8, 128, 128), F32),
            pltpu.VMEM((16, 128, 128), F32),
            pltpu.VMEM((128, 128), F32),
            pltpu.VMEM((128, 128), F32),
            pltpu.VMEM((8, 128, 128), F32),
            pltpu.VMEM((128, 1024), BF16),
            pltpu.VMEM((2048, 1024), BF16),
            pltpu.VMEM((2, 512, 1024), BF16),
            dma((5,)), dma((8,)), dma((8,)), dma((4,)), dma((4,)), dma, dma,
            dma((8,)), dma((8,)), dma((8,)), dma((8,)),
            dma((9,)), dma((9,)), dma((8,)), dma((8,)), dma((13,)), dma((13,)),
            dma((16,)), dma((16,)), dma((7,)), dma((8,)),
            dma((9,)), dma((5,)), dma((4,)), dma((10,)), dma((10,)),
            dma((8,)), dma((8,)), dma((13,)), dma((13,)),
            pltpu.VMEM((4, 8, 2, 128, 128), BF16),
            pltpu.SMEM((8,), jnp.int32),
            pltpu.VMEM((128, 1024), F32),
            dma((2,)), dma((4,)), dma((4,)), dma, dma,
        ],
        compiler_params=pltpu.CompilerParams(
            collective_id=1, has_side_effects=True, vmem_limit_bytes=VMEM_LIMIT
        ),
        cost_estimate=pl.CostEstimate(
            flops=13_000_000_000, bytes_accessed=30_000_000, transcendentals=0
        ),
    )(cols, u, v, p, q, sketch)


def body(left_u, left_v, tile_p, tile_q, sketch, tile_cols):
    factor_scale = math.sqrt(sketch.shape[0])
    new_left, new_right = update(
        left_u[0].reshape(4, 8, 2, 128, 128), left_v[0], tile_p[0], tile_q[0], sketch, tile_cols[0], factor_scale
    )
    return new_left[None], new_right[None]


def solution(mesh):
    return jax.shard_map(
        body,
        mesh=mesh,
        in_specs=(
            P("rows", "inner", None, None),
            P("rows", "inner", None, None),
            P("rows", None, None, None),
            P("rows", None, None, None),
            P(),
            P("rows", None),
        ),
        out_specs=(P("rows", None, "inner", None), P("rows", None, "inner", None)),
        check_vma=False,
    )
```

```python
import math

import jax
import jax.numpy as jnp
from jax import lax
from jax.experimental import pallas as pl
from jax.experimental.pallas import tpu as pltpu
from jax.sharding import PartitionSpec as P

MESH = pl.DeviceIdType.MESH
HIGHEST = lax.Precision.HIGHEST
F32 = jnp.float32
BF16 = jnp.bfloat16
VMEM_LIMIT = 61 * 1024 * 1024


def device(row, place):
    return {"rows": row, "inner": place}


def greet(partners, count):
    barrier = pltpu.get_barrier_semaphore()
    for row, place in partners:
        pl.semaphore_signal(barrier, inc=1, device_id=device(row, place), device_id_type=MESH)
    pl.semaphore_wait(barrier, count)


def remote(src, dst, send_sem, recv_sem, row, place):
    return pltpu.make_async_remote_copy(
        src_ref=src, dst_ref=dst, send_sem=send_sem, recv_sem=recv_sem,
        device_id=device(row, place), device_id_type=MESH,
    )


class Send:
    def __init__(self, src, dst, send_sem, recv_sem, row, place, is_self):
        self.far = remote(src, dst, send_sem, recv_sem, row, place)
        self.near = pltpu.make_async_copy(src, dst, recv_sem)
        self.is_self = is_self

    def start(self):
        @pl.when(jnp.logical_not(self.is_self))
        def _():
            self.far.start()

        @pl.when(self.is_self)
        def _():
            self.near.start()

    def wait_send(self):
        @pl.when(jnp.logical_not(self.is_self))
        def _():
            self.far.wait_send()


def arrived(ref, sem):
    pltpu.make_async_copy(ref, ref, sem).wait()


def dot(a, b, precision=None):
    return jnp.dot(a, b, preferred_element_type=F32, precision=precision)


def dot_t(a, b, precision=None):
    return lax.dot_general(
        a, b, (((0,), (0,)), ((), ())), preferred_element_type=F32, precision=precision
    )


def dot_nt(a, b, precision=None):
    return lax.dot_general(
        a, b, (((1,), (1,)), ((), ())), preferred_element_type=F32, precision=precision
    )

LOW, HIGH = pl.ds(0, 512), pl.ds(512, 512)
ORDER = [(1, 2), (1, 1), (1, 3), (1, 0), (0, 2), (0, 1), (0, 3), (0, 0)]


def position(n):
    return ORDER[n][0] * 4 + ORDER[n][1]


class Place:
    def __init__(self):
        self.row, self.me = lax.axis_index("rows"), lax.axis_index("inner")
        self.core = lax.rem(self.me, 2)
        self.chip = self.me // 2
        self.z, self.y = self.chip // 4, lax.rem(self.chip, 4)
        self.base = self.me - self.core
        self.sib = self.base + 1 - self.core

    def chip_at(self, dz, dy):
        return lax.rem(self.z + dz, 2) * 4 + lax.rem(self.y + dy, 4)

    def inner_at(self, dz, dy):
        return self.chip_at(dz, dy) * 2 + self.core

    def row_at(self, dx, dz):
        x, z = self.row // 2, lax.rem(self.row, 2)
        return lax.rem(x + dx, 4) * 2 + lax.rem(z + dz, 2)


def inverse_factor(gram, work, inv):
    order = gram.shape[0]
    strip = 16
    row_id = lax.broadcasted_iota(jnp.int32, (order, order), 0)
    col_id = lax.broadcasted_iota(jnp.int32, (order, order), 1)
    diagonal = row_id == col_id
    ridge = 1e-06 * jnp.sum(jnp.where(diagonal, gram, 0.0)) / order
    work[...] = gram + jnp.where(diagonal, ridge, 0.0)
    inv[...] = jnp.where(diagonal, 1.0, 0.0)
    within = lax.broadcasted_iota(jnp.int32, (strip, order), 0)
    for lo in range(0, order, strip):
        a, m = work[lo : lo + strip, :], inv[lo : lo + strip, :]
        for j in range(strip):
            scale = lax.rsqrt(a[j : j + 1, lo + j : lo + j + 1])
            a_row, m_row = a[j : j + 1, :] * scale, m[j : j + 1, :] * scale
            factor = jnp.where(within > j, a[:, lo + j : lo + j + 1] * scale, 0.0)
            a = jnp.where(within == j, a_row, a - factor * a_row)
            m = jnp.where(within == j, m_row, m - factor * m_row)
        inv[lo : lo + strip, :] = m
        rest = lo + strip
        if rest < order:
            update = dot_t(a, jnp.concatenate([a, m], axis=1), HIGHEST)
            work[rest:, :] = work[rest:, :] - update[rest:, :order]
            inv[rest:, :] = inv[rest:, :] - update[rest:, order:]


class Reduction:
    def __init__(self, at, part, sibbuf, wire, hops, last, sems):
        self.at, self.part, self.sibbuf = at, part, sibbuf
        self.wire, self.hops, self.last = wire, hops, last
        self.i_send, self.i_recv, self.send, self.recv = sems
        self.copies, self.inner = [], []

    def own(self, n):
        return self.part.at[position(n), self.at.core]

    def to_sibling(self, n):
        at = self.at
        return remote(
            self.part.at[position(n), 1 - at.core], self.sibbuf.at[n],
            self.i_send.at[n], self.i_recv.at[n], at.row, at.sib,
        )

    def offer(self, n):
        copy = self.to_sibling(n)
        copy.start()
        self.inner.append(copy)

    def merge(self, n):
        arrived(self.sibbuf.at[n], self.i_recv.at[n])
        own = self.own(n)
        own[...] = own[...] + self.sibbuf[n]

    def hop(self, n, half, s, kind, way):
        at = self.at
        if self.wire is None:
            source = self.part.at[position(n), at.core, :, half]
        else:
            source = self.wire.at[pl.ds(n * 128, 128), half]
            source[...] = self.own(n)[:, half].astype(source.dtype)
        slot = (s * 3 + kind) * 2 + way
        to = at.inner_at(0, 1 if way == 0 else 3)
        copy = remote(source, self.hops.at[slot], self.send.at[slot], self.recv.at[slot], at.row, to)
        copy.start()
        self.copies.append(copy)

    def took(self, s, kind, way):
        slot = (s * 3 + kind) * 2 + way
        arrived(self.hops.at[slot], self.recv.at[slot])
        return self.hops[slot].astype(F32)

    def act(self, n):
        s, dy = ORDER[n]
        self.merge(n)
        if dy == 2:
            self.hop(n, LOW, s, 0, 0)
            self.hop(n, HIGH, s, 0, 1)
        elif dy == 1:
            self.hop(n, HIGH, s, 1, 0)
        elif dy == 3:
            self.hop(n, LOW, s, 1, 1)

    def relay(self, s):
        first = 4 * (1 - s)
        for n, half, way in ((first + 1, LOW, 0), (first + 2, HIGH, 1)):
            own = self.own(n)
            own[:, half] = own[:, half] + self.took(s, 0, way)
            self.hop(n, half, s, 2, way)

    def finish(self, s):
        own = self.own(4 * (1 - s) + 3)
        for half, kinds in ((LOW, (2, 1)), (HIGH, (1, 2))):
            own[:, half] = own[:, half] + self.took(s, kinds[0], 0) + self.took(s, kinds[1], 1)
        if s == 1:
            at = self.at
            copy = remote(
                own, self.last, self.send.at[12], self.recv.at[12], at.row, at.inner_at(1, 0)
            )
            copy.start()
            self.copies.append(copy)

    def total(self):
        arrived(self.last, self.recv.at[12])
        own = self.own(7)
        own[...] = own[...] + self.last[...]
        return own

    def run(self, compute):
        for n in range(8):
            compute(n)
            self.offer(n)
            if 1 <= n <= 4:
                self.act(n - 1)
        return self.rest()

    def rest(self):
        self.relay(1)
        for n in range(4, 8):
            self.act(n)
        self.finish(1)
        self.relay(0)
        self.finish(0)
        return self.total()

    def wait_sends(self):
        for copy in self.inner + self.copies:
            copy.wait_send()


def update_kernel(
    scale, cols_ref, u_ref, v_ref, p_ref, q_ref, sketch_ref, left_ref, right_ref,
    panel, vbuf, sown, sbuf, gown, gsib, cown, coupled, coupling,
    tiles, mid, p_rows, q_rows, part, sibbuf, d_hops, d_last, r_hops, r_last,
    sample, dsum, gpart, grbuf, work, inv, lbuf, bown, basis, ib,
    local, v_send, v_recv, s_send, s_recv, g_send, g_recv, c_send, c_recv, k_send, k_recv,
    u_send, u_recv, di_send, di_recv, d_send, d_recv, gr_send, gr_recv, l_send, l_recv,
    b_send, b_recv, bh_recv, f_send, f_recv, ri_send, ri_recv, r_send, r_recv,
    u_own, their_cols, swapped, cols_sem, i_send, i_recv, t_send, t_recv,
):
    at = Place()
    row, me, core, base, sib = at.row, at.me, at.core, at.base, at.sib
    owner_core = row // 4
    slot = lax.rem(row, 4)
    my_rows = pl.ds(pl.multiple_of(me * 128, 128), 128)

    half_z = lax.rem(row, 2)
    partner = at.row_at(0, 1)
    own_u = pltpu.make_async_copy(u_ref, u_own, local.at[0])
    own_u.start()
    start_panel = pltpu.make_async_copy(u_ref.at[:, :, half_z], panel.at[row], local.at[4])
    start_panel.start()
    load_p = pltpu.make_async_copy(p_ref.at[:, my_rows, :], p_rows, local.at[1])
    load_p.start()
    load_q = pltpu.make_async_copy(q_ref.at[:, my_rows, :], q_rows, local.at[2])
    load_q.start()
    load_tiles = pltpu.make_async_copy(q_ref.at[pl.ds(0, 4)], tiles, local.at[3])
    load_tiles.start()

    partners = [(lax.rem(row + d, 8), base + h) for d in range(1, 8) for h in range(2)]
    partners += [(row, lax.rem(me + d, 16)) for d in range(1, 16)]
    greet(partners, len(partners))
    cols_copy = remote(cols_ref, their_cols, cols_sem.at[0], cols_sem.at[1], partner, me)
    cols_copy.start()

    v_copies = []
    for n in range(8):
        kk, hh = lax.rem(slot + n // 2, 4), lax.rem(n + core, 2)
        to = core * 4 + kk
        copy = Send(
            v_ref.at[kk, pl.ds(pl.multiple_of(hh * 1024, 1024), 1024), :],
            vbuf.at[:, pl.ds(pl.multiple_of(row * 128, 128), 128)],
            v_send.at[n], v_recv.at[row], to, base + hh,
            jnp.logical_and(to == row, core == hh),
        )
        copy.start()
        v_copies.append(copy)

    s_copies = []
    own_u.wait()
    for kk in range(4):
        sown[kk] = dot_t(u_own[kk].reshape(2048, 128), sketch_ref[...])
        to = core * 4 + kk
        copy = Send(
            sown.at[kk], sbuf.at[slot], s_send.at[kk], s_recv.at[slot],
            to, base + owner_core, jnp.logical_and(to == row, core == owner_core),
        )
        copy.start()
        s_copies.append(copy)

    load_tiles.wait()
    for c in range(4):
        mid[c] = dot_t(tiles[c], sketch_ref[...])
    load_tiles = pltpu.make_async_copy(q_ref.at[pl.ds(4, 4)], tiles, local.at[3])
    load_tiles.start()
    load_tiles.wait()
    for c in range(4):
        mid[4 + c] = dot_t(tiles[c], sketch_ref[...])
    load_p.wait()
    for c in range(8):
        sample[c] = dot(p_rows[c].astype(F32), mid[c], HIGHEST)
    load_tiles = pltpu.make_async_copy(p_ref.at[pl.ds(0, 4)], tiles, local.at[3])
    load_tiles.start()

    for i in range(8):
        arrived(vbuf.at[:, pl.ds(i * 128, 128)], v_recv.at[i])

    def gram_pair(pair, half):
        right = vbuf[:, pl.ds(pl.multiple_of(half * 512, 512), 512)]
        return dot_t(vbuf[:, pl.ds(pair * 256, 256)], right)

    g_copies = []
    for pair in range(4):
        value = gram_pair(pair, 1 - core)
        for p in range(2):
            part[pair * 2 + p, 0, :, :512] = value[p * 128 : p * 128 + 128]
        two = pl.ds(pair * 2, 2)
        copy = remote(
            part.at[two, 0, :, LOW], gsib.at[two], g_send.at[pair], g_recv.at[pair], row, sib
        )
        copy.start()
        g_copies.append(copy)
    for pair in range(4):
        value = gram_pair(pair, core)
        for p in range(2):
            for j in range(4):
                gown[pair * 2 + p, j] = value[p * 128 : p * 128 + 128, j * 128 : j * 128 + 128]
    for j in range(4):
        arrived(sbuf.at[j], s_recv.at[j])
    c_copies = []
    for i in range(8):
        if i % 2 == 0:
            g_copies[i // 2].wait_recv()
        for j in range(4):
            total = gown[i, j] + gsib[i, :, j * 128 : j * 128 + 128]
            gown[i, j] = total
            cown[i * 128 : i * 128 + 128, j * 128 : j * 128 + 128] = dot(
                total, sbuf[j], HIGHEST
            ).astype(BF16)
        copy = Send(
            cown.at[pl.ds(i * 128, 128), :],
            coupled.at[
                pl.ds(pl.multiple_of(slot * 128, 128), 128),
                pl.ds(pl.multiple_of(core * 512, 512), 512),
            ],
            c_send.at[i], c_recv.at[slot * 2 + core], i, base + owner_core,
            jnp.logical_and(row == i, core == owner_core),
        )
        copy.start()
        c_copies.append(copy)
    for kk in range(4):
        for hh in range(2):
            arrived(
                coupled.at[pl.ds(kk * 128, 128), pl.ds(hh * 512, 512)], c_recv.at[kk * 2 + hh]
            )
    for i in range(8):
        copy = Send(
            gown.at[i], coupling.at[slot, pl.ds(core * 4, 4)],
            k_send.at[i], k_recv.at[slot * 2 + core], i, base + owner_core,
            jnp.logical_and(row == i, core == owner_core),
        )
        copy.start()
        c_copies.append(copy)
    for copy in g_copies:
        copy.wait_send()

    u_copies = []

    def pass_panel(index, piece, dx, dz):
        ref = panel.at[index] if piece is None else panel.at[index, pl.ds(piece * 2, 2)]
        n = len(u_copies)
        copy = remote(ref, ref, u_send.at[n], u_recv.at[n], at.row_at(dx, dz), me)
        copy.start()
        u_copies.append(copy)

    def panel_here(n, index, piece=None):
        ref = panel.at[index] if piece is None else panel.at[index, pl.ds(piece * 2, 2)]
        arrived(ref, u_recv.at[n])

    start_panel.wait()
    give = u_own.at[:, :, 1 - half_z]
    copy = remote(give, panel.at[row], u_send.at[0], u_recv.at[0], partner, me)
    copy.start()
    u_copies.append(copy)
    pass_panel(row, None, 1, 0)
    pass_panel(row, None, 3, 0)

    def d_block(n):
        chip = at.chip_at(*ORDER[n])
        left = jnp.concatenate([u_own[kk, chip].reshape(256, 128) for kk in range(4)], axis=1)
        value = dot(left, coupled[...])
        part[position(n), 0] = value[:128]
        part[position(n), 1] = value[128:]

    def second_leg():
        panel_here(0, partner)
        pass_panel(partner, None, 1, 0)
        pass_panel(partner, None, 3, 0)
        for n, dx in ((1, 3), (2, 1)):
            panel_here(n, at.row_at(dx, 0))
            pass_panel(at.row_at(dx, 0), n - 1, 4 - dx, 0)

    def third_leg():
        for n, dx in ((3, 3), (4, 1)):
            panel_here(n, at.row_at(dx, 1))
            pass_panel(at.row_at(dx, 1), n - 3, 4 - dx, 0)

    reduction = Reduction(
        at, part, sibbuf, None, d_hops, d_last, (di_send, di_recv, d_send, d_recv)
    )
    total = reduction.run(d_block)
    for j in range(8):
        dsum[j] = total[:, j * 128 : j * 128 + 128]

    gram_copies = []
    for c in range(8):
        value = sample[c] - dsum[cols_ref[c]]
        sample[c] = value
        gpart[c] = dot_t(value, value, HIGHEST)
        to = c * 2 + c % 2
        copy = Send(
            gpart.at[c], grbuf.at[me], gr_send.at[c], gr_recv.at[me], row, to, me == to
        )
        copy.start()
        gram_copies.append(copy)
    second_leg()
    factors = core == lax.rem(at.chip, 2)
    l_copies = []
    for n, step in enumerate(ORDER[:7]):
        for h in range(2):
            l_copies.append(
                remote(
                    inv, lbuf.at[at.chip], l_send.at[n * 2 + h], l_recv.at[at.chip],
                    row, at.chip_at(*step) * 2 + h,
                )
            )
    l_copies.append(remote(inv, lbuf.at[at.chip], l_send.at[14], l_recv.at[at.chip], row, sib))

    @pl.when(factors)
    def _():
        gram = jnp.zeros((128, 128), F32)
        for m in range(16):
            arrived(grbuf.at[m], gr_recv.at[m])
            gram = gram + grbuf[m]
        inverse_factor(gram, work, inv)
        for copy in l_copies:
            copy.start()
        lbuf[at.chip] = inv[...]

    @pl.when(jnp.logical_not(factors))
    def _():
        arrived(lbuf.at[at.chip], l_recv.at[at.chip])

    third_leg()
    for step in ORDER[:7]:
        source = at.chip_at(*step)
        arrived(lbuf.at[source], l_recv.at[source])
    for c in range(8):
        value = dot_nt(sample[c], lbuf[c], HIGHEST)
        left_ref[c] = value * scale
        bown[:, c * 128 : c * 128 + 128] = value.astype(BF16)

    b_copies, f_copies = [], []

    def block(m, half=None):
        rows = pl.ds(pl.multiple_of(m * 128, 128), 128)
        return basis.at[rows, :] if half is None else basis.at[rows, half]

    def pass_basis(source, dest, recv, dz, dy):
        copy = remote(source, dest, b_send.at[len(b_copies)], recv, row, at.inner_at(dz, dy))
        copy.start()
        b_copies.append(copy)

    def to_sib(source, dest, n):
        copy = remote(source, dest, f_send.at[n], f_recv.at[n], row, sib)
        copy.start()
        f_copies.append(copy)

    pass_basis(bown, block(me), b_recv.at[0], 1, 0)
    pass_basis(bown, block(me), b_recv.at[1], 0, 1)
    pass_basis(bown, block(me), b_recv.at[2], 0, 3)
    to_sib(bown, block(me), 0)
    basis[my_rows, :] = bown[...]
    other = at.inner_at(1, 0)
    arrived(block(other), b_recv.at[0])
    pass_basis(block(other), block(other), b_recv.at[3], 0, 1)
    pass_basis(block(other), block(other), b_recv.at[4], 0, 3)
    to_sib(block(other), block(other), 1)
    for s in range(2):
        for way, dy in ((0, 3), (1, 1)):
            m = at.inner_at(s, dy)
            half = HIGH if way else LOW
            n = 1 + s * 2 + way
            arrived(block(m), b_recv.at[n])
            pass_basis(block(m, half), block(m, half), bh_recv.at[s * 2 + way], 0, 3 if way else 1)
            to_sib(block(m), block(m), 1 + n)
    reduction.wait_sends()

    def basis_term(n, dz, dy, first=False):
        chip = at.chip_at(dz, dy)
        if n < 6:
            m = chip * 2 + 1 - core
            arrived(block(m), f_recv.at[n])
        rows = pl.ds(pl.multiple_of(chip * 256, 256), 256)
        for kk in range(4):
            for h in range(2):
                value = dot_t(u_own[kk, chip].reshape(256, 128), basis[rows, h * 512 : h * 512 + 512])
                gsib[kk * 2 + h] = value if first else gsib[kk * 2 + h] + value

    basis_term(0, 0, 0, True)
    basis_term(1, 1, 0)
    basis_term(2, 0, 3)
    basis_term(3, 0, 1)
    basis_term(4, 1, 3)
    basis_term(5, 1, 1)
    for s in range(2):
        m = at.inner_at(s, 2)
        for way in range(2):
            half = HIGH if way else LOW
            arrived(block(m, half), bh_recv.at[s * 2 + way])
            to_sib(block(m, half), block(m, half), 6 + s * 2 + way)
    for s in range(2):
        m = at.chip_at(s, 2) * 2 + 1 - core
        for way in range(2):
            arrived(block(m, HIGH if way else LOW), f_recv.at[6 + s * 2 + way])
        basis_term(6 + s, s, 2)

    for kk in range(4):
        for hh in range(2):
            arrived(coupling.at[kk, pl.ds(hh * 4, 4)], k_recv.at[kk * 2 + hh])
    i_copies = []
    for kk in range(4):
        for c in range(8):
            lanes = pl.ds((c % 4) * 128, 128)
            ib[half_z, kk * 128 : kk * 128 + 128, c * 128 : c * 128 + 128] = dot_t(
                coupling[kk, cols_ref[c]], gsib[kk * 2 + c // 4, :, lanes], HIGHEST
            ).astype(BF16)
        ref = ib.at[half_z, pl.ds(kk * 128, 128), :]
        copy = remote(ref, ref, i_send.at[kk], i_recv.at[kk], partner, me)
        copy.start()
        i_copies.append(copy)
    panel_here(5, at.row_at(2, 0), 0)
    panel_here(6, at.row_at(2, 0), 1)
    panel_here(7, at.row_at(2, 1), 0)
    panel_here(8, at.row_at(2, 1), 1)

    def terms(s, which, cols):
        chips = pl.ds(pl.multiple_of(lax.rem(at.z + s, 2) * 4, 4), 4)
        for c in range(8):
            lanes = pl.ds(c * 128, 128)
            col = cols[c]
            left = jnp.concatenate(
                [panel[col, kk, chips].reshape(512, 128) for kk in range(4)], axis=1
            )
            value = dot(left, ib[which, :, lanes])
            for y in range(4):
                part[s * 4 + lax.rem(y + 4 - at.y, 4), which, :, lanes] = value[
                    y * 128 : y * 128 + 128
                ]

    mine = core == half_z
    others = core != half_z

    def projection():
        return Reduction(
            at, part, sibbuf, vbuf, r_hops, r_last, (ri_send, ri_recv, r_send, r_recv)
        )

    offers = [projection().to_sibling(n) for n in range(8)]
    for s in range(2):
        terms(1 - s, half_z, cols_ref)

        @pl.when(others)
        def _():
            for n in range(4):
                offers[s * 4 + n].start()

    @pl.when(mine)
    def _():
        sums = projection()
        for n in range(4):
            sums.act(n)
        sums.rest()
        for copy in sums.copies:
            copy.wait_send()

    def p_basis():
        for t in range(2):
            if t == 1:
                again = pltpu.make_async_copy(p_ref.at[pl.ds(4, 4)], tiles, local.at[3])
                again.start()
                again.wait()
            for c in range(4):
                n = t * 4 + c
                mid[n] = dot_t(tiles[c], basis[:, n * 128 : n * 128 + 128])
        for c in range(8):
            sample[c] = dot(q_rows[c].astype(F32), mid[c], HIGHEST)

    load_tiles.wait()
    load_q.wait()
    p_basis()
    arrived(their_cols, cols_sem.at[1])
    for kk in range(4):
        arrived(ib.at[1 - half_z, pl.ds(kk * 128, 128), :], i_recv.at[kk])
    for s in range(2):
        terms(1 - s, 1 - half_z, their_cols)

        @pl.when(mine)
        def _():
            for n in range(4):
                offers[s * 4 + n].start()

    def write_right(source):
        for c in range(8):
            right_ref[c] = (sample[c] - source[:, c * 128 : c * 128 + 128]) * (1.0 / scale)

    @pl.when(mine)
    def _():
        write_right(projection().own(7))

    @pl.when(others)
    def _():
        sums = projection()
        for n in range(4):
            sums.act(n)
        swap = remote(sums.rest(), swapped, t_send, t_recv, partner, sib)
        swap.start()
        for copy in sums.copies:
            copy.wait_send()
        swap.wait_recv()
        write_right(swapped)
        swap.wait_send()

    for copy in offers:
        copy.wait_send()
    cols_copy.wait_send()

    @pl.when(factors)
    def _():
        for copy in l_copies:
            copy.wait_send()

    for copy in v_copies + s_copies + c_copies + u_copies + gram_copies:
        copy.wait_send()
    for copy in b_copies + f_copies + i_copies:
        copy.wait_send()


def update(u, v, p, q, sketch, cols, scale):
    dma = pltpu.SemaphoreType.DMA
    vmem = pl.BlockSpec(memory_space=pltpu.VMEM)
    smem = pl.BlockSpec(memory_space=pltpu.SMEM)
    hbm = pl.BlockSpec(memory_space=pl.ANY)

    def kernel(*refs):
        update_kernel(scale, *refs)

    squares = jax.ShapeDtypeStruct((8, 128, 128), F32)
    return pl.pallas_call(
        kernel,
        out_shape=(squares, squares),
        in_specs=[smem, hbm, hbm, hbm, hbm, vmem],
        out_specs=(vmem, vmem),
        scratch_shapes=[
            pltpu.VMEM((8, 4, 8, 128, 128), BF16),
            pltpu.VMEM((1024, 1024), BF16),
            pltpu.VMEM((4, 128, 128), F32),
            pltpu.VMEM((4, 128, 128), F32),
            pltpu.VMEM((8, 4, 128, 128), F32),
            pltpu.VMEM((8, 128, 512), F32),
            pltpu.VMEM((1024, 512), BF16),
            pltpu.VMEM((512, 1024), BF16),
            pltpu.VMEM((4, 8, 128, 128), F32),
            pltpu.VMEM((4, 2048, 128), BF16),
            pltpu.VMEM((8, 128, 128), F32),
            pltpu.VMEM((8, 128, 128), BF16),
            pltpu.VMEM((8, 128, 128), BF16),
            pltpu.VMEM((8, 2, 128, 1024), F32),
            pltpu.VMEM((8, 128, 1024), F32),
            pltpu.VMEM((12, 128, 512), F32),
            pltpu.VMEM((128, 1024), F32),
            pltpu.VMEM((12, 128, 512), BF16),
            pltpu.VMEM((128, 1024), F32),
            pltpu.VMEM((8, 128, 128), F32),
            pltpu.VMEM((8, 128, 128), F32),
            pltpu.VMEM((8, 128, 128), F32),
            pltpu.VMEM((16, 128, 128), F32),
            pltpu.VMEM((128, 128), F32),
            pltpu.VMEM((128, 128), F32),
            pltpu.VMEM((8, 128, 128), F32),
            pltpu.VMEM((128, 1024), BF16),
            pltpu.VMEM((2048, 1024), BF16),
            pltpu.VMEM((2, 512, 1024), BF16),
            dma((5,)), dma((8,)), dma((8,)), dma((4,)), dma((4,)), dma((4,)), dma((4,)),
            dma((8,)), dma((8,)), dma((8,)), dma((8,)),
            dma((9,)), dma((9,)), dma((8,)), dma((8,)), dma((13,)), dma((13,)),
            dma((8,)), dma((16,)), dma((15,)), dma((8,)),
            dma((9,)), dma((5,)), dma((4,)), dma((10,)), dma((10,)),
            dma((8,)), dma((8,)), dma((13,)), dma((13,)),
            pltpu.VMEM((4, 8, 2, 128, 128), BF16),
            pltpu.SMEM((8,), jnp.int32),
            pltpu.VMEM((128, 1024), F32),
            dma((2,)), dma((4,)), dma((4,)), dma, dma,
        ],
        compiler_params=pltpu.CompilerParams(
            collective_id=1, has_side_effects=True, vmem_limit_bytes=VMEM_LIMIT
        ),
        cost_estimate=pl.CostEstimate(
            flops=13_000_000_000, bytes_accessed=30_000_000, transcendentals=0
        ),
    )(cols, u, v, p, q, sketch)


def body(left_u, left_v, tile_p, tile_q, sketch, tile_cols):
    factor_scale = math.sqrt(sketch.shape[0])
    new_left, new_right = update(
        left_u[0].reshape(4, 8, 2, 128, 128), left_v[0], tile_p[0], tile_q[0], sketch, tile_cols[0], factor_scale
    )
    return new_left[None], new_right[None]


def solution(mesh):
    return jax.shard_map(
        body,
        mesh=mesh,
        in_specs=(
            P("rows", "inner", None, None),
            P("rows", "inner", None, None),
            P("rows", None, None, None),
            P("rows", None, None, None),
            P(),
            P("rows", None),
        ),
        out_specs=(P("rows", None, "inner", None), P("rows", None, "inner", None)),
        check_vma=False,
    )
```

```python
import math

import jax
import jax.numpy as jnp
from jax import lax
from jax.experimental import pallas as pl
from jax.experimental.pallas import tpu as pltpu
from jax.sharding import PartitionSpec as P

MESH = pl.DeviceIdType.MESH
HIGHEST = lax.Precision.HIGHEST
F32 = jnp.float32
BF16 = jnp.bfloat16
VMEM_LIMIT = 61 * 1024 * 1024


def device(row, place):
    return {"rows": row, "inner": place}


def greet(partners, count):
    barrier = pltpu.get_barrier_semaphore()
    for row, place in partners:
        pl.semaphore_signal(barrier, inc=1, device_id=device(row, place), device_id_type=MESH)
    pl.semaphore_wait(barrier, count)


def remote(src, dst, send_sem, recv_sem, row, place):
    return pltpu.make_async_remote_copy(
        src_ref=src, dst_ref=dst, send_sem=send_sem, recv_sem=recv_sem,
        device_id=device(row, place), device_id_type=MESH,
    )


class Send:
    def __init__(self, src, dst, send_sem, recv_sem, row, place, is_self):
        self.far = remote(src, dst, send_sem, recv_sem, row, place)
        self.near = pltpu.make_async_copy(src, dst, recv_sem)
        self.is_self = is_self

    def start(self):
        @pl.when(jnp.logical_not(self.is_self))
        def _():
            self.far.start()

        @pl.when(self.is_self)
        def _():
            self.near.start()

    def wait_send(self):
        @pl.when(jnp.logical_not(self.is_self))
        def _():
            self.far.wait_send()


def arrived(ref, sem):
    pltpu.make_async_copy(ref, ref, sem).wait()


def dot(a, b, precision=None):
    return jnp.dot(a, b, preferred_element_type=F32, precision=precision)


def dot_t(a, b, precision=None):
    return lax.dot_general(
        a, b, (((0,), (0,)), ((), ())), preferred_element_type=F32, precision=precision
    )


def dot_nt(a, b, precision=None):
    return lax.dot_general(
        a, b, (((1,), (1,)), ((), ())), preferred_element_type=F32, precision=precision
    )

LOW, HIGH = pl.ds(0, 512), pl.ds(512, 512)
ORDER = [(1, 2), (1, 1), (1, 3), (1, 0), (0, 2), (0, 1), (0, 3), (0, 0)]


def position(n):
    return ORDER[n][0] * 4 + ORDER[n][1]


class Place:
    def __init__(self):
        self.row, self.me = lax.axis_index("rows"), lax.axis_index("inner")
        self.core = lax.rem(self.me, 2)
        self.chip = self.me // 2
        self.z, self.y = self.chip // 4, lax.rem(self.chip, 4)
        self.base = self.me - self.core
        self.sib = self.base + 1 - self.core

    def chip_at(self, dz, dy):
        return lax.rem(self.z + dz, 2) * 4 + lax.rem(self.y + dy, 4)

    def inner_at(self, dz, dy):
        return self.chip_at(dz, dy) * 2 + self.core

    def row_at(self, dx, dz):
        x, z = self.row // 2, lax.rem(self.row, 2)
        return lax.rem(x + dx, 4) * 2 + lax.rem(z + dz, 2)


def inverse_factor(gram, work, inv):
    order = gram.shape[0]
    strip, group = 16, 4
    row_id = lax.broadcasted_iota(jnp.int32, (order, order), 0)
    col_id = lax.broadcasted_iota(jnp.int32, (order, order), 1)
    diagonal = row_id == col_id
    ridge = 1e-06 * jnp.sum(jnp.where(diagonal, gram, 0.0)) / order
    work[...] = gram + jnp.where(diagonal, ridge, 0.0)
    inv[...] = jnp.where(diagonal, 1.0, 0.0)
    within = lax.broadcasted_iota(jnp.int32, (strip, order), 0)
    full = (strip, order)
    for lo in range(0, order, strip):
        a, m = work[lo : lo + strip, :], inv[lo : lo + strip, :]
        for first in range(0, strip, group):
            cols, rows, m_rows = [], [], []
            for k in range(group):
                at_col, at_row = lo + first + k, first + k
                cols.append(jnp.broadcast_to(a[:, at_col : at_col + 1], full))
                rows.append(jnp.broadcast_to(a[at_row : at_row + 1, :], full))
                m_rows.append(jnp.broadcast_to(m[at_row : at_row + 1, :], full))
            small = {}
            for k in range(group):
                for i in range(k, group):
                    at_row = first + i
                    value = jnp.broadcast_to(cols[k][at_row : at_row + 1, :], full)
                    for p in range(k):
                        value = value - small[i, p] * small[k, p]
                    small[i, k] = lax.rsqrt(value) if i == k else value * small[k, k]
            for k in range(group):
                for p in range(k):
                    cols[k] = cols[k] - small[k, p] * cols[p]
                    rows[k] = rows[k] - small[k, p] * rows[p]
                    m_rows[k] = m_rows[k] - small[k, p] * m_rows[p]
                cols[k] = cols[k] * small[k, k]
                rows[k] = rows[k] * small[k, k]
                m_rows[k] = m_rows[k] * small[k, k]
            below = within >= first + group
            for k in range(group):
                factor = jnp.where(below, cols[k], 0.0)
                a, m = a - factor * rows[k], m - factor * m_rows[k]
            for k in range(group):
                here = within == first + k
                a, m = jnp.where(here, rows[k], a), jnp.where(here, m_rows[k], m)
        inv[lo : lo + strip, :] = m
        rest = lo + strip
        if rest < order:
            update = dot_t(a, jnp.concatenate([a, m], axis=1), HIGHEST)
            work[rest:, :] = work[rest:, :] - update[rest:, :order]
            inv[rest:, :] = inv[rest:, :] - update[rest:, order:]


class Reduction:
    def __init__(self, at, part, sibbuf, wire, hops, last, sems):
        self.at, self.part, self.sibbuf = at, part, sibbuf
        self.wire, self.hops, self.last = wire, hops, last
        self.i_send, self.i_recv, self.send, self.recv = sems
        self.copies, self.inner = [], []

    def own(self, n):
        return self.part.at[position(n), self.at.core]

    def to_sibling(self, n):
        at = self.at
        return remote(
            self.part.at[position(n), 1 - at.core], self.sibbuf.at[n],
            self.i_send.at[n], self.i_recv.at[n], at.row, at.sib,
        )

    def offer(self, n):
        copy = self.to_sibling(n)
        copy.start()
        self.inner.append(copy)

    def merge(self, n):
        arrived(self.sibbuf.at[n], self.i_recv.at[n])
        own = self.own(n)
        own[...] = own[...] + self.sibbuf[n]

    def hop(self, n, half, s, kind, way):
        at = self.at
        if self.wire is None:
            source = self.part.at[position(n), at.core, :, half]
        else:
            source = self.wire.at[pl.ds(n * 128, 128), half]
            source[...] = self.own(n)[:, half].astype(source.dtype)
        slot = (s * 3 + kind) * 2 + way
        to = at.inner_at(0, 1 if way == 0 else 3)
        copy = remote(source, self.hops.at[slot], self.send.at[slot], self.recv.at[slot], at.row, to)
        copy.start()
        self.copies.append(copy)

    def took(self, s, kind, way):
        slot = (s * 3 + kind) * 2 + way
        arrived(self.hops.at[slot], self.recv.at[slot])
        return self.hops[slot].astype(F32)

    def act(self, n):
        s, dy = ORDER[n]
        self.merge(n)
        if dy == 2:
            self.hop(n, LOW, s, 0, 0)
            self.hop(n, HIGH, s, 0, 1)
        elif dy == 1:
            self.hop(n, HIGH, s, 1, 0)
        elif dy == 3:
            self.hop(n, LOW, s, 1, 1)

    def relay(self, s):
        first = 4 * (1 - s)
        for n, half, way in ((first + 1, LOW, 0), (first + 2, HIGH, 1)):
            own = self.own(n)
            own[:, half] = own[:, half] + self.took(s, 0, way)
            self.hop(n, half, s, 2, way)

    def finish(self, s):
        own = self.own(4 * (1 - s) + 3)
        for half, kinds in ((LOW, (2, 1)), (HIGH, (1, 2))):
            own[:, half] = own[:, half] + self.took(s, kinds[0], 0) + self.took(s, kinds[1], 1)
        if s == 1:
            at = self.at
            copy = remote(
                own, self.last, self.send.at[12], self.recv.at[12], at.row, at.inner_at(1, 0)
            )
            copy.start()
            self.copies.append(copy)

    def total(self):
        arrived(self.last, self.recv.at[12])
        own = self.own(7)
        own[...] = own[...] + self.last[...]
        return own

    def run(self, compute):
        for n in range(8):
            compute(n)
            self.offer(n)
            if 1 <= n <= 4:
                self.act(n - 1)
        return self.rest()

    def rest(self):
        self.relay(1)
        for n in range(4, 8):
            self.act(n)
        self.finish(1)
        self.relay(0)
        self.finish(0)
        return self.total()

    def wait_sends(self):
        for copy in self.inner + self.copies:
            copy.wait_send()


def update_kernel(
    scale, cols_ref, u_ref, v_ref, p_ref, q_ref, sketch_ref, left_ref, right_ref,
    panel, vbuf, sown, sbuf, gown, gsib, cown, coupled, coupling,
    tiles, mid, p_rows, q_rows, part, sibbuf, d_hops, d_last, r_hops, r_last,
    sample, dsum, gpart, grbuf, work, inv, lbuf, bown, basis, ib,
    local, v_send, v_recv, s_send, s_recv, g_send, g_recv, c_send, c_recv, k_send, k_recv,
    u_send, u_recv, di_send, di_recv, d_send, d_recv, gr_send, gr_recv, l_send, l_recv,
    b_send, b_recv, bh_recv, f_send, f_recv, ri_send, ri_recv, r_send, r_recv,
    u_own, their_cols, swapped, cols_sem, i_send, i_recv, t_send, t_recv,
):
    at = Place()
    row, me, core, base, sib = at.row, at.me, at.core, at.base, at.sib
    owner_core = row // 4
    slot = lax.rem(row, 4)
    my_rows = pl.ds(pl.multiple_of(me * 128, 128), 128)

    half_z = lax.rem(row, 2)
    partner = at.row_at(0, 1)
    own_u = pltpu.make_async_copy(u_ref, u_own, local.at[0])
    own_u.start()
    start_panel = pltpu.make_async_copy(u_ref.at[:, :, half_z], panel.at[row], local.at[4])
    start_panel.start()
    load_p = pltpu.make_async_copy(p_ref.at[:, my_rows, :], p_rows, local.at[1])
    load_p.start()
    load_q = pltpu.make_async_copy(q_ref.at[:, my_rows, :], q_rows, local.at[2])
    load_q.start()
    load_tiles = pltpu.make_async_copy(q_ref.at[pl.ds(0, 4)], tiles, local.at[3])
    load_tiles.start()

    partners = [(lax.rem(row + d, 8), base + h) for d in range(1, 8) for h in range(2)]
    partners += [(row, lax.rem(me + d, 16)) for d in range(1, 16)]
    greet(partners, len(partners))
    cols_copy = remote(cols_ref, their_cols, cols_sem.at[0], cols_sem.at[1], partner, me)
    cols_copy.start()

    v_copies = []
    for n in range(8):
        kk, hh = lax.rem(slot + n % 4, 4), lax.rem(n // 4 + core, 2)
        to = core * 4 + kk
        copy = Send(
            v_ref.at[kk, pl.ds(pl.multiple_of(hh * 1024, 1024), 1024), :],
            vbuf.at[:, pl.ds(pl.multiple_of(row * 128, 128), 128)],
            v_send.at[n], v_recv.at[row], to, base + hh,
            jnp.logical_and(to == row, core == hh),
        )
        copy.start()
        v_copies.append(copy)

    s_copies = []
    own_u.wait()
    for kk in range(4):
        sown[kk] = dot_t(u_own[kk].reshape(2048, 128), sketch_ref[...])
        to = core * 4 + kk
        copy = Send(
            sown.at[kk], sbuf.at[slot], s_send.at[kk], s_recv.at[slot],
            to, base + owner_core, jnp.logical_and(to == row, core == owner_core),
        )
        copy.start()
        s_copies.append(copy)

    load_tiles.wait()
    for c in range(4):
        mid[c] = dot_t(tiles[c], sketch_ref[...])
    load_tiles = pltpu.make_async_copy(q_ref.at[pl.ds(4, 4)], tiles, local.at[3])
    load_tiles.start()
    load_tiles.wait()
    for c in range(4):
        mid[4 + c] = dot_t(tiles[c], sketch_ref[...])
    load_p.wait()
    for c in range(8):
        sample[c] = dot(p_rows[c].astype(F32), mid[c], HIGHEST)
    load_tiles = pltpu.make_async_copy(p_ref.at[pl.ds(0, 4)], tiles, local.at[3])
    load_tiles.start()

    for i in range(8):
        arrived(vbuf.at[:, pl.ds(i * 128, 128)], v_recv.at[i])

    def gram_pair(pair, half):
        right = vbuf[:, pl.ds(pl.multiple_of(half * 512, 512), 512)]
        return dot_t(vbuf[:, pl.ds(pair * 256, 256)], right)

    g_copies = []
    for pair in range(4):
        value = gram_pair(pair, 1 - core)
        for p in range(2):
            part[pair * 2 + p, 0, :, :512] = value[p * 128 : p * 128 + 128]
        two = pl.ds(pair * 2, 2)
        copy = remote(
            part.at[two, 0, :, LOW], gsib.at[two], g_send.at[pair], g_recv.at[pair], row, sib
        )
        copy.start()
        g_copies.append(copy)
    for pair in range(4):
        value = gram_pair(pair, core)
        for p in range(2):
            for j in range(4):
                gown[pair * 2 + p, j] = value[p * 128 : p * 128 + 128, j * 128 : j * 128 + 128]
    for j in range(4):
        arrived(sbuf.at[j], s_recv.at[j])
    c_copies = []
    for i in range(8):
        if i % 2 == 0:
            g_copies[i // 2].wait_recv()
        for j in range(4):
            total = gown[i, j] + gsib[i, :, j * 128 : j * 128 + 128]
            gown[i, j] = total
            cown[i * 128 : i * 128 + 128, j * 128 : j * 128 + 128] = dot(
                total, sbuf[j], HIGHEST
            ).astype(BF16)
        copy = Send(
            cown.at[pl.ds(i * 128, 128), :],
            coupled.at[
                pl.ds(pl.multiple_of(slot * 128, 128), 128),
                pl.ds(pl.multiple_of(core * 512, 512), 512),
            ],
            c_send.at[i], c_recv.at[slot * 2 + core], i, base + owner_core,
            jnp.logical_and(row == i, core == owner_core),
        )
        copy.start()
        c_copies.append(copy)
    for kk in range(4):
        for hh in range(2):
            arrived(
                coupled.at[pl.ds(kk * 128, 128), pl.ds(hh * 512, 512)], c_recv.at[kk * 2 + hh]
            )
    for copy in g_copies:
        copy.wait_send()

    u_copies = []

    def pass_panel(index, piece, dx, dz):
        ref = panel.at[index] if piece is None else panel.at[index, pl.ds(piece * 2, 2)]
        n = len(u_copies)
        copy = remote(ref, ref, u_send.at[n], u_recv.at[n], at.row_at(dx, dz), me)
        copy.start()
        u_copies.append(copy)

    def panel_here(n, index, piece=None):
        ref = panel.at[index] if piece is None else panel.at[index, pl.ds(piece * 2, 2)]
        arrived(ref, u_recv.at[n])

    start_panel.wait()
    give = u_own.at[:, :, 1 - half_z]
    copy = remote(give, panel.at[row], u_send.at[0], u_recv.at[0], partner, me)
    copy.start()
    u_copies.append(copy)
    pass_panel(row, None, 1, 0)
    pass_panel(row, None, 3, 0)

    for i in range(8):
        copy = Send(
            gown.at[i], coupling.at[slot, pl.ds(core * 4, 4)],
            k_send.at[i], k_recv.at[slot * 2 + core], i, base + owner_core,
            jnp.logical_and(row == i, core == owner_core),
        )
        copy.start()
        c_copies.append(copy)

    def d_block(n):
        chip = at.chip_at(*ORDER[n])
        left = jnp.concatenate([u_own[kk, chip].reshape(256, 128) for kk in range(4)], axis=1)
        value = dot(left, coupled[...])
        part[position(n), 0] = value[:128]
        part[position(n), 1] = value[128:]

    def second_leg():
        panel_here(0, partner)
        pass_panel(partner, None, 1, 0)
        pass_panel(partner, None, 3, 0)
        for n, dx in ((1, 3), (2, 1)):
            panel_here(n, at.row_at(dx, 0))
            pass_panel(at.row_at(dx, 0), n - 1, 4 - dx, 0)

    def third_leg():
        for n, dx in ((3, 3), (4, 1)):
            panel_here(n, at.row_at(dx, 1))
            pass_panel(at.row_at(dx, 1), n - 3, 4 - dx, 0)

    reduction = Reduction(
        at, part, sibbuf, None, d_hops, d_last, (di_send, di_recv, d_send, d_recv)
    )
    total = reduction.run(d_block)
    for j in range(8):
        dsum[j] = total[:, j * 128 : j * 128 + 128]

    gram_copies = []
    for c in range(8):
        value = sample[c] - dsum[cols_ref[c]]
        sample[c] = value
        gpart[c] = dot_t(value, value, HIGHEST)
        to = c * 2 + c % 2
        copy = Send(
            gpart.at[c], grbuf.at[me], gr_send.at[c], gr_recv.at[me], row, to, me == to
        )
        copy.start()
        gram_copies.append(copy)
    second_leg()
    factors = core == lax.rem(at.chip, 2)
    l_copies = []
    for n, step in enumerate(ORDER[:7]):
        for h in range(2):
            l_copies.append(
                remote(
                    inv, lbuf.at[at.chip], l_send.at[n * 2 + h], l_recv.at[at.chip],
                    row, at.chip_at(*step) * 2 + h,
                )
            )
    l_copies.append(remote(inv, lbuf.at[at.chip], l_send.at[14], l_recv.at[at.chip], row, sib))

    @pl.when(factors)
    def _():
        gram = jnp.zeros((128, 128), F32)
        for m in range(16):
            arrived(grbuf.at[m], gr_recv.at[m])
            gram = gram + grbuf[m]
        inverse_factor(gram, work, inv)
        for copy in l_copies:
            copy.start()
        lbuf[at.chip] = inv[...]

    @pl.when(jnp.logical_not(factors))
    def _():
        arrived(lbuf.at[at.chip], l_recv.at[at.chip])

    for step in ORDER[:7]:
        source = at.chip_at(*step)
        arrived(lbuf.at[source], l_recv.at[source])
    for c in range(8):
        value = dot_nt(sample[c], lbuf[c], HIGHEST)
        left_ref[c] = value * scale
        bown[:, c * 128 : c * 128 + 128] = value.astype(BF16)

    b_copies, f_copies = [], []

    def block(m, half=None):
        rows = pl.ds(pl.multiple_of(m * 128, 128), 128)
        return basis.at[rows, :] if half is None else basis.at[rows, half]

    def pass_basis(source, dest, recv, dz, dy):
        copy = remote(source, dest, b_send.at[len(b_copies)], recv, row, at.inner_at(dz, dy))
        copy.start()
        b_copies.append(copy)

    def to_sib(source, dest, n):
        copy = remote(source, dest, f_send.at[n], f_recv.at[n], row, sib)
        copy.start()
        f_copies.append(copy)

    pass_basis(bown, block(me), b_recv.at[0], 1, 0)
    pass_basis(bown, block(me), b_recv.at[1], 0, 1)
    pass_basis(bown, block(me), b_recv.at[2], 0, 3)
    to_sib(bown, block(me), 0)
    basis[my_rows, :] = bown[...]
    other = at.inner_at(1, 0)
    arrived(block(other), b_recv.at[0])
    pass_basis(block(other), block(other), b_recv.at[3], 0, 1)
    pass_basis(block(other), block(other), b_recv.at[4], 0, 3)
    to_sib(block(other), block(other), 1)
    for s in range(2):
        for way, dy in ((0, 3), (1, 1)):
            m = at.inner_at(s, dy)
            half = HIGH if way else LOW
            n = 1 + s * 2 + way
            arrived(block(m), b_recv.at[n])
            pass_basis(block(m, half), block(m, half), bh_recv.at[s * 2 + way], 0, 3 if way else 1)
            to_sib(block(m), block(m), 1 + n)
    reduction.wait_sends()

    def basis_term(n, dz, dy, first=False):
        chip = at.chip_at(dz, dy)
        if n < 6:
            m = chip * 2 + 1 - core
            arrived(block(m), f_recv.at[n])
        rows = pl.ds(pl.multiple_of(chip * 256, 256), 256)
        for kk in range(4):
            for h in range(2):
                value = dot_t(u_own[kk, chip].reshape(256, 128), basis[rows, h * 512 : h * 512 + 512])
                gsib[kk * 2 + h] = value if first else gsib[kk * 2 + h] + value

    third_leg()
    basis_term(0, 0, 0, True)
    basis_term(1, 1, 0)
    basis_term(2, 0, 3)
    basis_term(3, 0, 1)
    basis_term(4, 1, 3)
    basis_term(5, 1, 1)
    for s in range(2):
        m = at.inner_at(s, 2)
        for way in range(2):
            half = HIGH if way else LOW
            arrived(block(m, half), bh_recv.at[s * 2 + way])
            to_sib(block(m, half), block(m, half), 6 + s * 2 + way)
    for s in range(2):
        m = at.chip_at(s, 2) * 2 + 1 - core
        for way in range(2):
            arrived(block(m, HIGH if way else LOW), f_recv.at[6 + s * 2 + way])
        basis_term(6 + s, s, 2)

    for kk in range(4):
        for hh in range(2):
            arrived(coupling.at[kk, pl.ds(hh * 4, 4)], k_recv.at[kk * 2 + hh])
    i_copies = []
    for kk in range(4):
        for c in range(8):
            lanes = pl.ds((c % 4) * 128, 128)
            ib[half_z, kk * 128 : kk * 128 + 128, c * 128 : c * 128 + 128] = dot_t(
                coupling[kk, cols_ref[c]], gsib[kk * 2 + c // 4, :, lanes], HIGHEST
            ).astype(BF16)
        ref = ib.at[half_z, pl.ds(kk * 128, 128), :]
        copy = remote(ref, ref, i_send.at[kk], i_recv.at[kk], partner, me)
        copy.start()
        i_copies.append(copy)
    panel_here(5, at.row_at(2, 0), 0)
    panel_here(6, at.row_at(2, 0), 1)
    panel_here(7, at.row_at(2, 1), 0)
    panel_here(8, at.row_at(2, 1), 1)

    def terms(s, which, cols):
        chips = pl.ds(pl.multiple_of(lax.rem(at.z + s, 2) * 4, 4), 4)
        for c in range(8):
            lanes = pl.ds(c * 128, 128)
            col = cols[c]
            left = jnp.concatenate(
                [panel[col, kk, chips].reshape(512, 128) for kk in range(4)], axis=1
            )
            value = dot(left, ib[which, :, lanes])
            for y in range(4):
                part[s * 4 + lax.rem(y + 4 - at.y, 4), which, :, lanes] = value[
                    y * 128 : y * 128 + 128
                ]

    mine = core == half_z
    others = core != half_z

    def projection():
        return Reduction(
            at, part, sibbuf, vbuf, r_hops, r_last, (ri_send, ri_recv, r_send, r_recv)
        )

    offers = [projection().to_sibling(n) for n in range(8)]
    for s in range(2):
        terms(1 - s, half_z, cols_ref)

        @pl.when(others)
        def _():
            for n in range(4):
                offers[s * 4 + n].start()

    @pl.when(mine)
    def _():
        sums = projection()
        for n in range(4):
            sums.act(n)
        sums.rest()
        for copy in sums.copies:
            copy.wait_send()

    def p_basis():
        for t in range(2):
            if t == 1:
                again = pltpu.make_async_copy(p_ref.at[pl.ds(4, 4)], tiles, local.at[3])
                again.start()
                again.wait()
            for c in range(4):
                n = t * 4 + c
                mid[n] = dot_t(tiles[c], basis[:, n * 128 : n * 128 + 128])
        for c in range(8):
            sample[c] = dot(q_rows[c].astype(F32), mid[c], HIGHEST)

    load_tiles.wait()
    load_q.wait()
    p_basis()
    arrived(their_cols, cols_sem.at[1])
    for kk in range(4):
        arrived(ib.at[1 - half_z, pl.ds(kk * 128, 128), :], i_recv.at[kk])
    for s in range(2):
        terms(1 - s, 1 - half_z, their_cols)

        @pl.when(mine)
        def _():
            for n in range(4):
                offers[s * 4 + n].start()

    def write_right(source):
        for c in range(8):
            right_ref[c] = (sample[c] - source[:, c * 128 : c * 128 + 128]) * (1.0 / scale)

    @pl.when(mine)
    def _():
        write_right(projection().own(7))

    @pl.when(others)
    def _():
        sums = projection()
        for n in range(4):
            sums.act(n)
        swap = remote(sums.rest(), swapped, t_send, t_recv, partner, sib)
        swap.start()
        for copy in sums.copies:
            copy.wait_send()
        swap.wait_recv()
        write_right(swapped)
        swap.wait_send()

    for copy in offers:
        copy.wait_send()
    cols_copy.wait_send()

    @pl.when(factors)
    def _():
        for copy in l_copies:
            copy.wait_send()

    for copy in v_copies + s_copies + c_copies + u_copies + gram_copies:
        copy.wait_send()
    for copy in b_copies + f_copies + i_copies:
        copy.wait_send()


def update(u, v, p, q, sketch, cols, scale):
    dma = pltpu.SemaphoreType.DMA
    vmem = pl.BlockSpec(memory_space=pltpu.VMEM)
    smem = pl.BlockSpec(memory_space=pltpu.SMEM)
    hbm = pl.BlockSpec(memory_space=pl.ANY)

    def kernel(*refs):
        update_kernel(scale, *refs)

    squares = jax.ShapeDtypeStruct((8, 128, 128), F32)
    return pl.pallas_call(
        kernel,
        out_shape=(squares, squares),
        in_specs=[smem, hbm, hbm, hbm, hbm, vmem],
        out_specs=(vmem, vmem),
        scratch_shapes=[
            pltpu.VMEM((8, 4, 8, 128, 128), BF16),
            pltpu.VMEM((1024, 1024), BF16),
            pltpu.VMEM((4, 128, 128), F32),
            pltpu.VMEM((4, 128, 128), F32),
            pltpu.VMEM((8, 4, 128, 128), F32),
            pltpu.VMEM((8, 128, 512), F32),
            pltpu.VMEM((1024, 512), BF16),
            pltpu.VMEM((512, 1024), BF16),
            pltpu.VMEM((4, 8, 128, 128), F32),
            pltpu.VMEM((4, 2048, 128), BF16),
            pltpu.VMEM((8, 128, 128), F32),
            pltpu.VMEM((8, 128, 128), BF16),
            pltpu.VMEM((8, 128, 128), BF16),
            pltpu.VMEM((8, 2, 128, 1024), F32),
            pltpu.VMEM((8, 128, 1024), F32),
            pltpu.VMEM((12, 128, 512), F32),
            pltpu.VMEM((128, 1024), F32),
            pltpu.VMEM((12, 128, 512), BF16),
            pltpu.VMEM((128, 1024), F32),
            pltpu.VMEM((8, 128, 128), F32),
            pltpu.VMEM((8, 128, 128), F32),
            pltpu.VMEM((8, 128, 128), F32),
            pltpu.VMEM((16, 128, 128), F32),
            pltpu.VMEM((128, 128), F32),
            pltpu.VMEM((128, 128), F32),
            pltpu.VMEM((8, 128, 128), F32),
            pltpu.VMEM((128, 1024), BF16),
            pltpu.VMEM((2048, 1024), BF16),
            pltpu.VMEM((2, 512, 1024), BF16),
            dma((5,)), dma((8,)), dma((8,)), dma((4,)), dma((4,)), dma((4,)), dma((4,)),
            dma((8,)), dma((8,)), dma((8,)), dma((8,)),
            dma((9,)), dma((9,)), dma((8,)), dma((8,)), dma((13,)), dma((13,)),
            dma((8,)), dma((16,)), dma((15,)), dma((8,)),
            dma((9,)), dma((5,)), dma((4,)), dma((10,)), dma((10,)),
            dma((8,)), dma((8,)), dma((13,)), dma((13,)),
            pltpu.VMEM((4, 8, 2, 128, 128), BF16),
            pltpu.SMEM((8,), jnp.int32),
            pltpu.VMEM((128, 1024), F32),
            dma((2,)), dma((4,)), dma((4,)), dma, dma,
        ],
        compiler_params=pltpu.CompilerParams(
            collective_id=1, has_side_effects=True, vmem_limit_bytes=VMEM_LIMIT
        ),
        cost_estimate=pl.CostEstimate(
            flops=13_000_000_000, bytes_accessed=30_000_000, transcendentals=0
        ),
    )(cols, u, v, p, q, sketch)


def body(left_u, left_v, tile_p, tile_q, sketch, tile_cols):
    factor_scale = math.sqrt(sketch.shape[0])
    new_left, new_right = update(
        left_u[0].reshape(4, 8, 2, 128, 128), left_v[0], tile_p[0], tile_q[0], sketch, tile_cols[0], factor_scale
    )
    return new_left[None], new_right[None]


def solution(mesh):
    return jax.shard_map(
        body,
        mesh=mesh,
        in_specs=(
            P("rows", "inner", None, None),
            P("rows", "inner", None, None),
            P("rows", None, None, None),
            P("rows", None, None, None),
            P(),
            P("rows", None),
        ),
        out_specs=(P("rows", None, "inner", None), P("rows", None, "inner", None)),
        check_vma=False,
    )
```

```python
import math

import jax
import jax.numpy as jnp
from jax import lax
from jax.experimental import pallas as pl
from jax.experimental.pallas import tpu as pltpu
from jax.sharding import PartitionSpec as P

MESH = pl.DeviceIdType.MESH
HIGHEST = lax.Precision.HIGHEST
F32 = jnp.float32
BF16 = jnp.bfloat16
VMEM_LIMIT = 61 * 1024 * 1024


def device(row, place):
    return {"rows": row, "inner": place}


def greet(partners, count):
    barrier = pltpu.get_barrier_semaphore()
    for row, place in partners:
        pl.semaphore_signal(barrier, inc=1, device_id=device(row, place), device_id_type=MESH)
    pl.semaphore_wait(barrier, count)


def remote(src, dst, send_sem, recv_sem, row, place):
    return pltpu.make_async_remote_copy(
        src_ref=src, dst_ref=dst, send_sem=send_sem, recv_sem=recv_sem,
        device_id=device(row, place), device_id_type=MESH,
    )


class Send:
    def __init__(self, src, dst, send_sem, recv_sem, row, place, is_self):
        self.far = remote(src, dst, send_sem, recv_sem, row, place)
        self.near = pltpu.make_async_copy(src, dst, recv_sem)
        self.is_self = is_self

    def start(self):
        @pl.when(jnp.logical_not(self.is_self))
        def _():
            self.far.start()

        @pl.when(self.is_self)
        def _():
            self.near.start()

    def wait_send(self):
        @pl.when(jnp.logical_not(self.is_self))
        def _():
            self.far.wait_send()


def arrived(ref, sem):
    pltpu.make_async_copy(ref, ref, sem).wait()


def dot(a, b, precision=None):
    return jnp.dot(a, b, preferred_element_type=F32, precision=precision)


def dot_t(a, b, precision=None):
    return lax.dot_general(
        a, b, (((0,), (0,)), ((), ())), preferred_element_type=F32, precision=precision
    )


def dot_nt(a, b, precision=None):
    return lax.dot_general(
        a, b, (((1,), (1,)), ((), ())), preferred_element_type=F32, precision=precision
    )

LOW, HIGH = pl.ds(0, 512), pl.ds(512, 512)
ORDER = [(1, 2), (1, 1), (1, 3), (1, 0), (0, 2), (0, 1), (0, 3), (0, 0)]


def position(n):
    return ORDER[n][0] * 4 + ORDER[n][1]


class Place:
    def __init__(self):
        self.row, self.me = lax.axis_index("rows"), lax.axis_index("inner")
        self.core = lax.rem(self.me, 2)
        self.chip = self.me // 2
        self.z, self.y = self.chip // 4, lax.rem(self.chip, 4)
        self.base = self.me - self.core
        self.sib = self.base + 1 - self.core

    def chip_at(self, dz, dy):
        return lax.rem(self.z + dz, 2) * 4 + lax.rem(self.y + dy, 4)

    def inner_at(self, dz, dy):
        return self.chip_at(dz, dy) * 2 + self.core

    def row_at(self, dx, dz):
        x, z = self.row // 2, lax.rem(self.row, 2)
        return lax.rem(x + dx, 4) * 2 + lax.rem(z + dz, 2)


def inverse_factor(gram, work, inv):
    order = gram.shape[0]
    strip, group = 16, 4
    row_id = lax.broadcasted_iota(jnp.int32, (order, order), 0)
    col_id = lax.broadcasted_iota(jnp.int32, (order, order), 1)
    diagonal = row_id == col_id
    ridge = 1e-06 * jnp.sum(jnp.where(diagonal, gram, 0.0)) / order
    work[...] = gram + jnp.where(diagonal, ridge, 0.0)
    inv[...] = jnp.where(diagonal, 1.0, 0.0)
    within = lax.broadcasted_iota(jnp.int32, (strip, order), 0)
    full = (strip, order)
    for lo in range(0, order, strip):
        a, m = work[lo : lo + strip, :], inv[lo : lo + strip, :]
        for first in range(0, strip, group):
            cols, rows, m_rows = [], [], []
            for k in range(group):
                at_col, at_row = lo + first + k, first + k
                cols.append(jnp.broadcast_to(a[:, at_col : at_col + 1], full))
                rows.append(jnp.broadcast_to(a[at_row : at_row + 1, :], full))
                m_rows.append(jnp.broadcast_to(m[at_row : at_row + 1, :], full))
            small = {}
            for k in range(group):
                for i in range(k, group):
                    at_row = first + i
                    value = jnp.broadcast_to(cols[k][at_row : at_row + 1, :], full)
                    for p in range(k):
                        value = value - small[i, p] * small[k, p]
                    small[i, k] = lax.rsqrt(value) if i == k else value * small[k, k]
            for k in range(group):
                for p in range(k):
                    cols[k] = cols[k] - small[k, p] * cols[p]
                    rows[k] = rows[k] - small[k, p] * rows[p]
                    m_rows[k] = m_rows[k] - small[k, p] * m_rows[p]
                cols[k] = cols[k] * small[k, k]
                rows[k] = rows[k] * small[k, k]
                m_rows[k] = m_rows[k] * small[k, k]
            below = within >= first + group
            for k in range(group):
                factor = jnp.where(below, cols[k], 0.0)
                a, m = a - factor * rows[k], m - factor * m_rows[k]
            for k in range(group):
                here = within == first + k
                a, m = jnp.where(here, rows[k], a), jnp.where(here, m_rows[k], m)
        inv[lo : lo + strip, :] = m
        rest = lo + strip
        if rest < order:
            update = dot_t(a, jnp.concatenate([a, m], axis=1), HIGHEST)
            work[rest:, :] = work[rest:, :] - update[rest:, :order]
            inv[rest:, :] = inv[rest:, :] - update[rest:, order:]


class Reduction:
    def __init__(self, at, part, sibbuf, wire, hops, last, sems):
        self.at, self.part, self.sibbuf = at, part, sibbuf
        self.wire, self.hops, self.last = wire, hops, last
        self.i_send, self.i_recv, self.send, self.recv = sems
        self.copies, self.inner = [], []

    def own(self, n):
        return self.part.at[position(n), self.at.core]

    def to_sibling(self, n):
        at = self.at
        return remote(
            self.part.at[position(n), 1 - at.core], self.sibbuf.at[n],
            self.i_send.at[n], self.i_recv.at[n], at.row, at.sib,
        )

    def offer(self, n):
        copy = self.to_sibling(n)
        copy.start()
        self.inner.append(copy)

    def merge(self, n):
        arrived(self.sibbuf.at[n], self.i_recv.at[n])
        own = self.own(n)
        own[...] = own[...] + self.sibbuf[n]

    def hop(self, n, half, s, kind, way):
        at = self.at
        if self.wire is None:
            source = self.part.at[position(n), at.core, :, half]
        else:
            source = self.wire.at[pl.ds(n * 128, 128), half]
            source[...] = self.own(n)[:, half].astype(source.dtype)
        slot = (s * 3 + kind) * 2 + way
        to = at.inner_at(0, 1 if way == 0 else 3)
        copy = remote(source, self.hops.at[slot], self.send.at[slot], self.recv.at[slot], at.row, to)
        copy.start()
        self.copies.append(copy)

    def took(self, s, kind, way):
        slot = (s * 3 + kind) * 2 + way
        arrived(self.hops.at[slot], self.recv.at[slot])
        return self.hops[slot].astype(F32)

    def act(self, n):
        s, dy = ORDER[n]
        self.merge(n)
        if dy == 2:
            self.hop(n, LOW, s, 0, 0)
            self.hop(n, HIGH, s, 0, 1)
        elif dy == 1:
            self.hop(n, HIGH, s, 1, 0)
        elif dy == 3:
            self.hop(n, LOW, s, 1, 1)

    def relay(self, s):
        first = 4 * (1 - s)
        for n, half, way in ((first + 1, LOW, 0), (first + 2, HIGH, 1)):
            own = self.own(n)
            own[:, half] = own[:, half] + self.took(s, 0, way)
            self.hop(n, half, s, 2, way)

    def finish(self, s):
        own = self.own(4 * (1 - s) + 3)
        for half, kinds in ((LOW, (2, 1)), (HIGH, (1, 2))):
            own[:, half] = own[:, half] + self.took(s, kinds[0], 0) + self.took(s, kinds[1], 1)
        if s == 1:
            at = self.at
            copy = remote(
                own, self.last, self.send.at[12], self.recv.at[12], at.row, at.inner_at(1, 0)
            )
            copy.start()
            self.copies.append(copy)

    def total(self):
        arrived(self.last, self.recv.at[12])
        own = self.own(7)
        own[...] = own[...] + self.last[...]
        return own

    def run(self, compute):
        for n in range(8):
            compute(n)
            self.offer(n)
            if 1 <= n <= 4:
                self.act(n - 1)
        return self.rest()

    def rest(self):
        self.relay(1)
        for n in range(4, 8):
            self.act(n)
        self.finish(1)
        self.relay(0)
        self.finish(0)
        return self.total()

    def wait_sends(self):
        for copy in self.inner + self.copies:
            copy.wait_send()


def update_kernel(
    scale, cols_ref, u_ref, v_ref, p_ref, q_ref, sketch_ref, left_ref, right_ref,
    panel, vbuf, sown, sbuf, gown, gsib, cown, coupled, coupling,
    tiles, mid, p_rows, q_rows, part, sibbuf, d_hops, d_last, r_hops, r_last,
    sample, dsum, gpart, grbuf, work, inv, lbuf, bown, basis, ib,
    local, v_send, v_recv, s_send, s_recv, g_send, g_recv, c_send, c_recv, k_send, k_recv,
    u_send, u_recv, di_send, di_recv, d_send, d_recv, gr_send, gr_recv, l_send, l_recv,
    b_send, b_recv, bh_recv, f_send, f_recv, ri_send, ri_recv, r_send, r_recv,
    u_own, their_cols, swapped, cols_sem, i_send, i_recv, t_send, t_recv,
):
    at = Place()
    row, me, core, base, sib = at.row, at.me, at.core, at.base, at.sib
    owner_core = row // 4
    slot = lax.rem(row, 4)
    my_rows = pl.ds(pl.multiple_of(me * 128, 128), 128)

    half_z = lax.rem(row, 2)
    partner = at.row_at(0, 1)
    own_u = pltpu.make_async_copy(u_ref, u_own, local.at[0])
    own_u.start()
    start_panel = pltpu.make_async_copy(u_ref.at[:, :, half_z], panel.at[row], local.at[4])
    start_panel.start()
    load_p = pltpu.make_async_copy(p_ref.at[:, my_rows, :], p_rows, local.at[1])
    load_p.start()
    load_q = pltpu.make_async_copy(q_ref.at[:, my_rows, :], q_rows, local.at[2])
    load_q.start()
    load_tiles = pltpu.make_async_copy(q_ref.at[pl.ds(0, 4)], tiles, local.at[3])
    load_tiles.start()

    partners = [(lax.rem(row + d, 8), base + h) for d in range(1, 8) for h in range(2)]
    partners += [(row, lax.rem(me + d, 16)) for d in range(1, 16)]
    greet(partners, len(partners))
    cols_copy = remote(cols_ref, their_cols, cols_sem.at[0], cols_sem.at[1], partner, me)
    cols_copy.start()

    v_copies = []
    for n in range(8):
        kk, hh = lax.rem(slot + n % 4, 4), lax.rem(n // 4 + core, 2)
        to = core * 4 + kk
        copy = Send(
            v_ref.at[kk, pl.ds(pl.multiple_of(hh * 1024, 1024), 1024), :],
            vbuf.at[:, pl.ds(pl.multiple_of(row * 128, 128), 128)],
            v_send.at[n], v_recv.at[row], to, base + hh,
            jnp.logical_and(to == row, core == hh),
        )
        copy.start()
        v_copies.append(copy)

    s_copies = []
    own_u.wait()
    for kk in range(4):
        sown[kk] = dot_t(u_own[kk].reshape(2048, 128), sketch_ref[...])
        to = core * 4 + kk
        copy = Send(
            sown.at[kk], sbuf.at[slot], s_send.at[kk], s_recv.at[slot],
            to, base + owner_core, jnp.logical_and(to == row, core == owner_core),
        )
        copy.start()
        s_copies.append(copy)

    load_tiles.wait()
    for c in range(4):
        mid[c] = dot_t(tiles[c], sketch_ref[...])
    load_tiles = pltpu.make_async_copy(q_ref.at[pl.ds(4, 4)], tiles, local.at[3])
    load_tiles.start()
    load_tiles.wait()
    for c in range(4):
        mid[4 + c] = dot_t(tiles[c], sketch_ref[...])
    load_p.wait()
    for c in range(8):
        sample[c] = dot(p_rows[c].astype(F32), mid[c], HIGHEST)
    load_tiles = pltpu.make_async_copy(p_ref.at[pl.ds(0, 4)], tiles, local.at[3])
    load_tiles.start()

    for i in range(8):
        arrived(vbuf.at[:, pl.ds(i * 128, 128)], v_recv.at[i])

    def gram_pair(pair, half):
        right = vbuf[:, pl.ds(pl.multiple_of(half * 512, 512), 512)]
        return dot_t(vbuf[:, pl.ds(pair * 256, 256)], right)

    g_copies = []
    for pair in range(4):
        value = gram_pair(pair, 1 - core)
        for p in range(2):
            part[pair * 2 + p, 0, :, :512] = value[p * 128 : p * 128 + 128]
        two = pl.ds(pair * 2, 2)
        copy = remote(
            part.at[two, 0, :, LOW], gsib.at[two], g_send.at[pair], g_recv.at[pair], row, sib
        )
        copy.start()
        g_copies.append(copy)
    for pair in range(4):
        value = gram_pair(pair, core)
        for p in range(2):
            for j in range(4):
                gown[pair * 2 + p, j] = value[p * 128 : p * 128 + 128, j * 128 : j * 128 + 128]
    for j in range(4):
        arrived(sbuf.at[j], s_recv.at[j])
    c_copies = []
    for i in range(8):
        if i % 2 == 0:
            g_copies[i // 2].wait_recv()
        for j in range(4):
            total = gown[i, j] + gsib[i, :, j * 128 : j * 128 + 128]
            gown[i, j] = total
            cown[i * 128 : i * 128 + 128, j * 128 : j * 128 + 128] = dot(
                total, sbuf[j], HIGHEST
            ).astype(BF16)
        copy = Send(
            cown.at[pl.ds(i * 128, 128), :],
            coupled.at[
                pl.ds(pl.multiple_of(slot * 128, 128), 128),
                pl.ds(pl.multiple_of(core * 512, 512), 512),
            ],
            c_send.at[i], c_recv.at[slot * 2 + core], i, base + owner_core,
            jnp.logical_and(row == i, core == owner_core),
        )
        copy.start()
        c_copies.append(copy)
    for kk in range(4):
        for hh in range(2):
            arrived(
                coupled.at[pl.ds(kk * 128, 128), pl.ds(hh * 512, 512)], c_recv.at[kk * 2 + hh]
            )
    for copy in g_copies:
        copy.wait_send()

    u_copies = []

    def pass_panel(index, piece, dx, dz):
        ref = panel.at[index] if piece is None else panel.at[index, pl.ds(piece * 2, 2)]
        n = len(u_copies)
        copy = remote(ref, ref, u_send.at[n], u_recv.at[n], at.row_at(dx, dz), me)
        copy.start()
        u_copies.append(copy)

    def panel_here(n, index, piece=None):
        ref = panel.at[index] if piece is None else panel.at[index, pl.ds(piece * 2, 2)]
        arrived(ref, u_recv.at[n])

    start_panel.wait()
    give = u_own.at[:, :, 1 - half_z]
    copy = remote(give, panel.at[row], u_send.at[0], u_recv.at[0], partner, me)
    copy.start()
    u_copies.append(copy)
    pass_panel(row, None, 1, 0)
    pass_panel(row, None, 3, 0)

    def d_block(n):
        chip = at.chip_at(*ORDER[n])
        left = jnp.concatenate([u_own[kk, chip].reshape(256, 128) for kk in range(4)], axis=1)
        value = dot(left, coupled[...])
        part[position(n), 0] = value[:128]
        part[position(n), 1] = value[128:]

    def second_leg():
        panel_here(0, partner)
        pass_panel(partner, None, 1, 0)
        pass_panel(partner, None, 3, 0)
        for n, dx in ((1, 3), (2, 1)):
            panel_here(n, at.row_at(dx, 0))
            pass_panel(at.row_at(dx, 0), n - 1, 4 - dx, 0)

    def third_leg():
        for n, dx in ((3, 3), (4, 1)):
            panel_here(n, at.row_at(dx, 1))
            pass_panel(at.row_at(dx, 1), n - 3, 4 - dx, 0)

    reduction = Reduction(
        at, part, sibbuf, None, d_hops, d_last, (di_send, di_recv, d_send, d_recv)
    )
    total = reduction.run(d_block)
    for j in range(8):
        dsum[j] = total[:, j * 128 : j * 128 + 128]

    gram_copies = []
    for c in range(8):
        value = sample[c] - dsum[cols_ref[c]]
        sample[c] = value
        gpart[c] = dot_t(value, value, HIGHEST)
        to = c * 2 + c % 2
        copy = Send(
            gpart.at[c], grbuf.at[me], gr_send.at[c], gr_recv.at[me], row, to, me == to
        )
        copy.start()
        gram_copies.append(copy)
    second_leg()
    for i in range(8):
        copy = Send(
            gown.at[i], coupling.at[slot, pl.ds(core * 4, 4)],
            k_send.at[i], k_recv.at[slot * 2 + core], i, base + owner_core,
            jnp.logical_and(row == i, core == owner_core),
        )
        copy.start()
        c_copies.append(copy)

    factors = core == lax.rem(at.chip, 2)
    l_copies = []
    for n, step in enumerate(ORDER[:7]):
        for h in range(2):
            l_copies.append(
                remote(
                    inv, lbuf.at[at.chip], l_send.at[n * 2 + h], l_recv.at[at.chip],
                    row, at.chip_at(*step) * 2 + h,
                )
            )
    l_copies.append(remote(inv, lbuf.at[at.chip], l_send.at[14], l_recv.at[at.chip], row, sib))

    @pl.when(factors)
    def _():
        gram = jnp.zeros((128, 128), F32)
        for m in range(16):
            arrived(grbuf.at[m], gr_recv.at[m])
            gram = gram + grbuf[m]
        inverse_factor(gram, work, inv)
        for copy in l_copies:
            copy.start()
        lbuf[at.chip] = inv[...]

    @pl.when(jnp.logical_not(factors))
    def _():
        arrived(lbuf.at[at.chip], l_recv.at[at.chip])

    for step in ORDER[:7]:
        source = at.chip_at(*step)
        arrived(lbuf.at[source], l_recv.at[source])
    for c in range(8):
        value = dot_nt(sample[c], lbuf[c], HIGHEST)
        left_ref[c] = value * scale
        bown[:, c * 128 : c * 128 + 128] = value.astype(BF16)

    b_copies, f_copies = [], []

    def block(m, half=None):
        rows = pl.ds(pl.multiple_of(m * 128, 128), 128)
        return basis.at[rows, :] if half is None else basis.at[rows, half]

    def pass_basis(source, dest, recv, dz, dy):
        copy = remote(source, dest, b_send.at[len(b_copies)], recv, row, at.inner_at(dz, dy))
        copy.start()
        b_copies.append(copy)

    def to_sib(source, dest, n):
        copy = remote(source, dest, f_send.at[n], f_recv.at[n], row, sib)
        copy.start()
        f_copies.append(copy)

    pass_basis(bown, block(me), b_recv.at[0], 1, 0)
    pass_basis(bown, block(me), b_recv.at[1], 0, 1)
    pass_basis(bown, block(me), b_recv.at[2], 0, 3)
    to_sib(bown, block(me), 0)
    basis[my_rows, :] = bown[...]
    other = at.inner_at(1, 0)
    arrived(block(other), b_recv.at[0])
    pass_basis(block(other), block(other), b_recv.at[3], 0, 1)
    pass_basis(block(other), block(other), b_recv.at[4], 0, 3)
    to_sib(block(other), block(other), 1)
    for s in range(2):
        for way, dy in ((0, 3), (1, 1)):
            m = at.inner_at(s, dy)
            half = HIGH if way else LOW
            n = 1 + s * 2 + way
            arrived(block(m), b_recv.at[n])
            pass_basis(block(m, half), block(m, half), bh_recv.at[s * 2 + way], 0, 3 if way else 1)
            to_sib(block(m), block(m), 1 + n)
    reduction.wait_sends()

    def basis_term(n, dz, dy, first=False):
        chip = at.chip_at(dz, dy)
        if n < 6:
            m = chip * 2 + 1 - core
            arrived(block(m), f_recv.at[n])
        rows = pl.ds(pl.multiple_of(chip * 256, 256), 256)
        for kk in range(4):
            for h in range(2):
                value = dot_t(u_own[kk, chip].reshape(256, 128), basis[rows, h * 512 : h * 512 + 512])
                gsib[kk * 2 + h] = value if first else gsib[kk * 2 + h] + value

    basis_term(0, 0, 0, True)
    basis_term(1, 1, 0)
    basis_term(2, 0, 3)
    basis_term(3, 0, 1)
    basis_term(4, 1, 3)
    basis_term(5, 1, 1)
    third_leg()
    for s in range(2):
        m = at.inner_at(s, 2)
        for way in range(2):
            half = HIGH if way else LOW
            arrived(block(m, half), bh_recv.at[s * 2 + way])
            to_sib(block(m, half), block(m, half), 6 + s * 2 + way)
    for s in range(2):
        m = at.chip_at(s, 2) * 2 + 1 - core
        for way in range(2):
            arrived(block(m, HIGH if way else LOW), f_recv.at[6 + s * 2 + way])
        basis_term(6 + s, s, 2)

    for kk in range(4):
        for hh in range(2):
            arrived(coupling.at[kk, pl.ds(hh * 4, 4)], k_recv.at[kk * 2 + hh])
    i_copies = []
    for kk in range(4):
        for c in range(8):
            lanes = pl.ds((c % 4) * 128, 128)
            ib[half_z, kk * 128 : kk * 128 + 128, c * 128 : c * 128 + 128] = dot_t(
                coupling[kk, cols_ref[c]], gsib[kk * 2 + c // 4, :, lanes], HIGHEST
            ).astype(BF16)
        ref = ib.at[half_z, pl.ds(kk * 128, 128), :]
        copy = remote(ref, ref, i_send.at[kk], i_recv.at[kk], partner, me)
        copy.start()
        i_copies.append(copy)
    panel_here(5, at.row_at(2, 0), 0)
    panel_here(6, at.row_at(2, 0), 1)
    panel_here(7, at.row_at(2, 1), 0)
    panel_here(8, at.row_at(2, 1), 1)

    def terms(s, which, cols):
        chips = pl.ds(pl.multiple_of(lax.rem(at.z + s, 2) * 4, 4), 4)
        for c in range(8):
            lanes = pl.ds(c * 128, 128)
            col = cols[c]
            left = jnp.concatenate(
                [panel[col, kk, chips].reshape(512, 128) for kk in range(4)], axis=1
            )
            value = dot(left, ib[which, :, lanes])
            for y in range(4):
                part[s * 4 + lax.rem(y + 4 - at.y, 4), which, :, lanes] = value[
                    y * 128 : y * 128 + 128
                ]

    mine = core == half_z
    others = core != half_z

    def projection():
        return Reduction(
            at, part, sibbuf, vbuf, r_hops, r_last, (ri_send, ri_recv, r_send, r_recv)
        )

    offers = [projection().to_sibling(n) for n in range(8)]
    for s in range(2):
        terms(1 - s, half_z, cols_ref)

        @pl.when(others)
        def _():
            for n in range(4):
                offers[s * 4 + n].start()

    @pl.when(mine)
    def _():
        sums = projection()
        for n in range(4):
            sums.act(n)
        sums.rest()
        for copy in sums.copies:
            copy.wait_send()

    def p_basis():
        for t in range(2):
            if t == 1:
                again = pltpu.make_async_copy(p_ref.at[pl.ds(4, 4)], tiles, local.at[3])
                again.start()
                again.wait()
            for c in range(4):
                n = t * 4 + c
                mid[n] = dot_t(tiles[c], basis[:, n * 128 : n * 128 + 128])
        for c in range(8):
            sample[c] = dot(q_rows[c].astype(F32), mid[c], HIGHEST)

    load_tiles.wait()
    load_q.wait()
    p_basis()
    arrived(their_cols, cols_sem.at[1])
    for kk in range(4):
        arrived(ib.at[1 - half_z, pl.ds(kk * 128, 128), :], i_recv.at[kk])
    for s in range(2):
        terms(1 - s, 1 - half_z, their_cols)

        @pl.when(mine)
        def _():
            for n in range(4):
                offers[s * 4 + n].start()

    def write_right(source):
        for c in range(8):
            right_ref[c] = (sample[c] - source[:, c * 128 : c * 128 + 128]) * (1.0 / scale)

    @pl.when(mine)
    def _():
        write_right(projection().own(7))

    @pl.when(others)
    def _():
        sums = projection()
        for n in range(4):
            sums.act(n)
        swap = remote(sums.rest(), swapped, t_send, t_recv, partner, sib)
        swap.start()
        for copy in sums.copies:
            copy.wait_send()
        swap.wait_recv()
        write_right(swapped)
        swap.wait_send()

    for copy in offers:
        copy.wait_send()
    cols_copy.wait_send()

    @pl.when(factors)
    def _():
        for copy in l_copies:
            copy.wait_send()

    for copy in v_copies + s_copies + c_copies + u_copies + gram_copies:
        copy.wait_send()
    for copy in b_copies + f_copies + i_copies:
        copy.wait_send()


def update(u, v, p, q, sketch, cols, scale):
    dma = pltpu.SemaphoreType.DMA
    vmem = pl.BlockSpec(memory_space=pltpu.VMEM)
    smem = pl.BlockSpec(memory_space=pltpu.SMEM)
    hbm = pl.BlockSpec(memory_space=pl.ANY)

    def kernel(*refs):
        update_kernel(scale, *refs)

    squares = jax.ShapeDtypeStruct((8, 128, 128), F32)
    return pl.pallas_call(
        kernel,
        out_shape=(squares, squares),
        in_specs=[smem, hbm, hbm, hbm, hbm, vmem],
        out_specs=(vmem, vmem),
        scratch_shapes=[
            pltpu.VMEM((8, 4, 8, 128, 128), BF16),
            pltpu.VMEM((1024, 1024), BF16),
            pltpu.VMEM((4, 128, 128), F32),
            pltpu.VMEM((4, 128, 128), F32),
            pltpu.VMEM((8, 4, 128, 128), F32),
            pltpu.VMEM((8, 128, 512), F32),
            pltpu.VMEM((1024, 512), BF16),
            pltpu.VMEM((512, 1024), BF16),
            pltpu.VMEM((4, 8, 128, 128), F32),
            pltpu.VMEM((4, 2048, 128), BF16),
            pltpu.VMEM((8, 128, 128), F32),
            pltpu.VMEM((8, 128, 128), BF16),
            pltpu.VMEM((8, 128, 128), BF16),
            pltpu.VMEM((8, 2, 128, 1024), F32),
            pltpu.VMEM((8, 128, 1024), F32),
            pltpu.VMEM((12, 128, 512), F32),
            pltpu.VMEM((128, 1024), F32),
            pltpu.VMEM((12, 128, 512), BF16),
            pltpu.VMEM((128, 1024), F32),
            pltpu.VMEM((8, 128, 128), F32),
            pltpu.VMEM((8, 128, 128), F32),
            pltpu.VMEM((8, 128, 128), F32),
            pltpu.VMEM((16, 128, 128), F32),
            pltpu.VMEM((128, 128), F32),
            pltpu.VMEM((128, 128), F32),
            pltpu.VMEM((8, 128, 128), F32),
            pltpu.VMEM((128, 1024), BF16),
            pltpu.VMEM((2048, 1024), BF16),
            pltpu.VMEM((2, 512, 1024), BF16),
            dma((5,)), dma((8,)), dma((8,)), dma((4,)), dma((4,)), dma((4,)), dma((4,)),
            dma((8,)), dma((8,)), dma((8,)), dma((8,)),
            dma((9,)), dma((9,)), dma((8,)), dma((8,)), dma((13,)), dma((13,)),
            dma((8,)), dma((16,)), dma((15,)), dma((8,)),
            dma((9,)), dma((5,)), dma((4,)), dma((10,)), dma((10,)),
            dma((8,)), dma((8,)), dma((13,)), dma((13,)),
            pltpu.VMEM((4, 8, 2, 128, 128), BF16),
            pltpu.SMEM((8,), jnp.int32),
            pltpu.VMEM((128, 1024), F32),
            dma((2,)), dma((4,)), dma((4,)), dma, dma,
        ],
        compiler_params=pltpu.CompilerParams(
            collective_id=1, has_side_effects=True, vmem_limit_bytes=VMEM_LIMIT
        ),
        cost_estimate=pl.CostEstimate(
            flops=13_000_000_000, bytes_accessed=30_000_000, transcendentals=0
        ),
    )(cols, u, v, p, q, sketch)


def body(left_u, left_v, tile_p, tile_q, sketch, tile_cols):
    factor_scale = math.sqrt(sketch.shape[0])
    new_left, new_right = update(
        left_u[0].reshape(4, 8, 2, 128, 128), left_v[0], tile_p[0], tile_q[0], sketch, tile_cols[0], factor_scale
    )
    return new_left[None], new_right[None]


def solution(mesh):
    return jax.shard_map(
        body,
        mesh=mesh,
        in_specs=(
            P("rows", "inner", None, None),
            P("rows", "inner", None, None),
            P("rows", None, None, None),
            P("rows", None, None, None),
            P(),
            P("rows", None),
        ),
        out_specs=(P("rows", None, "inner", None), P("rows", None, "inner", None)),
        check_vma=False,
    )
```

```python
import math

import jax
import jax.numpy as jnp
from jax import lax
from jax.experimental import pallas as pl
from jax.experimental.pallas import tpu as pltpu
from jax.sharding import PartitionSpec as P

MESH = pl.DeviceIdType.MESH
HIGHEST = lax.Precision.HIGHEST
F32 = jnp.float32
BF16 = jnp.bfloat16
VMEM_LIMIT = 61 * 1024 * 1024


def device(row, place):
    return {"rows": row, "inner": place}


def greet(partners, count):
    barrier = pltpu.get_barrier_semaphore()
    for row, place in partners:
        pl.semaphore_signal(barrier, inc=1, device_id=device(row, place), device_id_type=MESH)
    pl.semaphore_wait(barrier, count)


def remote(src, dst, send_sem, recv_sem, row, place):
    return pltpu.make_async_remote_copy(
        src_ref=src, dst_ref=dst, send_sem=send_sem, recv_sem=recv_sem,
        device_id=device(row, place), device_id_type=MESH,
    )


class Send:
    def __init__(self, src, dst, send_sem, recv_sem, row, place, is_self):
        self.far = remote(src, dst, send_sem, recv_sem, row, place)
        self.near = pltpu.make_async_copy(src, dst, recv_sem)
        self.is_self = is_self

    def start(self):
        @pl.when(jnp.logical_not(self.is_self))
        def _():
            self.far.start()

        @pl.when(self.is_self)
        def _():
            self.near.start()

    def wait_send(self):
        @pl.when(jnp.logical_not(self.is_self))
        def _():
            self.far.wait_send()


def arrived(ref, sem):
    pltpu.make_async_copy(ref, ref, sem).wait()


def dot(a, b, precision=None):
    return jnp.dot(a, b, preferred_element_type=F32, precision=precision)


def dot_t(a, b, precision=None):
    return lax.dot_general(
        a, b, (((0,), (0,)), ((), ())), preferred_element_type=F32, precision=precision
    )


def dot_nt(a, b, precision=None):
    return lax.dot_general(
        a, b, (((1,), (1,)), ((), ())), preferred_element_type=F32, precision=precision
    )

LOW, HIGH = pl.ds(0, 512), pl.ds(512, 512)
ORDER = [(1, 2), (1, 1), (1, 3), (1, 0), (0, 2), (0, 1), (0, 3), (0, 0)]


def position(n):
    return ORDER[n][0] * 4 + ORDER[n][1]


class Place:
    def __init__(self):
        self.row, self.me = lax.axis_index("rows"), lax.axis_index("inner")
        self.core = lax.rem(self.me, 2)
        self.chip = self.me // 2
        self.z, self.y = self.chip // 4, lax.rem(self.chip, 4)
        self.base = self.me - self.core
        self.sib = self.base + 1 - self.core

    def chip_at(self, dz, dy):
        return lax.rem(self.z + dz, 2) * 4 + lax.rem(self.y + dy, 4)

    def inner_at(self, dz, dy):
        return self.chip_at(dz, dy) * 2 + self.core

    def row_at(self, dx, dz):
        x, z = self.row // 2, lax.rem(self.row, 2)
        return lax.rem(x + dx, 4) * 2 + lax.rem(z + dz, 2)


def inverse_factor(gram, work, inv):
    order = gram.shape[0]
    strip, group = 16, 4
    row_id = lax.broadcasted_iota(jnp.int32, (order, order), 0)
    col_id = lax.broadcasted_iota(jnp.int32, (order, order), 1)
    diagonal = row_id == col_id
    ridge = 1e-06 * jnp.sum(jnp.where(diagonal, gram, 0.0)) / order
    work[...] = gram + jnp.where(diagonal, ridge, 0.0)
    inv[...] = jnp.where(diagonal, 1.0, 0.0)
    within = lax.broadcasted_iota(jnp.int32, (strip, order), 0)
    full = (strip, order)
    for lo in range(0, order, strip):
        a, m = work[lo : lo + strip, :], inv[lo : lo + strip, :]
        for first in range(0, strip, group):
            cols, rows, m_rows = [], [], []
            for k in range(group):
                at_col, at_row = lo + first + k, first + k
                cols.append(jnp.broadcast_to(a[:, at_col : at_col + 1], full))
                rows.append(jnp.broadcast_to(a[at_row : at_row + 1, :], full))
                m_rows.append(jnp.broadcast_to(m[at_row : at_row + 1, :], full))
            small = {}
            for k in range(group):
                for i in range(k, group):
                    at_row = first + i
                    value = jnp.broadcast_to(cols[k][at_row : at_row + 1, :], full)
                    for p in range(k):
                        value = value - small[i, p] * small[k, p]
                    small[i, k] = lax.rsqrt(value) if i == k else value * small[k, k]
            for k in range(group):
                for p in range(k):
                    cols[k] = cols[k] - small[k, p] * cols[p]
                    rows[k] = rows[k] - small[k, p] * rows[p]
                    m_rows[k] = m_rows[k] - small[k, p] * m_rows[p]
                cols[k] = cols[k] * small[k, k]
                rows[k] = rows[k] * small[k, k]
                m_rows[k] = m_rows[k] * small[k, k]
            below = within >= first + group
            for k in range(group):
                factor = jnp.where(below, cols[k], 0.0)
                a, m = a - factor * rows[k], m - factor * m_rows[k]
            for k in range(group):
                here = within == first + k
                a, m = jnp.where(here, rows[k], a), jnp.where(here, m_rows[k], m)
        inv[lo : lo + strip, :] = m
        rest = lo + strip
        if rest < order:
            update = dot_t(a, jnp.concatenate([a, m], axis=1), HIGHEST)
            work[rest:, :] = work[rest:, :] - update[rest:, :order]
            inv[rest:, :] = inv[rest:, :] - update[rest:, order:]


class Reduction:
    def __init__(self, at, part, sibbuf, wire, hops, last, sems):
        self.at, self.part, self.sibbuf = at, part, sibbuf
        self.wire, self.hops, self.last = wire, hops, last
        self.i_send, self.i_recv, self.send, self.recv = sems
        self.copies, self.inner = [], []

    def own(self, n):
        return self.part.at[position(n), self.at.core]

    def to_sibling(self, n):
        at = self.at
        return remote(
            self.part.at[position(n), 1 - at.core], self.sibbuf.at[n],
            self.i_send.at[n], self.i_recv.at[n], at.row, at.sib,
        )

    def offer(self, n):
        copy = self.to_sibling(n)
        copy.start()
        self.inner.append(copy)

    def merge(self, n):
        arrived(self.sibbuf.at[n], self.i_recv.at[n])
        own = self.own(n)
        own[...] = own[...] + self.sibbuf[n]

    def hop(self, n, half, s, kind, way):
        at = self.at
        if self.wire is None:
            source = self.part.at[position(n), at.core, :, half]
        else:
            source = self.wire.at[pl.ds(n * 128, 128), half]
            source[...] = self.own(n)[:, half].astype(source.dtype)
        slot = (s * 3 + kind) * 2 + way
        to = at.inner_at(0, 1 if way == 0 else 3)
        copy = remote(source, self.hops.at[slot], self.send.at[slot], self.recv.at[slot], at.row, to)
        copy.start()
        self.copies.append(copy)

    def took(self, s, kind, way):
        slot = (s * 3 + kind) * 2 + way
        arrived(self.hops.at[slot], self.recv.at[slot])
        return self.hops[slot].astype(F32)

    def act(self, n):
        s, dy = ORDER[n]
        self.merge(n)
        if dy == 2:
            self.hop(n, LOW, s, 0, 0)
            self.hop(n, HIGH, s, 0, 1)
        elif dy == 1:
            self.hop(n, HIGH, s, 1, 0)
        elif dy == 3:
            self.hop(n, LOW, s, 1, 1)

    def relay(self, s):
        first = 4 * (1 - s)
        for n, half, way in ((first + 1, LOW, 0), (first + 2, HIGH, 1)):
            own = self.own(n)
            own[:, half] = own[:, half] + self.took(s, 0, way)
            self.hop(n, half, s, 2, way)

    def finish(self, s):
        own = self.own(4 * (1 - s) + 3)
        for half, kinds in ((LOW, (2, 1)), (HIGH, (1, 2))):
            own[:, half] = own[:, half] + self.took(s, kinds[0], 0) + self.took(s, kinds[1], 1)
        if s == 1:
            at = self.at
            copy = remote(
                own, self.last, self.send.at[12], self.recv.at[12], at.row, at.inner_at(1, 0)
            )
            copy.start()
            self.copies.append(copy)

    def total(self):
        arrived(self.last, self.recv.at[12])
        own = self.own(7)
        own[...] = own[...] + self.last[...]
        return own

    def run(self, compute):
        for n in range(8):
            compute(n)
            self.offer(n)
            if 1 <= n <= 4:
                self.act(n - 1)
        return self.rest()

    def rest(self):
        self.relay(1)
        for n in range(4, 8):
            self.act(n)
        self.finish(1)
        self.relay(0)
        self.finish(0)
        return self.total()

    def wait_sends(self):
        for copy in self.inner + self.copies:
            copy.wait_send()


def update_kernel(
    scale, cols_ref, u_ref, v_ref, p_ref, q_ref, sketch_ref, left_ref, right_ref,
    panel, vbuf, sown, sbuf, gown, gsib, cown, coupled, coupling,
    tiles, mid, p_rows, q_rows, part, sibbuf, d_hops, d_last, r_hops, r_last,
    sample, dsum, gpart, grbuf, work, inv, lbuf, bown, basis, ib,
    local, v_send, v_recv, s_send, s_recv, g_send, g_recv, c_send, c_recv, k_send, k_recv,
    u_send, u_recv, di_send, di_recv, d_send, d_recv, gr_send, gr_recv, l_send, l_recv,
    b_send, b_recv, bh_recv, f_send, f_recv, ri_send, ri_recv, r_send, r_recv,
    u_own, their_cols, swapped, cols_sem, i_send, i_recv, t_send, t_recv,
):
    at = Place()
    row, me, core, base, sib = at.row, at.me, at.core, at.base, at.sib
    owner_core = row // 4
    slot = lax.rem(row, 4)
    my_rows = pl.ds(pl.multiple_of(me * 128, 128), 128)

    half_z = lax.rem(row, 2)
    partner = at.row_at(0, 1)
    own_u = pltpu.make_async_copy(u_ref, u_own, local.at[0])
    own_u.start()
    start_panel = pltpu.make_async_copy(u_ref.at[:, :, half_z], panel.at[row], local.at[4])
    start_panel.start()
    load_p = pltpu.make_async_copy(p_ref.at[:, my_rows, :], p_rows, local.at[1])
    load_p.start()
    load_q = pltpu.make_async_copy(q_ref.at[:, my_rows, :], q_rows, local.at[2])
    load_q.start()
    load_tiles = pltpu.make_async_copy(q_ref.at[pl.ds(0, 4)], tiles, local.at[3])
    load_tiles.start()

    partners = [(lax.rem(row + d, 8), base + h) for d in range(1, 8) for h in range(2)]
    partners += [(row, lax.rem(me + d, 16)) for d in range(1, 16)]
    greet(partners, len(partners))
    cols_copy = remote(cols_ref, their_cols, cols_sem.at[0], cols_sem.at[1], partner, me)
    cols_copy.start()

    v_copies = []
    for n in range(8):
        kk, hh = lax.rem(slot + n % 4, 4), lax.rem(n // 4 + core, 2)
        to = core * 4 + kk
        copy = Send(
            v_ref.at[kk, pl.ds(pl.multiple_of(hh * 1024, 1024), 1024), :],
            vbuf.at[:, pl.ds(pl.multiple_of(row * 128, 128), 128)],
            v_send.at[n], v_recv.at[row], to, base + hh,
            jnp.logical_and(to == row, core == hh),
        )
        copy.start()
        v_copies.append(copy)

    s_copies = []
    own_u.wait()
    for kk in range(4):
        sown[kk] = dot_t(u_own[kk].reshape(2048, 128), sketch_ref[...])
        to = core * 4 + kk
        copy = Send(
            sown.at[kk], sbuf.at[slot], s_send.at[kk], s_recv.at[slot],
            to, base + owner_core, jnp.logical_and(to == row, core == owner_core),
        )
        copy.start()
        s_copies.append(copy)

    load_tiles.wait()
    for c in range(4):
        mid[c] = dot_t(tiles[c], sketch_ref[...])
    load_tiles = pltpu.make_async_copy(q_ref.at[pl.ds(4, 4)], tiles, local.at[3])
    load_tiles.start()
    load_tiles.wait()
    for c in range(4):
        mid[4 + c] = dot_t(tiles[c], sketch_ref[...])
    load_p.wait()
    for c in range(8):
        sample[c] = dot(p_rows[c].astype(F32), mid[c], HIGHEST)
    load_tiles = pltpu.make_async_copy(p_ref.at[pl.ds(0, 4)], tiles, local.at[3])
    load_tiles.start()

    for i in range(8):
        arrived(vbuf.at[:, pl.ds(i * 128, 128)], v_recv.at[i])

    def gram_pair(pair, half):
        right = vbuf[:, pl.ds(pl.multiple_of(half * 512, 512), 512)]
        return dot_t(vbuf[:, pl.ds(pair * 256, 256)], right)

    g_copies = []
    for pair in range(4):
        value = gram_pair(pair, 1 - core)
        for p in range(2):
            part[pair * 2 + p, 0, :, :512] = value[p * 128 : p * 128 + 128]
        two = pl.ds(pair * 2, 2)
        copy = remote(
            part.at[two, 0, :, LOW], gsib.at[two], g_send.at[pair], g_recv.at[pair], row, sib
        )
        copy.start()
        g_copies.append(copy)
    for pair in range(4):
        value = gram_pair(pair, core)
        for p in range(2):
            for j in range(4):
                gown[pair * 2 + p, j] = value[p * 128 : p * 128 + 128, j * 128 : j * 128 + 128]
    for j in range(4):
        arrived(sbuf.at[j], s_recv.at[j])
    c_copies = []
    for i in range(8):
        if i % 2 == 0:
            g_copies[i // 2].wait_recv()
        for j in range(4):
            total = gown[i, j] + gsib[i, :, j * 128 : j * 128 + 128]
            gown[i, j] = total
            cown[i * 128 : i * 128 + 128, j * 128 : j * 128 + 128] = dot(
                total, sbuf[j], HIGHEST
            ).astype(BF16)
        copy = Send(
            cown.at[pl.ds(i * 128, 128), :],
            coupled.at[
                pl.ds(pl.multiple_of(slot * 128, 128), 128),
                pl.ds(pl.multiple_of(core * 512, 512), 512),
            ],
            c_send.at[i], c_recv.at[slot * 2 + core], i, base + owner_core,
            jnp.logical_and(row == i, core == owner_core),
        )
        copy.start()
        c_copies.append(copy)
    for kk in range(4):
        for hh in range(2):
            arrived(
                coupled.at[pl.ds(kk * 128, 128), pl.ds(hh * 512, 512)], c_recv.at[kk * 2 + hh]
            )
    for copy in g_copies:
        copy.wait_send()

    u_copies = []

    def pass_panel(index, piece, dx, dz):
        ref = panel.at[index] if piece is None else panel.at[index, pl.ds(piece * 2, 2)]
        n = len(u_copies)
        copy = remote(ref, ref, u_send.at[n], u_recv.at[n], at.row_at(dx, dz), me)
        copy.start()
        u_copies.append(copy)

    def panel_here(n, index, piece=None):
        ref = panel.at[index] if piece is None else panel.at[index, pl.ds(piece * 2, 2)]
        arrived(ref, u_recv.at[n])

    start_panel.wait()
    give = u_own.at[:, :, 1 - half_z]
    copy = remote(give, panel.at[row], u_send.at[0], u_recv.at[0], partner, me)
    copy.start()
    u_copies.append(copy)
    pass_panel(row, None, 1, 0)
    pass_panel(row, None, 3, 0)

    def d_block(n):
        chip = at.chip_at(*ORDER[n])
        left = jnp.concatenate([u_own[kk, chip].reshape(256, 128) for kk in range(4)], axis=1)
        value = dot(left, coupled[...])
        part[position(n), 0] = value[:128]
        part[position(n), 1] = value[128:]

    def second_leg():
        panel_here(0, partner)
        pass_panel(partner, None, 1, 0)
        pass_panel(partner, None, 3, 0)
        for n, dx in ((1, 3), (2, 1)):
            panel_here(n, at.row_at(dx, 0))
            pass_panel(at.row_at(dx, 0), n - 1, 4 - dx, 0)

    def third_leg():
        for n, dx in ((3, 3), (4, 1)):
            panel_here(n, at.row_at(dx, 1))
            pass_panel(at.row_at(dx, 1), n - 3, 4 - dx, 0)

    reduction = Reduction(
        at, part, sibbuf, None, d_hops, d_last, (di_send, di_recv, d_send, d_recv)
    )
    total = reduction.run(d_block)
    for j in range(8):
        dsum[j] = total[:, j * 128 : j * 128 + 128]

    gram_copies = []
    for c in range(8):
        value = sample[c] - dsum[cols_ref[c]]
        sample[c] = value
        gpart[c] = dot_t(value, value, HIGHEST)
        to = c * 2 + c % 2
        copy = Send(
            gpart.at[c], grbuf.at[me], gr_send.at[c], gr_recv.at[me], row, to, me == to
        )
        copy.start()
        gram_copies.append(copy)
    second_leg()

    factors = core == lax.rem(at.chip, 2)
    l_copies = []
    for n, step in enumerate(ORDER[:7]):
        for h in range(2):
            l_copies.append(
                remote(
                    inv, lbuf.at[at.chip], l_send.at[n * 2 + h], l_recv.at[at.chip],
                    row, at.chip_at(*step) * 2 + h,
                )
            )
    l_copies.append(remote(inv, lbuf.at[at.chip], l_send.at[14], l_recv.at[at.chip], row, sib))

    @pl.when(factors)
    def _():
        gram = jnp.zeros((128, 128), F32)
        for m in range(16):
            arrived(grbuf.at[m], gr_recv.at[m])
            gram = gram + grbuf[m]
        inverse_factor(gram, work, inv)
        for copy in l_copies:
            copy.start()
        lbuf[at.chip] = inv[...]

    @pl.when(jnp.logical_not(factors))
    def _():
        arrived(lbuf.at[at.chip], l_recv.at[at.chip])

    for i in range(8):
        copy = Send(
            gown.at[i], coupling.at[slot, pl.ds(core * 4, 4)],
            k_send.at[i], k_recv.at[slot * 2 + core], i, base + owner_core,
            jnp.logical_and(row == i, core == owner_core),
        )
        copy.start()
        c_copies.append(copy)
    for step in ORDER[:7]:
        source = at.chip_at(*step)
        arrived(lbuf.at[source], l_recv.at[source])
    for c in range(8):
        value = dot_nt(sample[c], lbuf[c], HIGHEST)
        left_ref[c] = value * scale
        bown[:, c * 128 : c * 128 + 128] = value.astype(BF16)

    b_copies, f_copies = [], []

    def block(m, half=None):
        rows = pl.ds(pl.multiple_of(m * 128, 128), 128)
        return basis.at[rows, :] if half is None else basis.at[rows, half]

    def pass_basis(source, dest, recv, dz, dy):
        copy = remote(source, dest, b_send.at[len(b_copies)], recv, row, at.inner_at(dz, dy))
        copy.start()
        b_copies.append(copy)

    def to_sib(source, dest, n):
        copy = remote(source, dest, f_send.at[n], f_recv.at[n], row, sib)
        copy.start()
        f_copies.append(copy)

    pass_basis(bown, block(me), b_recv.at[0], 1, 0)
    pass_basis(bown, block(me), b_recv.at[1], 0, 1)
    pass_basis(bown, block(me), b_recv.at[2], 0, 3)
    to_sib(bown, block(me), 0)
    basis[my_rows, :] = bown[...]
    other = at.inner_at(1, 0)
    arrived(block(other), b_recv.at[0])
    pass_basis(block(other), block(other), b_recv.at[3], 0, 1)
    pass_basis(block(other), block(other), b_recv.at[4], 0, 3)
    to_sib(block(other), block(other), 1)
    for s in range(2):
        for way, dy in ((0, 3), (1, 1)):
            m = at.inner_at(s, dy)
            half = HIGH if way else LOW
            n = 1 + s * 2 + way
            arrived(block(m), b_recv.at[n])
            pass_basis(block(m, half), block(m, half), bh_recv.at[s * 2 + way], 0, 3 if way else 1)
            to_sib(block(m), block(m), 1 + n)
    reduction.wait_sends()

    def basis_term(n, dz, dy, first=False):
        chip = at.chip_at(dz, dy)
        if n < 6:
            m = chip * 2 + 1 - core
            arrived(block(m), f_recv.at[n])
        rows = pl.ds(pl.multiple_of(chip * 256, 256), 256)
        for kk in range(4):
            for h in range(2):
                value = dot_t(u_own[kk, chip].reshape(256, 128), basis[rows, h * 512 : h * 512 + 512])
                gsib[kk * 2 + h] = value if first else gsib[kk * 2 + h] + value

    basis_term(0, 0, 0, True)
    basis_term(1, 1, 0)
    basis_term(2, 0, 3)
    basis_term(3, 0, 1)
    basis_term(4, 1, 3)
    basis_term(5, 1, 1)
    third_leg()
    for s in range(2):
        m = at.inner_at(s, 2)
        for way in range(2):
            half = HIGH if way else LOW
            arrived(block(m, half), bh_recv.at[s * 2 + way])
            to_sib(block(m, half), block(m, half), 6 + s * 2 + way)
    for s in range(2):
        m = at.chip_at(s, 2) * 2 + 1 - core
        for way in range(2):
            arrived(block(m, HIGH if way else LOW), f_recv.at[6 + s * 2 + way])
        basis_term(6 + s, s, 2)

    for kk in range(4):
        for hh in range(2):
            arrived(coupling.at[kk, pl.ds(hh * 4, 4)], k_recv.at[kk * 2 + hh])
    i_copies = []
    for kk in range(4):
        for c in range(8):
            lanes = pl.ds((c % 4) * 128, 128)
            ib[half_z, kk * 128 : kk * 128 + 128, c * 128 : c * 128 + 128] = dot_t(
                coupling[kk, cols_ref[c]], gsib[kk * 2 + c // 4, :, lanes], HIGHEST
            ).astype(BF16)
        ref = ib.at[half_z, pl.ds(kk * 128, 128), :]
        copy = remote(ref, ref, i_send.at[kk], i_recv.at[kk], partner, me)
        copy.start()
        i_copies.append(copy)
    panel_here(5, at.row_at(2, 0), 0)
    panel_here(6, at.row_at(2, 0), 1)
    panel_here(7, at.row_at(2, 1), 0)
    panel_here(8, at.row_at(2, 1), 1)

    def terms(s, which, cols):
        chips = pl.ds(pl.multiple_of(lax.rem(at.z + s, 2) * 4, 4), 4)
        for c in range(8):
            lanes = pl.ds(c * 128, 128)
            col = cols[c]
            left = jnp.concatenate(
                [panel[col, kk, chips].reshape(512, 128) for kk in range(4)], axis=1
            )
            value = dot(left, ib[which, :, lanes])
            for y in range(4):
                part[s * 4 + lax.rem(y + 4 - at.y, 4), which, :, lanes] = value[
                    y * 128 : y * 128 + 128
                ]

    mine = core == half_z
    others = core != half_z

    def projection():
        return Reduction(
            at, part, sibbuf, vbuf, r_hops, r_last, (ri_send, ri_recv, r_send, r_recv)
        )

    offers = [projection().to_sibling(n) for n in range(8)]
    for s in range(2):
        terms(1 - s, half_z, cols_ref)

        @pl.when(others)
        def _():
            for n in range(4):
                offers[s * 4 + n].start()

    @pl.when(mine)
    def _():
        sums = projection()
        for n in range(4):
            sums.act(n)
        sums.rest()
        for copy in sums.copies:
            copy.wait_send()

    def p_basis():
        for t in range(2):
            if t == 1:
                again = pltpu.make_async_copy(p_ref.at[pl.ds(4, 4)], tiles, local.at[3])
                again.start()
                again.wait()
            for c in range(4):
                n = t * 4 + c
                mid[n] = dot_t(tiles[c], basis[:, n * 128 : n * 128 + 128])
        for c in range(8):
            sample[c] = dot(q_rows[c].astype(F32), mid[c], HIGHEST)

    load_tiles.wait()
    load_q.wait()
    p_basis()
    arrived(their_cols, cols_sem.at[1])
    for kk in range(4):
        arrived(ib.at[1 - half_z, pl.ds(kk * 128, 128), :], i_recv.at[kk])
    for s in range(2):
        terms(1 - s, 1 - half_z, their_cols)

        @pl.when(mine)
        def _():
            for n in range(4):
                offers[s * 4 + n].start()

    def write_right(source):
        for c in range(8):
            right_ref[c] = (sample[c] - source[:, c * 128 : c * 128 + 128]) * (1.0 / scale)

    @pl.when(mine)
    def _():
        write_right(projection().own(7))

    @pl.when(others)
    def _():
        sums = projection()
        for n in range(4):
            sums.act(n)
        swap = remote(sums.rest(), swapped, t_send, t_recv, partner, sib)
        swap.start()
        for copy in sums.copies:
            copy.wait_send()
        swap.wait_recv()
        write_right(swapped)
        swap.wait_send()

    for copy in offers:
        copy.wait_send()
    cols_copy.wait_send()

    @pl.when(factors)
    def _():
        for copy in l_copies:
            copy.wait_send()

    for copy in v_copies + s_copies + c_copies + u_copies + gram_copies:
        copy.wait_send()
    for copy in b_copies + f_copies + i_copies:
        copy.wait_send()


def update(u, v, p, q, sketch, cols, scale):
    dma = pltpu.SemaphoreType.DMA
    vmem = pl.BlockSpec(memory_space=pltpu.VMEM)
    smem = pl.BlockSpec(memory_space=pltpu.SMEM)
    hbm = pl.BlockSpec(memory_space=pl.ANY)

    def kernel(*refs):
        update_kernel(scale, *refs)

    squares = jax.ShapeDtypeStruct((8, 128, 128), F32)
    return pl.pallas_call(
        kernel,
        out_shape=(squares, squares),
        in_specs=[smem, hbm, hbm, hbm, hbm, vmem],
        out_specs=(vmem, vmem),
        scratch_shapes=[
            pltpu.VMEM((8, 4, 8, 128, 128), BF16),
            pltpu.VMEM((1024, 1024), BF16),
            pltpu.VMEM((4, 128, 128), F32),
            pltpu.VMEM((4, 128, 128), F32),
            pltpu.VMEM((8, 4, 128, 128), F32),
            pltpu.VMEM((8, 128, 512), F32),
            pltpu.VMEM((1024, 512), BF16),
            pltpu.VMEM((512, 1024), BF16),
            pltpu.VMEM((4, 8, 128, 128), F32),
            pltpu.VMEM((4, 2048, 128), BF16),
            pltpu.VMEM((8, 128, 128), F32),
            pltpu.VMEM((8, 128, 128), BF16),
            pltpu.VMEM((8, 128, 128), BF16),
            pltpu.VMEM((8, 2, 128, 1024), F32),
            pltpu.VMEM((8, 128, 1024), F32),
            pltpu.VMEM((12, 128, 512), F32),
            pltpu.VMEM((128, 1024), F32),
            pltpu.VMEM((12, 128, 512), BF16),
            pltpu.VMEM((128, 1024), F32),
            pltpu.VMEM((8, 128, 128), F32),
            pltpu.VMEM((8, 128, 128), F32),
            pltpu.VMEM((8, 128, 128), F32),
            pltpu.VMEM((16, 128, 128), F32),
            pltpu.VMEM((128, 128), F32),
            pltpu.VMEM((128, 128), F32),
            pltpu.VMEM((8, 128, 128), F32),
            pltpu.VMEM((128, 1024), BF16),
            pltpu.VMEM((2048, 1024), BF16),
            pltpu.VMEM((2, 512, 1024), BF16),
            dma((5,)), dma((8,)), dma((8,)), dma((4,)), dma((4,)), dma((4,)), dma((4,)),
            dma((8,)), dma((8,)), dma((8,)), dma((8,)),
            dma((9,)), dma((9,)), dma((8,)), dma((8,)), dma((13,)), dma((13,)),
            dma((8,)), dma((16,)), dma((15,)), dma((8,)),
            dma((9,)), dma((5,)), dma((4,)), dma((10,)), dma((10,)),
            dma((8,)), dma((8,)), dma((13,)), dma((13,)),
            pltpu.VMEM((4, 8, 2, 128, 128), BF16),
            pltpu.SMEM((8,), jnp.int32),
            pltpu.VMEM((128, 1024), F32),
            dma((2,)), dma((4,)), dma((4,)), dma, dma,
        ],
        compiler_params=pltpu.CompilerParams(
            collective_id=1, has_side_effects=True, vmem_limit_bytes=VMEM_LIMIT
        ),
        cost_estimate=pl.CostEstimate(
            flops=13_000_000_000, bytes_accessed=30_000_000, transcendentals=0
        ),
    )(cols, u, v, p, q, sketch)


def body(left_u, left_v, tile_p, tile_q, sketch, tile_cols):
    factor_scale = math.sqrt(sketch.shape[0])
    new_left, new_right = update(
        left_u[0].reshape(4, 8, 2, 128, 128), left_v[0], tile_p[0], tile_q[0], sketch, tile_cols[0], factor_scale
    )
    return new_left[None], new_right[None]


def solution(mesh):
    return jax.shard_map(
        body,
        mesh=mesh,
        in_specs=(
            P("rows", "inner", None, None),
            P("rows", "inner", None, None),
            P("rows", None, None, None),
            P("rows", None, None, None),
            P(),
            P("rows", None),
        ),
        out_specs=(P("rows", None, "inner", None), P("rows", None, "inner", None)),
        check_vma=False,
    )
```

```python
import math

import jax
import jax.numpy as jnp
from jax import lax
from jax.experimental import pallas as pl
from jax.experimental.pallas import tpu as pltpu
from jax.sharding import PartitionSpec as P

MESH = pl.DeviceIdType.MESH
HIGHEST = lax.Precision.HIGHEST
F32 = jnp.float32
BF16 = jnp.bfloat16
VMEM_LIMIT = 61 * 1024 * 1024


def device(row, place):
    return {"rows": row, "inner": place}


def greet(partners, count):
    barrier = pltpu.get_barrier_semaphore()
    for row, place in partners:
        pl.semaphore_signal(barrier, inc=1, device_id=device(row, place), device_id_type=MESH)
    pl.semaphore_wait(barrier, count)


def remote(src, dst, send_sem, recv_sem, row, place):
    return pltpu.make_async_remote_copy(
        src_ref=src, dst_ref=dst, send_sem=send_sem, recv_sem=recv_sem,
        device_id=device(row, place), device_id_type=MESH,
    )


class Send:
    def __init__(self, src, dst, send_sem, recv_sem, row, place, is_self):
        self.far = remote(src, dst, send_sem, recv_sem, row, place)
        self.near = pltpu.make_async_copy(src, dst, recv_sem)
        self.is_self = is_self

    def start(self):
        @pl.when(jnp.logical_not(self.is_self))
        def _():
            self.far.start()

        @pl.when(self.is_self)
        def _():
            self.near.start()

    def wait_send(self):
        @pl.when(jnp.logical_not(self.is_self))
        def _():
            self.far.wait_send()


def arrived(ref, sem):
    pltpu.make_async_copy(ref, ref, sem).wait()


def dot(a, b, precision=None):
    return jnp.dot(a, b, preferred_element_type=F32, precision=precision)


def dot_t(a, b, precision=None):
    return lax.dot_general(
        a, b, (((0,), (0,)), ((), ())), preferred_element_type=F32, precision=precision
    )


def dot_nt(a, b, precision=None):
    return lax.dot_general(
        a, b, (((1,), (1,)), ((), ())), preferred_element_type=F32, precision=precision
    )

LOW, HIGH = pl.ds(0, 512), pl.ds(512, 512)
ORDER = [(1, 2), (1, 1), (1, 3), (1, 0), (0, 2), (0, 1), (0, 3), (0, 0)]


def position(n):
    return ORDER[n][0] * 4 + ORDER[n][1]


class Place:
    def __init__(self):
        self.row, self.me = lax.axis_index("rows"), lax.axis_index("inner")
        self.core = lax.rem(self.me, 2)
        self.chip = self.me // 2
        self.z, self.y = self.chip // 4, lax.rem(self.chip, 4)
        self.base = self.me - self.core
        self.sib = self.base + 1 - self.core

    def chip_at(self, dz, dy):
        return lax.rem(self.z + dz, 2) * 4 + lax.rem(self.y + dy, 4)

    def inner_at(self, dz, dy):
        return self.chip_at(dz, dy) * 2 + self.core

    def row_at(self, dx, dz):
        x, z = self.row // 2, lax.rem(self.row, 2)
        return lax.rem(x + dx, 4) * 2 + lax.rem(z + dz, 2)


def inverse_factor(gram, work, inv):
    order = gram.shape[0]
    strip, group = 16, 4
    row_id = lax.broadcasted_iota(jnp.int32, (order, order), 0)
    col_id = lax.broadcasted_iota(jnp.int32, (order, order), 1)
    diagonal = row_id == col_id
    ridge = 1e-06 * jnp.sum(jnp.where(diagonal, gram, 0.0)) / order
    work[...] = gram + jnp.where(diagonal, ridge, 0.0)
    inv[...] = jnp.where(diagonal, 1.0, 0.0)
    within = lax.broadcasted_iota(jnp.int32, (strip, order), 0)
    full = (strip, order)
    for lo in range(0, order, strip):
        a, m = work[lo : lo + strip, :], inv[lo : lo + strip, :]
        for first in range(0, strip, group):
            cols, rows, m_rows = [], [], []
            for k in range(group):
                at_col, at_row = lo + first + k, first + k
                cols.append(jnp.broadcast_to(a[:, at_col : at_col + 1], full))
                rows.append(jnp.broadcast_to(a[at_row : at_row + 1, :], full))
                m_rows.append(jnp.broadcast_to(m[at_row : at_row + 1, :], full))
            small = {}
            for k in range(group):
                for i in range(k, group):
                    at_row = first + i
                    value = jnp.broadcast_to(cols[k][at_row : at_row + 1, :], full)
                    for p in range(k):
                        value = value - small[i, p] * small[k, p]
                    small[i, k] = lax.rsqrt(value) if i == k else value * small[k, k]
            for k in range(group):
                for p in range(k):
                    cols[k] = cols[k] - small[k, p] * cols[p]
                    rows[k] = rows[k] - small[k, p] * rows[p]
                    m_rows[k] = m_rows[k] - small[k, p] * m_rows[p]
                cols[k] = cols[k] * small[k, k]
                rows[k] = rows[k] * small[k, k]
                m_rows[k] = m_rows[k] * small[k, k]
            below = within >= first + group
            for k in range(group):
                factor = jnp.where(below, cols[k], 0.0)
                a, m = a - factor * rows[k], m - factor * m_rows[k]
            for k in range(group):
                here = within == first + k
                a, m = jnp.where(here, rows[k], a), jnp.where(here, m_rows[k], m)
        inv[lo : lo + strip, :] = m
        rest = lo + strip
        if rest < order:
            update = dot_t(a, jnp.concatenate([a, m], axis=1), HIGHEST)
            work[rest:, :] = work[rest:, :] - update[rest:, :order]
            inv[rest:, :] = inv[rest:, :] - update[rest:, order:]


class Reduction:
    def __init__(self, at, part, sibbuf, wire, hops, last, sems):
        self.at, self.part, self.sibbuf = at, part, sibbuf
        self.wire, self.hops, self.last = wire, hops, last
        self.i_send, self.i_recv, self.send, self.recv = sems
        self.copies, self.inner = [], []

    def own(self, n):
        return self.part.at[position(n), self.at.core]

    def to_sibling(self, n):
        at = self.at
        return remote(
            self.part.at[position(n), 1 - at.core], self.sibbuf.at[n],
            self.i_send.at[n], self.i_recv.at[n], at.row, at.sib,
        )

    def offer(self, n):
        copy = self.to_sibling(n)
        copy.start()
        self.inner.append(copy)

    def merge(self, n):
        arrived(self.sibbuf.at[n], self.i_recv.at[n])
        own = self.own(n)
        own[...] = own[...] + self.sibbuf[n]

    def hop(self, n, half, s, kind, way):
        at = self.at
        if self.wire is None:
            source = self.part.at[position(n), at.core, :, half]
        else:
            source = self.wire.at[pl.ds(n * 128, 128), half]
            source[...] = self.own(n)[:, half].astype(source.dtype)
        slot = (s * 3 + kind) * 2 + way
        to = at.inner_at(0, 1 if way == 0 else 3)
        copy = remote(source, self.hops.at[slot], self.send.at[slot], self.recv.at[slot], at.row, to)
        copy.start()
        self.copies.append(copy)

    def took(self, s, kind, way):
        slot = (s * 3 + kind) * 2 + way
        arrived(self.hops.at[slot], self.recv.at[slot])
        return self.hops[slot].astype(F32)

    def act(self, n):
        s, dy = ORDER[n]
        self.merge(n)
        if dy == 2:
            self.hop(n, LOW, s, 0, 0)
            self.hop(n, HIGH, s, 0, 1)
        elif dy == 1:
            self.hop(n, HIGH, s, 1, 0)
        elif dy == 3:
            self.hop(n, LOW, s, 1, 1)

    def relay(self, s):
        first = 4 * (1 - s)
        for n, half, way in ((first + 1, LOW, 0), (first + 2, HIGH, 1)):
            own = self.own(n)
            own[:, half] = own[:, half] + self.took(s, 0, way)
            self.hop(n, half, s, 2, way)

    def finish(self, s):
        own = self.own(4 * (1 - s) + 3)
        for half, kinds in ((LOW, (2, 1)), (HIGH, (1, 2))):
            own[:, half] = own[:, half] + self.took(s, kinds[0], 0) + self.took(s, kinds[1], 1)
        if s == 1:
            at = self.at
            copy = remote(
                own, self.last, self.send.at[12], self.recv.at[12], at.row, at.inner_at(1, 0)
            )
            copy.start()
            self.copies.append(copy)

    def total(self):
        arrived(self.last, self.recv.at[12])
        own = self.own(7)
        own[...] = own[...] + self.last[...]
        return own

    def run(self, compute):
        for n in range(8):
            compute(n)
            self.offer(n)
            if 1 <= n <= 4:
                self.act(n - 1)
        return self.rest()

    def rest(self):
        self.relay(1)
        for n in range(4, 8):
            self.act(n)
        self.finish(1)
        self.relay(0)
        self.finish(0)
        return self.total()

    def wait_sends(self):
        for copy in self.inner + self.copies:
            copy.wait_send()


def update_kernel(
    scale, cols_ref, u_ref, v_ref, p_ref, q_ref, sketch_ref, left_ref, right_ref,
    panel, vbuf, sown, sbuf, gown, gsib, cown, coupled, coupling,
    tiles, mid, p_rows, q_rows, part, sibbuf, d_hops, d_last, r_hops, r_last,
    sample, dsum, gpart, grbuf, work, inv, lbuf, bown, basis, ib,
    local, v_send, v_recv, s_send, s_recv, g_send, g_recv, c_send, c_recv, k_send, k_recv,
    u_send, u_recv, di_send, di_recv, d_send, d_recv, gr_send, gr_recv, l_send, l_recv,
    b_send, b_recv, bh_recv, f_send, f_recv, ri_send, ri_recv, r_send, r_recv,
    u_own, their_cols, swapped, cols_sem, i_send, i_recv, t_send, t_recv,
):
    at = Place()
    row, me, core, base, sib = at.row, at.me, at.core, at.base, at.sib
    owner_core = row // 4
    slot = lax.rem(row, 4)
    my_rows = pl.ds(pl.multiple_of(me * 128, 128), 128)

    half_z = lax.rem(row, 2)
    partner = at.row_at(0, 1)
    own_u = pltpu.make_async_copy(u_ref, u_own, local.at[0])
    own_u.start()
    start_panel = pltpu.make_async_copy(u_ref.at[:, :, half_z], panel.at[row], local.at[4])
    start_panel.start()
    load_p = pltpu.make_async_copy(p_ref.at[:, my_rows, :], p_rows, local.at[1])
    load_p.start()
    load_q = pltpu.make_async_copy(q_ref.at[:, my_rows, :], q_rows, local.at[2])
    load_q.start()
    load_tiles = pltpu.make_async_copy(q_ref.at[pl.ds(0, 4)], tiles, local.at[3])
    load_tiles.start()

    partners = [(lax.rem(row + d, 8), base + h) for d in range(1, 8) for h in range(2)]
    partners += [(row, lax.rem(me + d, 16)) for d in range(1, 16)]
    greet(partners, len(partners))
    cols_copy = remote(cols_ref, their_cols, cols_sem.at[0], cols_sem.at[1], partner, me)
    cols_copy.start()

    v_copies = []
    for n in range(8):
        kk, hh = lax.rem(slot + n % 4, 4), lax.rem(n // 4 + core, 2)
        to = core * 4 + kk
        copy = Send(
            v_ref.at[kk, pl.ds(pl.multiple_of(hh * 1024, 1024), 1024), :],
            vbuf.at[:, pl.ds(pl.multiple_of(row * 128, 128), 128)],
            v_send.at[n], v_recv.at[row], to, base + hh,
            jnp.logical_and(to == row, core == hh),
        )
        copy.start()
        v_copies.append(copy)

    s_copies = []
    own_u.wait()
    for kk in range(4):
        sown[kk] = dot_t(u_own[kk].reshape(2048, 128), sketch_ref[...])
        to = core * 4 + kk
        copy = Send(
            sown.at[kk], sbuf.at[slot], s_send.at[kk], s_recv.at[slot],
            to, base + owner_core, jnp.logical_and(to == row, core == owner_core),
        )
        copy.start()
        s_copies.append(copy)

    load_tiles.wait()
    for c in range(4):
        mid[c] = dot_t(tiles[c], sketch_ref[...])
    load_tiles = pltpu.make_async_copy(q_ref.at[pl.ds(4, 4)], tiles, local.at[3])
    load_tiles.start()
    load_tiles.wait()
    for c in range(4):
        mid[4 + c] = dot_t(tiles[c], sketch_ref[...])
    load_p.wait()
    for c in range(8):
        sample[c] = dot(p_rows[c].astype(F32), mid[c], HIGHEST)
    load_tiles = pltpu.make_async_copy(p_ref.at[pl.ds(0, 4)], tiles, local.at[3])
    load_tiles.start()

    for i in range(8):
        arrived(vbuf.at[:, pl.ds(i * 128, 128)], v_recv.at[i])

    def gram_pair(pair, half):
        right = vbuf[:, pl.ds(pl.multiple_of(half * 512, 512), 512)]
        return dot_t(vbuf[:, pl.ds(pair * 256, 256)], right)

    g_copies = []
    for pair in range(4):
        value = gram_pair(pair, 1 - core)
        for p in range(2):
            part[pair * 2 + p, 0, :, :512] = value[p * 128 : p * 128 + 128]
        two = pl.ds(pair * 2, 2)
        copy = remote(
            part.at[two, 0, :, LOW], gsib.at[two], g_send.at[pair], g_recv.at[pair], row, sib
        )
        copy.start()
        g_copies.append(copy)
    for pair in range(4):
        value = gram_pair(pair, core)
        for p in range(2):
            for j in range(4):
                gown[pair * 2 + p, j] = value[p * 128 : p * 128 + 128, j * 128 : j * 128 + 128]
    for j in range(4):
        arrived(sbuf.at[j], s_recv.at[j])
    c_copies = []
    for i in range(8):
        if i % 2 == 0:
            g_copies[i // 2].wait_recv()
        for j in range(4):
            total = gown[i, j] + gsib[i, :, j * 128 : j * 128 + 128]
            gown[i, j] = total
            cown[i * 128 : i * 128 + 128, j * 128 : j * 128 + 128] = dot(
                total, sbuf[j], HIGHEST
            ).astype(BF16)
        copy = Send(
            cown.at[pl.ds(i * 128, 128), :],
            coupled.at[
                pl.ds(pl.multiple_of(slot * 128, 128), 128),
                pl.ds(pl.multiple_of(core * 512, 512), 512),
            ],
            c_send.at[i], c_recv.at[slot * 2 + core], i, base + owner_core,
            jnp.logical_and(row == i, core == owner_core),
        )
        copy.start()
        c_copies.append(copy)
    for kk in range(4):
        for hh in range(2):
            arrived(
                coupled.at[pl.ds(kk * 128, 128), pl.ds(hh * 512, 512)], c_recv.at[kk * 2 + hh]
            )
    for copy in g_copies:
        copy.wait_send()

    u_copies = []

    def pass_panel(index, piece, dx, dz):
        ref = panel.at[index] if piece is None else panel.at[index, pl.ds(piece * 2, 2)]
        n = len(u_copies)
        copy = remote(ref, ref, u_send.at[n], u_recv.at[n], at.row_at(dx, dz), me)
        copy.start()
        u_copies.append(copy)

    def panel_here(n, index, piece=None):
        ref = panel.at[index] if piece is None else panel.at[index, pl.ds(piece * 2, 2)]
        arrived(ref, u_recv.at[n])

    start_panel.wait()
    give = u_own.at[:, :, 1 - half_z]
    copy = remote(give, panel.at[row], u_send.at[0], u_recv.at[0], partner, me)
    copy.start()
    u_copies.append(copy)
    pass_panel(row, None, 1, 0)
    pass_panel(row, None, 3, 0)

    def d_block(n):
        chip = at.chip_at(*ORDER[n])
        left = jnp.concatenate([u_own[kk, chip].reshape(256, 128) for kk in range(4)], axis=1)
        value = dot(left, coupled[...])
        part[position(n), 0] = value[:128]
        part[position(n), 1] = value[128:]

    def second_leg():
        panel_here(0, partner)
        pass_panel(partner, None, 1, 0)
        pass_panel(partner, None, 3, 0)
        for n, dx in ((1, 3), (2, 1)):
            panel_here(n, at.row_at(dx, 0))
            pass_panel(at.row_at(dx, 0), n - 1, 4 - dx, 0)

    def third_leg():
        for n, dx in ((3, 3), (4, 1)):
            panel_here(n, at.row_at(dx, 1))
            pass_panel(at.row_at(dx, 1), n - 3, 4 - dx, 0)

    reduction = Reduction(
        at, part, sibbuf, None, d_hops, d_last, (di_send, di_recv, d_send, d_recv)
    )
    total = reduction.run(d_block)
    for j in range(8):
        dsum[j] = total[:, j * 128 : j * 128 + 128]

    gram_copies = []
    for c in range(8):
        value = sample[c] - dsum[cols_ref[c]]
        sample[c] = value
        gpart[c] = dot_t(value, value, HIGHEST)
        to = c * 2 + c % 2
        copy = Send(
            gpart.at[c], grbuf.at[me], gr_send.at[c], gr_recv.at[me], row, to, me == to
        )
        copy.start()
        gram_copies.append(copy)
    second_leg()

    factors = core == lax.rem(at.chip, 2)
    l_copies = []
    for n, step in enumerate(ORDER[:7]):
        for h in range(2):
            l_copies.append(
                remote(
                    inv, lbuf.at[at.chip], l_send.at[n * 2 + h], l_recv.at[at.chip],
                    row, at.chip_at(*step) * 2 + h,
                )
            )
    l_copies.append(remote(inv, lbuf.at[at.chip], l_send.at[14], l_recv.at[at.chip], row, sib))

    @pl.when(factors)
    def _():
        gram = jnp.zeros((128, 128), F32)
        for m in range(16):
            arrived(grbuf.at[m], gr_recv.at[m])
            gram = gram + grbuf[m]
        inverse_factor(gram, work, inv)
        for copy in l_copies:
            copy.start()
        lbuf[at.chip] = inv[...]

    @pl.when(jnp.logical_not(factors))
    def _():
        arrived(lbuf.at[at.chip], l_recv.at[at.chip])

    for i in range(8):
        copy = Send(
            gown.at[i], coupling.at[slot, pl.ds(core * 4, 4)],
            k_send.at[i], k_recv.at[slot * 2 + core], i, base + owner_core,
            jnp.logical_and(row == i, core == owner_core),
        )
        copy.start()
        c_copies.append(copy)
    for step in ORDER[:7]:
        source = at.chip_at(*step)
        arrived(lbuf.at[source], l_recv.at[source])
    for c in range(8):
        value = dot_nt(sample[c], lbuf[c], HIGHEST)
        left_ref[c] = value * scale
        bown[:, c * 128 : c * 128 + 128] = value.astype(BF16)

    b_copies, f_copies = [], []

    def block(m, half=None):
        rows = pl.ds(pl.multiple_of(m * 128, 128), 128)
        return basis.at[rows, :] if half is None else basis.at[rows, half]

    def pass_basis(source, dest, recv, dz, dy):
        copy = remote(source, dest, b_send.at[len(b_copies)], recv, row, at.inner_at(dz, dy))
        copy.start()
        b_copies.append(copy)

    def to_sib(source, dest, n):
        copy = remote(source, dest, f_send.at[n], f_recv.at[n], row, sib)
        copy.start()
        f_copies.append(copy)

    pass_basis(bown, block(me), b_recv.at[0], 1, 0)
    pass_basis(bown, block(me), b_recv.at[1], 0, 1)
    pass_basis(bown, block(me), b_recv.at[2], 0, 3)
    to_sib(bown, block(me), 0)
    basis[my_rows, :] = bown[...]
    other = at.inner_at(1, 0)
    arrived(block(other), b_recv.at[0])
    pass_basis(block(other), block(other), b_recv.at[3], 0, 1)
    pass_basis(block(other), block(other), b_recv.at[4], 0, 3)
    to_sib(block(other), block(other), 1)
    for s in range(2):
        for way, dy in ((0, 3), (1, 1)):
            m = at.inner_at(s, dy)
            half = HIGH if way else LOW
            n = 1 + s * 2 + way
            arrived(block(m), b_recv.at[n])
            pass_basis(block(m, half), block(m, half), bh_recv.at[s * 2 + way], 0, 3 if way else 1)
            to_sib(block(m), block(m), 1 + n)
    reduction.wait_sends()

    def basis_term(n, dz, dy, first=False):
        chip = at.chip_at(dz, dy)
        if n < 6:
            m = chip * 2 + 1 - core
            arrived(block(m), f_recv.at[n])
        rows = pl.ds(pl.multiple_of(chip * 256, 256), 256)
        for kk in range(4):
            for h in range(2):
                value = dot_t(u_own[kk, chip].reshape(256, 128), basis[rows, h * 512 : h * 512 + 512])
                gsib[kk * 2 + h] = value if first else gsib[kk * 2 + h] + value

    basis_term(0, 0, 0, True)
    basis_term(1, 1, 0)
    basis_term(2, 0, 3)
    basis_term(3, 0, 1)
    third_leg()
    basis_term(4, 1, 3)
    basis_term(5, 1, 1)
    for s in range(2):
        m = at.inner_at(s, 2)
        for way in range(2):
            half = HIGH if way else LOW
            arrived(block(m, half), bh_recv.at[s * 2 + way])
            to_sib(block(m, half), block(m, half), 6 + s * 2 + way)
    for s in range(2):
        m = at.chip_at(s, 2) * 2 + 1 - core
        for way in range(2):
            arrived(block(m, HIGH if way else LOW), f_recv.at[6 + s * 2 + way])
        basis_term(6 + s, s, 2)

    for kk in range(4):
        for hh in range(2):
            arrived(coupling.at[kk, pl.ds(hh * 4, 4)], k_recv.at[kk * 2 + hh])
    i_copies = []
    for kk in range(4):
        for c in range(8):
            lanes = pl.ds((c % 4) * 128, 128)
            ib[half_z, kk * 128 : kk * 128 + 128, c * 128 : c * 128 + 128] = dot_t(
                coupling[kk, cols_ref[c]], gsib[kk * 2 + c // 4, :, lanes], HIGHEST
            ).astype(BF16)
        ref = ib.at[half_z, pl.ds(kk * 128, 128), :]
        copy = remote(ref, ref, i_send.at[kk], i_recv.at[kk], partner, me)
        copy.start()
        i_copies.append(copy)
    panel_here(5, at.row_at(2, 0), 0)
    panel_here(6, at.row_at(2, 0), 1)
    panel_here(7, at.row_at(2, 1), 0)
    panel_here(8, at.row_at(2, 1), 1)

    def terms(s, which, cols):
        chips = pl.ds(pl.multiple_of(lax.rem(at.z + s, 2) * 4, 4), 4)
        for c in range(8):
            lanes = pl.ds(c * 128, 128)
            col = cols[c]
            left = jnp.concatenate(
                [panel[col, kk, chips].reshape(512, 128) for kk in range(4)], axis=1
            )
            value = dot(left, ib[which, :, lanes])
            for y in range(4):
                part[s * 4 + lax.rem(y + 4 - at.y, 4), which, :, lanes] = value[
                    y * 128 : y * 128 + 128
                ]

    mine = core == half_z
    others = core != half_z

    def projection():
        return Reduction(
            at, part, sibbuf, vbuf, r_hops, r_last, (ri_send, ri_recv, r_send, r_recv)
        )

    offers = [projection().to_sibling(n) for n in range(8)]
    for s in range(2):
        terms(1 - s, half_z, cols_ref)

        @pl.when(others)
        def _():
            for n in range(4):
                offers[s * 4 + n].start()

    @pl.when(mine)
    def _():
        sums = projection()
        for n in range(4):
            sums.act(n)
        sums.rest()
        for copy in sums.copies:
            copy.wait_send()

    def p_basis():
        for t in range(2):
            if t == 1:
                again = pltpu.make_async_copy(p_ref.at[pl.ds(4, 4)], tiles, local.at[3])
                again.start()
                again.wait()
            for c in range(4):
                n = t * 4 + c
                mid[n] = dot_t(tiles[c], basis[:, n * 128 : n * 128 + 128])
        for c in range(8):
            sample[c] = dot(q_rows[c].astype(F32), mid[c], HIGHEST)

    load_tiles.wait()
    load_q.wait()
    p_basis()
    arrived(their_cols, cols_sem.at[1])
    for kk in range(4):
        arrived(ib.at[1 - half_z, pl.ds(kk * 128, 128), :], i_recv.at[kk])
    for s in range(2):
        terms(1 - s, 1 - half_z, their_cols)

        @pl.when(mine)
        def _():
            for n in range(4):
                offers[s * 4 + n].start()

    def write_right(source):
        for c in range(8):
            right_ref[c] = (sample[c] - source[:, c * 128 : c * 128 + 128]) * (1.0 / scale)

    @pl.when(mine)
    def _():
        write_right(projection().own(7))

    @pl.when(others)
    def _():
        sums = projection()
        for n in range(4):
            sums.act(n)
        swap = remote(sums.rest(), swapped, t_send, t_recv, partner, sib)
        swap.start()
        for copy in sums.copies:
            copy.wait_send()
        swap.wait_recv()
        write_right(swapped)
        swap.wait_send()

    for copy in offers:
        copy.wait_send()
    cols_copy.wait_send()

    @pl.when(factors)
    def _():
        for copy in l_copies:
            copy.wait_send()

    for copy in v_copies + s_copies + c_copies + u_copies + gram_copies:
        copy.wait_send()
    for copy in b_copies + f_copies + i_copies:
        copy.wait_send()


def update(u, v, p, q, sketch, cols, scale):
    dma = pltpu.SemaphoreType.DMA
    vmem = pl.BlockSpec(memory_space=pltpu.VMEM)
    smem = pl.BlockSpec(memory_space=pltpu.SMEM)
    hbm = pl.BlockSpec(memory_space=pl.ANY)

    def kernel(*refs):
        update_kernel(scale, *refs)

    squares = jax.ShapeDtypeStruct((8, 128, 128), F32)
    return pl.pallas_call(
        kernel,
        out_shape=(squares, squares),
        in_specs=[smem, hbm, hbm, hbm, hbm, vmem],
        out_specs=(vmem, vmem),
        scratch_shapes=[
            pltpu.VMEM((8, 4, 8, 128, 128), BF16),
            pltpu.VMEM((1024, 1024), BF16),
            pltpu.VMEM((4, 128, 128), F32),
            pltpu.VMEM((4, 128, 128), F32),
            pltpu.VMEM((8, 4, 128, 128), F32),
            pltpu.VMEM((8, 128, 512), F32),
            pltpu.VMEM((1024, 512), BF16),
            pltpu.VMEM((512, 1024), BF16),
            pltpu.VMEM((4, 8, 128, 128), F32),
            pltpu.VMEM((4, 2048, 128), BF16),
            pltpu.VMEM((8, 128, 128), F32),
            pltpu.VMEM((8, 128, 128), BF16),
            pltpu.VMEM((8, 128, 128), BF16),
            pltpu.VMEM((8, 2, 128, 1024), F32),
            pltpu.VMEM((8, 128, 1024), F32),
            pltpu.VMEM((12, 128, 512), F32),
            pltpu.VMEM((128, 1024), F32),
            pltpu.VMEM((12, 128, 512), BF16),
            pltpu.VMEM((128, 1024), F32),
            pltpu.VMEM((8, 128, 128), F32),
            pltpu.VMEM((8, 128, 128), F32),
            pltpu.VMEM((8, 128, 128), F32),
            pltpu.VMEM((16, 128, 128), F32),
            pltpu.VMEM((128, 128), F32),
            pltpu.VMEM((128, 128), F32),
            pltpu.VMEM((8, 128, 128), F32),
            pltpu.VMEM((128, 1024), BF16),
            pltpu.VMEM((2048, 1024), BF16),
            pltpu.VMEM((2, 512, 1024), BF16),
            dma((5,)), dma((8,)), dma((8,)), dma((4,)), dma((4,)), dma((4,)), dma((4,)),
            dma((8,)), dma((8,)), dma((8,)), dma((8,)),
            dma((9,)), dma((9,)), dma((8,)), dma((8,)), dma((13,)), dma((13,)),
            dma((8,)), dma((16,)), dma((15,)), dma((8,)),
            dma((9,)), dma((5,)), dma((4,)), dma((10,)), dma((10,)),
            dma((8,)), dma((8,)), dma((13,)), dma((13,)),
            pltpu.VMEM((4, 8, 2, 128, 128), BF16),
            pltpu.SMEM((8,), jnp.int32),
            pltpu.VMEM((128, 1024), F32),
            dma((2,)), dma((4,)), dma((4,)), dma, dma,
        ],
        compiler_params=pltpu.CompilerParams(
            collective_id=1, has_side_effects=True, vmem_limit_bytes=VMEM_LIMIT
        ),
        cost_estimate=pl.CostEstimate(
            flops=13_000_000_000, bytes_accessed=30_000_000, transcendentals=0
        ),
    )(cols, u, v, p, q, sketch)


def body(left_u, left_v, tile_p, tile_q, sketch, tile_cols):
    factor_scale = math.sqrt(sketch.shape[0])
    new_left, new_right = update(
        left_u[0].reshape(4, 8, 2, 128, 128), left_v[0], tile_p[0], tile_q[0], sketch, tile_cols[0], factor_scale
    )
    return new_left[None], new_right[None]


def solution(mesh):
    return jax.shard_map(
        body,
        mesh=mesh,
        in_specs=(
            P("rows", "inner", None, None),
            P("rows", "inner", None, None),
            P("rows", None, None, None),
            P("rows", None, None, None),
            P(),
            P("rows", None),
        ),
        out_specs=(P("rows", None, "inner", None), P("rows", None, "inner", None)),
        check_vma=False,
    )
```
